128 devices in a mesh: batch: 32 (over z_hi, y, x), dim: 4 (over z_lo, core).
Axes of the slice: x: 4, y: 4, z: 4 (z_hi: 2, z_lo: 2; z = z_hi * 2 + z_lo), core: 2. Of those that a mesh axis runs over, the one named last changes fastest.
Arguments:
- picture_embeds: bfloat16 [11264, 1152], P('batch', 'dim'), may hold values from -0.1875 to 0.1875
- caption_embeds: bfloat16 [11264, 1152], P('batch', 'dim'), may hold values from -0.1875 to 0.1875
- logit_scaler: float32 [1], replicated, may hold values from 10 to 30
- logit_offset_term: float32 [1], replicated, may hold values from -4 to -2
Outputs:
- image_grad: float32 [11264, 1152], P('batch', 'dim')
- text_grad: float32 [11264, 1152], P('batch', 'dim')
- scalar_grads: float32 [2], replicated
The draws below stay inside these ranges and needn't reach their ends.
All inputs are finite; a program needn't handle non-finite values.
Results may differ from the reference program's by a relative error of at most 0.0003.
The reference program's roundings to bfloat16 on the way (of `coeff_low`) count: a program that leaves them out, or rounds other values in their place, can miss the bound.
Values may be sent and summed in bfloat16 or wider, within the bound.
No kernel may reach another device: no remote copies, remote signals or barrier semaphores. Data moves between devices by JAX's collectives and lax.ppermute only.
A program may use at most 64 MiB of HBM per device.

```python
import math
import jax
import jax.numpy as jnp
from jax import lax

D = 1152
ROWS_DEV = 352
NTOT = 11264
N_BATCH = 32


def steps_of(own_key, extent, split, smallest, largest):
    loudness = 1.0
    for axis_at, blocks in split:
        heights = jax.random.uniform(jax.random.fold_in(jax.random.fold_in(own_key, 6), axis_at), (blocks,), jnp.float32, smallest / len(split), largest / len(split))
        loudness = loudness * jnp.repeat(jnp.exp(heights), extent[axis_at] // blocks).reshape((-1,) + (1,) * (len(extent) - 1 - axis_at))
    return loudness


def noise(key, shape, spread, limit, split=(), kind=jnp.bfloat16):
    gain = steps_of(key, shape, split, -0.22, 0.18) if split else 1.0
    values = jax.random.normal(key, shape, jnp.float32) * spread * gain
    return jnp.minimum(jnp.maximum(values, -limit), limit).astype(kind)


def setup_inputs(seed: int = 0) -> dict:
    key_list = jax.random.split(jax.random.key(seed), 5)
    return {
        "picture_embeds": noise(key_list[0], (NTOT, D), 0.03, 0.1875, ((0, 32), (1, 4))),
        "caption_embeds": noise(key_list[1], (NTOT, D), 0.03, 0.1875, ((0, 32), (1, 4))),
        "logit_scaler": jnp.clip(jnp.exp(jax.random.uniform(key_list[2], (1,), jnp.float32, math.log(10.0), math.log(30.0))), 10.0, 30.0),
        "logit_offset_term": jnp.clip(jax.random.uniform(key_list[3], (1,), jnp.float32, -4.0, -2.0), -4.0, -2.0),
    }


def reference(picture_embeds, caption_embeds, logit_scaler, logit_offset_term):
    scaling_factor = logit_scaler[0]
    offset = logit_offset_term[0]
    row_blocks = picture_embeds.reshape(N_BATCH, ROWS_DEV, D)
    columns = jnp.arange(NTOT, dtype=jnp.int32)

    def one_block(carry, bundled_operands):
        text_acc, temp_acc, bias_running_total = carry
        block_index, image_block = bundled_operands
        similar = jnp.dot(image_block, caption_embeds.T, preferred_element_type=jnp.float32)
        logits = scaling_factor * similar + offset
        row_ids = block_index * ROWS_DEV + jnp.arange(ROWS_DEV, dtype=jnp.int32)
        labels = jnp.where(row_ids[:, None] == columns[None, :], jnp.float32(1.0), jnp.float32(-1.0))
        coeff = -labels * jax.nn.sigmoid(-labels * logits)
        coeff_low = coeff.astype(jnp.bfloat16)
        image_part = scaling_factor * jnp.dot(coeff_low, caption_embeds, preferred_element_type=jnp.float32)
        text_acc = text_acc + scaling_factor * jnp.dot(coeff_low.T, image_block, preferred_element_type=jnp.float32)
        temp_acc = temp_acc + jnp.sum(coeff * similar)
        bias_running_total = bias_running_total + jnp.sum(coeff)
        return (text_acc, temp_acc, bias_running_total), image_part

    start = (jnp.zeros((NTOT, D), jnp.float32), jnp.float32(0.0), jnp.float32(0.0))
    block_ids = jnp.arange(N_BATCH, dtype=jnp.int32)
    (text_grad, temp_grad, bias_gradient), image_parts = lax.scan(one_block, start, (block_ids, row_blocks))
    image_grad = image_parts.reshape(NTOT, D)
    return image_grad, text_grad, jnp.stack([temp_grad, bias_gradient])
```

```python
import functools

import jax
import jax.numpy as jnp
from jax import lax
from jax.experimental import pallas as pl
from jax.experimental.pallas import tpu as pltpu
from jax.sharding import PartitionSpec as P

BF = jnp.bfloat16
F32 = jnp.float32
AXES = ("batch", "dim")
CORE = 1


def x_mask(k):
    return k << 2


def y_mask(k):
    return k << 4


def z_mask(k):
    return ((k >> 1) << 6) | ((k & 1) << 1)


def swap(array, mask0, mask1=None):
    mask1 = mask0 if mask1 is None else mask1
    n = lax.axis_size("batch") * lax.axis_size("dim")
    return lax.ppermute(array, AXES, [(i, i ^ (mask1 if i & 1 else mask0)) for i in range(n)])


LOW = 2.0**-3.5


def encode(v, m):
    a = jnp.abs(v) * (127.0 * LOW / m) + LOW
    for _ in range(5):
        a = a * a
    return jnp.where(v < 0, -a, a)


def decode(code, m):
    c = code.astype(F32)
    a = jnp.exp(jnp.log(jnp.abs(c)) * (1.0 / 32.0)) * (1.0 / LOW) - 1.0
    v = a * (m * (1.0 / 127.0))
    return jnp.where(c < 0, -v, v)


def top_of(largest):
    return (largest * 1.01 + 1e-30).astype(BF).astype(F32)


def tile_kernel(
    rows, half, feats,
    core_ref, scale_ref, text_ids, image_ids, own_ref, t1_ref, t2_ref, t3_ref, im0_ref, im1_ref,
    text_own, m1_ref, m2_ref, m3_ref, img0_ref, img1_ref, sums_ref,
    texts, images, t_rel, coeff_low, grads, img_acc, sems,
):
    core = core_ref[0]
    scaling, offset = scale_ref[0], scale_ref[1]
    quarter = 4 * rows
    copies = [
        pltpu.make_async_copy(src, texts.at[j], sems.at[j])
        for j, src in enumerate((own_ref, t1_ref, t2_ref, t3_ref))
    ] + [
        pltpu.make_async_copy(src, images.at[pl.ds(o * quarter, quarter)], sems.at[4 + o])
        for o, src in enumerate((im0_ref, im1_ref))
    ]
    for copy in copies:
        copy.start()
    for copy in copies:
        copy.wait()
    img_acc[...] = jnp.zeros_like(img_acc)
    step = 2 * rows

    def chunk(zp, sums):
        def build(yo, carry):
            def block(zo):
                return texts[jnp.where(core == 0, zo, yo), jnp.where(core == 0, yo, zo)].astype(F32)

            p0, p1 = block(2 * zp), block(2 * zp + 1)
            top = jnp.concatenate([p0[:, :half], p1[:, :half]], axis=1)
            bottom = jnp.concatenate([p0[:, half:], p1[:, half:]], axis=1)
            at = pl.ds(pl.multiple_of(yo * step, 16), step)
            t_rel[at, :] = jnp.concatenate([top, bottom], axis=0).astype(BF)
            return carry

        lax.fori_loop(0, 4, build, 0)
        similar = lax.dot_general(
            t_rel[...], images[...], (((1,), (1,)), ((), ())), preferred_element_type=F32
        )
        logits = scaling * similar + offset
        matched = text_ids[zp] == image_ids[...]
        signed = jnp.where(matched, -logits, logits)
        sig = 1.0 / (1.0 + jnp.exp(-signed))
        coeff = jnp.where(matched, -sig, sig)
        coeff_low[...] = coeff.astype(BF)
        temp = sums[0] + jnp.sum(coeff * similar, axis=0, keepdims=True)
        bias = sums[1] + jnp.sum(coeff, axis=0, keepdims=True)
        text_part = jnp.dot(coeff_low[...], images[...], preferred_element_type=F32)
        for yo in range(4):
            top = text_part[yo * step : yo * step + rows]
            bottom = text_part[yo * step + rows : (yo + 1) * step]
            grads[2 * zp, yo] = jnp.concatenate([top[:, :half], bottom[:, :half]], axis=1)
            grads[2 * zp + 1, yo] = jnp.concatenate([top[:, half:], bottom[:, half:]], axis=1)
        img_acc[...] += lax.dot_general(
            coeff_low[...], t_rel[...], (((0,), (0,)), ((), ())), preferred_element_type=F32
        )
        return (temp, bias)

    zero = jnp.zeros((1, 2 * quarter), F32)
    temp, bias = lax.fori_loop(0, 2, chunk, (zero, zero))
    sums_ref[...] = jnp.concatenate(
        [jnp.broadcast_to(jnp.sum(v, axis=1, keepdims=True), (4, 128)) for v in (temp, bias)], axis=0
    )
    img0_ref[...] = img_acc[0:quarter]
    img1_ref[...] = img_acc[quarter : 2 * quarter]

    def grad_block(j, i):
        return grads[jnp.where(core == 0, j, i), jnp.where(core == 0, i, j)]

    for i in range(4):
        text_own[i] = grad_block(0, i)
    for j, m_ref in ((1, m1_ref), (2, m2_ref), (3, m3_ref)):
        whole = jnp.concatenate([grad_block(j, i) for i in range(4)], axis=0)
        m = top_of(jnp.max(jnp.max(jnp.abs(whole), axis=0, keepdims=True), axis=1, keepdims=True))
        m_ref[0:quarter, :] = encode(whole, m).astype(BF)
        m_ref[quarter : quarter + 16, :] = jnp.broadcast_to(m, (16, feats)).astype(BF)


def first_sum_kernel(rows, feats, own_ref, r1_ref, r2_ref, r3_ref, out_ref, m1_ref, m2_ref, m3_ref):
    quarter = 4 * rows
    received = [(r[0:quarter], r[quarter : quarter + 16].astype(F32)[0:1, :]) for r in (r1_ref, r2_ref, r3_ref)]
    total = jnp.concatenate([own_ref[i] for i in range(4)], axis=0)
    for code, m in received:
        total = total + decode(code, m)
    out_ref[...] = total[0:rows]
    for i, m_ref in ((1, m1_ref), (2, m2_ref), (3, m3_ref)):
        part = total[i * rows : (i + 1) * rows]
        m = top_of(jnp.max(jnp.max(jnp.abs(part), axis=0, keepdims=True), axis=1, keepdims=True))
        m_ref[...] = jnp.concatenate([encode(part, m), jnp.broadcast_to(m, (16, feats))], axis=0).astype(BF)


def last_sum_kernel(rows, scale_ref, own_ref, r1_ref, r2_ref, r3_ref, out_ref):
    total = own_ref[...]
    for r in (r1_ref, r2_ref, r3_ref):
        whole = r[...].astype(F32)
        total = total + decode(whole[0:rows], whole[rows : rows + 1])
    out_ref[...] = total * scale_ref[0]


VMEM = pl.BlockSpec(memory_space=pltpu.VMEM)
SMEM = pl.BlockSpec(memory_space=pltpu.SMEM)
HBM = pl.BlockSpec(memory_space=pl.ANY)
BIG = pltpu.CompilerParams(vmem_limit_bytes=56 * 1024 * 1024)


def body(picture_embeds, caption_embeds, logit_scaler, logit_offset_term):
    height, width = picture_embeds.shape
    rows, half, feats = height // 4, 2 * width, 4 * width
    step, quarter = 2 * rows, 4 * rows
    index = lax.axis_index("batch") * lax.axis_size("dim") + lax.axis_index("dim")
    core, z_lo = index & 1, (index >> 1) & 1
    on0, lo0 = core == 0, z_lo == 0
    scaling = logit_scaler[0]

    def by_core(first, second):
        return jnp.where(on0, first, second), jnp.where(on0, second, first)

    keep, send = by_core(caption_embeds[:step], caption_embeds[step:])
    got = swap(send, CORE)
    chip = jnp.concatenate(by_core(keep, got), axis=1)
    packed = jnp.concatenate([chip[:rows], chip[rows:]], axis=1)
    dim = index & 3
    parts = [lax.dynamic_slice(picture_embeds, (rows * (dim ^ q), 0), (rows, width)) for q in range(4)]
    parts = [parts[0]] + [swap(parts[q], q) for q in range(1, 4)]
    image = jnp.concatenate(by_core(parts[0], parts[1]) + by_core(parts[2], parts[3]), axis=1)

    first = [packed] + [swap(packed, y_mask(i), z_mask(i)) for i in range(1, 4)]
    images_own = jnp.concatenate([image] + [swap(image, x_mask(k)) for k in range(1, 4)], axis=0)
    stack = jnp.stack(first)
    images_other = swap(images_own, CORE)
    second = [stack] + [swap(stack, z_mask(j), y_mask(j)) for j in range(1, 4)]

    batch = index >> 2
    zh_bit, x_of = lax.axis_size("batch") // 2, batch & 3
    r = jnp.arange(step, dtype=jnp.int32)
    text_ids = jnp.concatenate(
        [(batch ^ (zp * zh_bit) ^ (yo << 2)) * height + step * core + r for zp in range(2) for yo in range(4)]
    ).reshape(2, 4 * step, 1)
    r = jnp.arange(rows, dtype=jnp.int32)
    image_ids = jnp.concatenate(
        [(batch ^ k) * height + rows * (2 * z_lo + (core ^ o)) + r for o in range(2) for k in range(4)]
    ).reshape(1, 2 * quarter)

    message = jax.ShapeDtypeStruct((quarter + 16, feats), BF)
    text_own, m1, m2, m3, img_own, img_other, sums = pl.pallas_call(
        functools.partial(tile_kernel, rows, half, feats),
        out_shape=(
            jax.ShapeDtypeStruct((4, rows, feats), F32), message, message, message,
            jax.ShapeDtypeStruct((quarter, feats), F32), jax.ShapeDtypeStruct((quarter, feats), F32),
            jax.ShapeDtypeStruct((8, 128), F32),
        ),
        in_specs=[SMEM, SMEM, VMEM, VMEM] + [HBM] * 6,
        out_specs=(VMEM,) * 7,
        scratch_shapes=[
            pltpu.VMEM((4, 4, rows, feats), BF),
            pltpu.VMEM((2 * quarter, feats), BF),
            pltpu.VMEM((4 * step, feats), BF),
            pltpu.VMEM((4 * step, 2 * quarter), BF),
            pltpu.VMEM((4, 4, rows, feats), F32),
            pltpu.VMEM((2 * quarter, feats), F32),
            pltpu.SemaphoreType.DMA((6,)),
        ],
        compiler_params=BIG,
        name="tile",
    )(core.reshape(1), jnp.stack([scaling, logit_offset_term[0]]), text_ids, image_ids, *second, images_own, images_other)

    got = [swap(m, z_mask(j), y_mask(j)) for j, m in ((1, m1), (2, m2), (3, m3))]
    img = img_own + swap(img_other, CORE)
    img = img.reshape(4, rows, feats)
    img_got = [swap(img[k], x_mask(k)) for k in range(1, 4)]

    message = jax.ShapeDtypeStruct((rows + 16, feats), BF)
    text, n1, n2, n3 = pl.pallas_call(
        functools.partial(first_sum_kernel, rows, feats),
        out_shape=(jax.ShapeDtypeStruct((rows, feats), F32), message, message, message),
        in_specs=[VMEM] * 4,
        out_specs=(VMEM,) * 4,
        compiler_params=BIG,
        name="first_sum",
    )(text_own, *got)
    got = [swap(m, y_mask(i), z_mask(i)) for i, m in ((1, n1), (2, n2), (3, n3))]

    img = scaling * (img[0] + img_got[0] + img_got[1] + img_got[2])
    quarters = by_core(img[:, :width], img[:, width:half]) + by_core(img[:, half : half + width], img[:, half + width :])
    back = [quarters[0]] + [swap(quarters[q], q) for q in range(1, 4)]
    back = list(by_core(back[0], back[1]) + by_core(back[2], back[3]))
    back = [jnp.where(lo0, back[e], back[e ^ 2]) for e in range(4)]
    image_grad = jnp.concatenate(back, axis=0)

    for mask in (CORE, x_mask(1), x_mask(2), y_mask(1), y_mask(2), z_mask(1), z_mask(2)):
        sums = sums + swap(sums, mask)
    scalar_grads = jnp.stack([sums[0, 0], sums[4, 0]])

    text = pl.pallas_call(
        functools.partial(last_sum_kernel, rows),
        out_shape=jax.ShapeDtypeStruct((rows, feats), F32),
        in_specs=[SMEM] + [VMEM] * 4,
        out_specs=VMEM,
        compiler_params=BIG,
        name="last_sum",
    )(logit_scaler, text, *got)
    chip = jnp.concatenate([text[:, :half], text[:, half:]], axis=0)
    mine, other = by_core(chip[:, :width], chip[:, width:])
    text_grad = jnp.concatenate(by_core(mine, swap(other, CORE)), axis=0)
    return (image_grad, text_grad, scalar_grads)


def solution(mesh):
    placed = (P("batch", "dim"), P("batch", "dim"), P(), P())
    return jax.shard_map(
        body,
        mesh=mesh,
        in_specs=placed,
        out_specs=(P("batch", "dim"), P("batch", "dim"), P()),
        check_vma=False,
    )
```

```python
import functools

import jax
import jax.numpy as jnp
from jax import lax
from jax.experimental import pallas as pl
from jax.experimental.pallas import tpu as pltpu
from jax.sharding import PartitionSpec as P

BF = jnp.bfloat16
F32 = jnp.float32
AXES = ("batch", "dim")
CORE = 1


def x_mask(k):
    return k << 2


def y_mask(k):
    return k << 4


def z_mask(k):
    return ((k >> 1) << 6) | ((k & 1) << 1)


def swap(array, mask0, mask1=None):
    mask1 = mask0 if mask1 is None else mask1
    n = lax.axis_size("batch") * lax.axis_size("dim")
    return lax.ppermute(array, AXES, [(i, i ^ (mask1 if i & 1 else mask0)) for i in range(n)])


LOW = 2.0**-3.5


def encode(v, m):
    a = jnp.abs(v) * (127.0 * LOW / m) + LOW
    for _ in range(5):
        a = a * a
    return jnp.where(v < 0, -a, a)


def decode(code, m):
    c = code.astype(F32)
    a = jnp.exp(jnp.log(jnp.abs(c)) * (1.0 / 32.0)) * (1.0 / LOW) - 1.0
    v = a * (m * (1.0 / 127.0))
    return jnp.where(c < 0, -v, v)


def top_of(largest):
    return (largest * 1.01 + 1e-30).astype(BF).astype(F32)


def tile_kernel(
    first, rows, half, feats,
    info_ref, scale_ref, *refs,
):
    if first:
        ta_ref, tb_ref, im0_ref, im1_ref, own_ref, msg_ref, acc_ref, sums_ref, texts, images, t_rel, coeff_low, grads, sems = refs
    else:
        (ta_ref, tb_ref, im0_ref, im1_ref, before_ref, sums_before, ma_ref, mb_ref, img0_ref, img1_ref, sums_ref,
         texts, images, t_rel, coeff_low, grads, sems) = refs
    core, z_lo = info_ref[0], info_ref[1]
    scaling, offset = scale_ref[0], scale_ref[1]
    quarter, step = 4 * rows, 2 * rows
    copies = [pltpu.make_async_copy(src, texts.at[j], sems.at[j]) for j, src in enumerate((ta_ref, tb_ref))] + [
        pltpu.make_async_copy(src, images.at[pl.ds(o * quarter, quarter)], sems.at[2 + o])
        for o, src in enumerate((im0_ref, im1_ref))
    ]
    for copy in copies:
        copy.start()
    for copy in copies:
        copy.wait()

    def place(b, e):
        return jnp.where(core == 0, e, b >> 1), jnp.where(core == 0, b, 2 * (b & 1) + e)

    for b in range(4):
        p0, p1 = (texts[place(b, e)].astype(F32) for e in range(2))
        top = jnp.concatenate([p0[:, :half], p1[:, :half]], axis=1)
        bottom = jnp.concatenate([p0[:, half:], p1[:, half:]], axis=1)
        t_rel[b * step : (b + 1) * step, :] = jnp.concatenate([top, bottom], axis=0).astype(BF)
    similar = lax.dot_general(t_rel[...], images[...], (((1,), (1,)), ((), ())), preferred_element_type=F32)
    temp, bias = jnp.zeros((1, 2 * quarter), F32), jnp.zeros((1, 2 * quarter), F32)
    for b in range(4):
        part = similar[b * step : (b + 1) * step]
        logits = scaling * part + offset
        if first and b == 0:
            row = lax.broadcasted_iota(jnp.int32, part.shape, 0)
            column = lax.broadcasted_iota(jnp.int32, part.shape, 1)
            matched = (row - rows * z_lo == column) & (column < rows)
            sig = 1.0 / (1.0 + jnp.exp(jnp.where(matched, logits, -logits)))
            coeff = jnp.where(matched, -sig, sig)
        else:
            coeff = 1.0 / (1.0 + jnp.exp(-logits))
        coeff_low[b * step : (b + 1) * step, :] = coeff.astype(BF)
        temp = temp + jnp.sum(coeff * part, axis=0, keepdims=True)
        bias = bias + jnp.sum(coeff, axis=0, keepdims=True)
    sums = jnp.concatenate(
        [jnp.broadcast_to(jnp.sum(v, axis=1, keepdims=True), (4, 128)) for v in (temp, bias)], axis=0
    )
    text_part = jnp.dot(coeff_low[...], images[...], preferred_element_type=F32)
    for b in range(4):
        top = text_part[b * step : b * step + rows]
        bottom = text_part[b * step + rows : (b + 1) * step]
        grads[place(b, 0)] = jnp.concatenate([top[:, :half], bottom[:, :half]], axis=1)
        grads[place(b, 1)] = jnp.concatenate([top[:, half:], bottom[:, half:]], axis=1)
    acc = lax.dot_general(coeff_low[...], t_rel[...], (((0,), (0,)), ((), ())), preferred_element_type=F32)

    def send(e, m_ref):
        whole = jnp.concatenate([grads[e, i] for i in range(4)], axis=0)
        m = top_of(jnp.max(jnp.max(jnp.abs(whole), axis=0, keepdims=True), axis=1, keepdims=True))
        m_ref[0:quarter, :] = encode(whole, m).astype(BF)
        m_ref[quarter : quarter + 16, :] = jnp.broadcast_to(m, (16, feats)).astype(BF)

    if first:
        acc_ref[...] = acc
        sums_ref[...] = sums
        own_ref[...] = jnp.concatenate([grads[0, i] for i in range(4)], axis=0)
        send(1, msg_ref)
    else:
        acc = acc + before_ref[...]
        img0_ref[...] = acc[0:quarter]
        img1_ref[...] = acc[quarter : 2 * quarter]
        sums_ref[...] = sums + sums_before[...]
        send(0, ma_ref)
        send(1, mb_ref)


def split3(v):
    hi = v.astype(BF).astype(F32)
    mid = (v - hi).astype(BF).astype(F32)
    return [hi, mid, v - hi - mid]


def first_sum_kernel(rows, feats, coded, own_ref, sums_ref, *refs):
    received, (out_ref, m1_ref, m2_ref, m3_ref) = refs[:-4], refs[-4:]
    quarter = 4 * rows
    total = own_ref[...]
    for r in received:
        total = total + (decode(r[0:quarter], r[quarter : quarter + 16].astype(F32)[0:1, :]) if coded else r[...])
    out_ref[...] = total[0:rows]
    scalars = [jnp.broadcast_to(v, (1, feats)) for at in (0, 4) for v in split3(sums_ref[at : at + 1, 0:1])]
    for i, m_ref in ((1, m1_ref), (2, m2_ref), (3, m3_ref)):
        part = total[i * rows : (i + 1) * rows]
        m = top_of(jnp.max(jnp.max(jnp.abs(part), axis=0, keepdims=True), axis=1, keepdims=True))
        m = jnp.broadcast_to(m, (10, feats))
        m_ref[...] = jnp.concatenate([encode(part, m[0:1]), *scalars, m], axis=0).astype(BF)


def last_sum_kernel(rows, scale_ref, own_ref, sums_ref, r1_ref, r2_ref, r3_ref, out_ref, sums_out):
    total = own_ref[...]
    wholes = [r[...].astype(F32) for r in (r1_ref, r2_ref, r3_ref)]
    for whole in wholes:
        total = total + decode(whole[0:rows], whole[rows + 8 : rows + 9])
    out_ref[...] = total * scale_ref[0]
    extra = [whole[rows : rows + 8, 0:128] for whole in wholes]

    def three(e, at):
        return e[at : at + 1] + (e[at + 1 : at + 2] + e[at + 2 : at + 3])

    for at, src in ((0, 0), (4, 3)):
        a, b, c = (three(e, src) for e in extra)
        sums_out[at : at + 4, :] = jnp.broadcast_to((sums_ref[at : at + 1, :] + a) + (b + c), (4, 128))


VMEM = pl.BlockSpec(memory_space=pltpu.VMEM)
SMEM = pl.BlockSpec(memory_space=pltpu.SMEM)
HBM = pl.BlockSpec(memory_space=pl.ANY)
BIG = pltpu.CompilerParams(vmem_limit_bytes=56 * 1024 * 1024)


def after(array, *others):
    return lax.optimization_barrier((array, *others))[0]


def body(picture_embeds, caption_embeds, logit_scaler, logit_offset_term):
    height, width = picture_embeds.shape
    rows, half, feats = height // 4, 2 * width, 4 * width
    step, quarter = 2 * rows, 4 * rows
    index = lax.axis_index("batch") * lax.axis_size("dim") + lax.axis_index("dim")
    core, z_lo = index & 1, (index >> 1) & 1
    on0, lo0 = core == 0, z_lo == 0
    scaling = logit_scaler[0]

    def by(first_one, own, other):
        return [jnp.where(first_one, own, other), jnp.where(first_one, other, own)]

    both = [jnp.concatenate([t[:step], i[:step]]) for t, i in ((caption_embeds, picture_embeds),)]
    both.append(jnp.concatenate([caption_embeds[step:], picture_embeds[step:]]))
    keep, send = by(on0, *both)
    chip = jnp.concatenate(by(on0, keep, swap(send, CORE)), axis=1)
    packed = jnp.concatenate([chip[:rows], chip[rows:step]], axis=1)
    keep, send = by(lo0, chip[step : step + rows], chip[step + rows :])
    first = [packed] + [swap(packed, y_mask(i), z_mask(i)) for i in range(1, 4)]
    image = jnp.concatenate([keep, swap(send, z_mask(1))], axis=1)
    stack = jnp.stack(first)
    second1, second3 = swap(stack, z_mask(1), y_mask(1)), swap(stack, z_mask(3), y_mask(3))
    images_own = jnp.concatenate([image] + [swap(image, x_mask(k)) for k in range(1, 4)], axis=0)
    images_other = swap(images_own, CORE)
    second2 = swap(after(stack, second1, second3), z_mask(2), y_mask(2))

    info = jnp.stack([core, z_lo]).astype(jnp.int32)
    scales = jnp.stack([scaling, logit_offset_term[0]])
    message = jax.ShapeDtypeStruct((quarter + 16, feats), BF)
    image_part = jax.ShapeDtypeStruct((quarter, feats), F32)
    acc_shape = jax.ShapeDtypeStruct((2 * quarter, feats), F32)
    sums_shape = jax.ShapeDtypeStruct((8, 128), F32)
    scratch = [
        pltpu.VMEM((2, 4, rows, feats), BF),
        pltpu.VMEM((2 * quarter, feats), BF),
        pltpu.VMEM((4 * step, feats), BF),
        pltpu.VMEM((4 * step, 2 * quarter), BF),
        pltpu.VMEM((2, 4, rows, feats), F32),
        pltpu.SemaphoreType.DMA((4,)),
    ]
    cost = pl.CostEstimate(
        flops=3 * 2 * 4 * step * 2 * quarter * feats, bytes_accessed=12 * 4 * step * feats, transcendentals=8 * step * quarter
    )
    text_own, m1, acc, sums = pl.pallas_call(
        functools.partial(tile_kernel, True, rows, half, feats),
        out_shape=(image_part, message, acc_shape, sums_shape),
        in_specs=[SMEM, SMEM] + [HBM] * 4,
        out_specs=(VMEM,) * 4,
        scratch_shapes=scratch,
        compiler_params=BIG,
        cost_estimate=cost,
        name="tile_first",
    )(info, scales, stack, second1, images_own, images_other)
    m2, m3, img_own, img_other, sums = pl.pallas_call(
        functools.partial(tile_kernel, False, rows, half, feats),
        out_shape=(message, message, image_part, image_part, sums_shape),
        in_specs=[SMEM, SMEM] + [HBM] * 4 + [VMEM] * 2,
        out_specs=(VMEM,) * 5,
        scratch_shapes=scratch,
        compiler_params=BIG,
        cost_estimate=cost,
        name="tile_second",
    )(info, scales, second2, second3, images_own, images_other, acc, sums)

    message = jax.ShapeDtypeStruct((rows + 16, feats), BF)

    def first_sum(name, coded, *args):
        return pl.pallas_call(
            functools.partial(first_sum_kernel, rows, feats, coded),
            out_shape=(jax.ShapeDtypeStruct((rows, feats), F32), message, message, message),
            in_specs=[VMEM] * len(args),
            out_specs=(VMEM,) * 4,
            compiler_params=BIG,
            name=name,
        )(*args)

    def last_sum(name, *args):
        return pl.pallas_call(
            functools.partial(last_sum_kernel, rows),
            out_shape=(jax.ShapeDtypeStruct((rows, feats), F32), sums_shape),
            in_specs=[SMEM] + [VMEM] * 5,
            out_specs=(VMEM, VMEM),
            compiler_params=BIG,
            name=name,
        )(logit_scaler, *args)

    got1 = swap(m1, z_mask(1), y_mask(1))
    img, i1, i2, i3 = first_sum("image_first", False, img_own, sums, after(swap(img_other, CORE), got1))
    got2, got3 = swap(m2, z_mask(2), y_mask(2)), swap(m3, z_mask(3), y_mask(3))
    i1, sums = lax.optimization_barrier((i1, sums))
    img_got = [swap(m, x_mask(k)) for k, m in ((1, i1), (2, i2), (3, i3))]
    for mask in ((x_mask(1),), (x_mask(2),), (z_mask(1), y_mask(1)), (z_mask(2), y_mask(2))):
        sums = sums + swap(sums, *mask)

    text, n1, n2, n3 = first_sum("text_first", True, text_own, sums, got1, got2, got3)
    got = [swap(m, y_mask(i), z_mask(i)) for i, m in ((1, n1), (2, n2), (3, n3))]

    img, _ = last_sum("image_last", img, sums, *img_got)
    image = jnp.concatenate(by(lo0, img[:, :half], swap(img[:, half:], z_mask(1))), axis=0)
    text, sums = last_sum("text_last", after(text, image), sums, *got)
    whole = jnp.concatenate([text[:, :half], text[:, half:], image], axis=0)
    mine, other = by(on0, whole[:, :width], whole[:, width:])
    tail = jnp.pad(sums, ((0, 0), (0, width - sums.shape[1])))
    other = swap(jnp.concatenate([other, tail], axis=0), CORE)
    text_grad = jnp.concatenate(by(on0, mine[:step], other[:step]), axis=0)
    image_grad = jnp.concatenate(by(on0, mine[step:], other[step : 2 * step]), axis=0)
    sums = sums + other[2 * step :, :128]
    scalar_grads = jnp.stack([sums[0, 0], sums[4, 0]])
    return (image_grad, text_grad, scalar_grads)


def solution(mesh):
    placed = (P("batch", "dim"), P("batch", "dim"), P(), P())
    return jax.shard_map(
        body,
        mesh=mesh,
        in_specs=placed,
        out_specs=(P("batch", "dim"), P("batch", "dim"), P()),
        check_vma=False,
    )
```

```python
import functools

import jax
import jax.numpy as jnp
from jax import lax
from jax.experimental import pallas as pl
from jax.experimental.pallas import tpu as pltpu
from jax.sharding import PartitionSpec as P

BF = jnp.bfloat16
F32 = jnp.float32
AXES = ("batch", "dim")
CORE = 1


def x_mask(k):
    return k << 2


def y_mask(k):
    return k << 4


def z_mask(k):
    return ((k >> 1) << 6) | ((k & 1) << 1)


def swap(array, mask0, mask1=None):
    mask1 = mask0 if mask1 is None else mask1
    n = lax.axis_size("batch") * lax.axis_size("dim")
    return lax.ppermute(array, AXES, [(i, i ^ (mask1 if i & 1 else mask0)) for i in range(n)])


LOW = 2.0**-3.5


def encode(v, m):
    a = jnp.abs(v) * (127.0 * LOW / m) + LOW
    for _ in range(5):
        a = a * a
    return jnp.where(v < 0, -a, a)


def decode(code, m):
    c = code.astype(F32)
    a = jnp.exp(jnp.log(jnp.abs(c)) * (1.0 / 32.0)) * (1.0 / LOW) - 1.0
    v = a * (m * (1.0 / 127.0))
    return jnp.where(c < 0, -v, v)


def top_of(largest):
    return (largest * 1.01 + 1e-30).astype(BF).astype(F32)


def tile_kernel(
    first, rows, half, feats,
    info_ref, scale_ref, *refs,
):
    if first:
        ta_ref, tb_ref, im0_ref, im1_ref, own_ref, msg_ref, acc_ref, sums_ref, texts, images, t_rel, coeff_low, grads, sems = refs
    else:
        (ta_ref, tb_ref, im0_ref, im1_ref, before_ref, sums_before, ma_ref, mb_ref, img0_ref, img1_ref, sums_ref,
         texts, images, t_rel, coeff_low, grads, sems) = refs
    core, z_lo = info_ref[0], info_ref[1]
    scaling, offset = scale_ref[0], scale_ref[1]
    quarter, step = 4 * rows, 2 * rows
    copies = [pltpu.make_async_copy(src, texts.at[j], sems.at[j]) for j, src in enumerate((ta_ref, tb_ref))] + [
        pltpu.make_async_copy(src, images.at[pl.ds(o * quarter, quarter)], sems.at[2 + o])
        for o, src in enumerate((im0_ref, im1_ref))
    ]
    for copy in copies:
        copy.start()
    for copy in copies:
        copy.wait()

    def place(b, e):
        return jnp.where(core == 0, e, b >> 1), jnp.where(core == 0, b, 2 * (b & 1) + e)

    for b in range(4):
        p0, p1 = (texts[place(b, e)].astype(F32) for e in range(2))
        top = jnp.concatenate([p0[:, :half], p1[:, :half]], axis=1)
        bottom = jnp.concatenate([p0[:, half:], p1[:, half:]], axis=1)
        t_rel[b * step : (b + 1) * step, :] = jnp.concatenate([top, bottom], axis=0).astype(BF)
    similar = lax.dot_general(t_rel[...], images[...], (((1,), (1,)), ((), ())), preferred_element_type=F32)
    temp, bias = jnp.zeros((1, 2 * quarter), F32), jnp.zeros((1, 2 * quarter), F32)
    for b in range(4):
        part = similar[b * step : (b + 1) * step]
        logits = scaling * part + offset
        if first and b == 0:
            row = lax.broadcasted_iota(jnp.int32, part.shape, 0)
            column = lax.broadcasted_iota(jnp.int32, part.shape, 1)
            matched = (row - rows * z_lo == column) & (column < rows)
            sig = 1.0 / (1.0 + jnp.exp(jnp.where(matched, logits, -logits)))
            coeff = jnp.where(matched, -sig, sig)
        else:
            coeff = 1.0 / (1.0 + jnp.exp(-logits))
        coeff_low[b * step : (b + 1) * step, :] = coeff.astype(BF)
        temp = temp + jnp.sum(coeff * part, axis=0, keepdims=True)
        bias = bias + jnp.sum(coeff, axis=0, keepdims=True)
    even = lax.broadcasted_iota(jnp.int32, (8, 128), 1) % 2 == 0
    sums = jnp.where(even, jnp.sum(temp, axis=1, keepdims=True), jnp.sum(bias, axis=1, keepdims=True))
    text_part = jnp.dot(coeff_low[...], images[...], preferred_element_type=F32)
    for b in range(4):
        top = text_part[b * step : b * step + rows]
        bottom = text_part[b * step + rows : (b + 1) * step]
        grads[place(b, 0)] = jnp.concatenate([top[:, :half], bottom[:, :half]], axis=1)
        grads[place(b, 1)] = jnp.concatenate([top[:, half:], bottom[:, half:]], axis=1)
    acc = lax.dot_general(coeff_low[...], t_rel[...], (((0,), (0,)), ((), ())), preferred_element_type=F32)

    def send(e, m_ref):
        whole = jnp.concatenate([grads[e, i] for i in range(4)], axis=0)
        m = top_of(jnp.max(jnp.max(jnp.abs(whole), axis=0, keepdims=True), axis=1, keepdims=True))
        m_ref[0:quarter, :] = encode(whole, m).astype(BF)
        m_ref[quarter : quarter + 16, :] = jnp.broadcast_to(m, (16, feats)).astype(BF)

    if first:
        acc_ref[...] = acc
        sums_ref[...] = sums
        own_ref[...] = jnp.concatenate([grads[0, i] for i in range(4)], axis=0)
        send(1, msg_ref)
    else:
        acc = acc + before_ref[...]
        img0_ref[...] = acc[0:quarter]
        img1_ref[...] = acc[quarter : 2 * quarter]
        sums_ref[...] = sums + sums_before[...]
        send(0, ma_ref)
        send(1, mb_ref)


def split3(v):
    hi = v.astype(BF).astype(F32)
    mid = (v - hi).astype(BF).astype(F32)
    return [hi, mid, v - hi - mid]


def first_sum_kernel(rows, feats, coded, own_ref, sums_ref, *refs):
    received, (out_ref, m1_ref, m2_ref, m3_ref) = refs[:-4], refs[-4:]
    quarter = 4 * rows
    total = own_ref[...]
    for r in received:
        total = total + (decode(r[0:quarter], r[quarter : quarter + 16].astype(F32)[0:1, :]) if coded else r[...])
    out_ref[...] = total[0:rows]
    scalars = [jnp.concatenate([v] * (feats // 128), axis=1) for v in split3(sums_ref[0:1, :])]
    for i, m_ref in ((1, m1_ref), (2, m2_ref), (3, m3_ref)):
        part = total[i * rows : (i + 1) * rows]
        m = top_of(jnp.max(jnp.max(jnp.abs(part), axis=0, keepdims=True), axis=1, keepdims=True))
        m = jnp.broadcast_to(m, (13, feats))
        m_ref[...] = jnp.concatenate([encode(part, m[0:1]), *scalars, m], axis=0).astype(BF)


def last_sum_kernel(rows, scale_ref, own_ref, sums_ref, r1_ref, r2_ref, r3_ref, out_ref, sums_out):
    total = own_ref[...]
    wholes = [r[...].astype(F32) for r in (r1_ref, r2_ref, r3_ref)]
    for whole in wholes:
        total = total + decode(whole[0:rows], whole[rows + 8 : rows + 9])
    out_ref[...] = total * scale_ref[0]
    a, b, c = (w[rows : rows + 1, :128] + (w[rows + 1 : rows + 2, :128] + w[rows + 2 : rows + 3, :128]) for w in wholes)
    sums_out[...] = jnp.broadcast_to((sums_ref[0:1, :] + a) + (b + c), (8, 128))


VMEM = pl.BlockSpec(memory_space=pltpu.VMEM)
SMEM = pl.BlockSpec(memory_space=pltpu.SMEM)
HBM = pl.BlockSpec(memory_space=pl.ANY)


def grant(mib):
    return pltpu.CompilerParams(vmem_limit_bytes=mib * 1024 * 1024)


def after(array, *others):
    return lax.optimization_barrier((array, *others))[0]


def body(picture_embeds, caption_embeds, logit_scaler, logit_offset_term):
    height, width = picture_embeds.shape
    rows, half, feats = height // 4, 2 * width, 4 * width
    step, quarter = 2 * rows, 4 * rows
    index = lax.axis_index("batch") * lax.axis_size("dim") + lax.axis_index("dim")
    core, z_lo = index & 1, (index >> 1) & 1
    on0, lo0 = core == 0, z_lo == 0
    scaling = logit_scaler[0]

    def by(first_one, own, other):
        return [jnp.where(first_one, own, other), jnp.where(first_one, other, own)]

    both = [jnp.concatenate([t[:step], i[:step]]) for t, i in ((caption_embeds, picture_embeds),)]
    both.append(jnp.concatenate([caption_embeds[step:], picture_embeds[step:]]))
    keep, send = by(on0, *both)
    chip = jnp.concatenate(by(on0, keep, swap(send, CORE)), axis=1)
    packed = jnp.concatenate([chip[:rows], chip[rows:step]], axis=1)
    keep, send = by(lo0, chip[step : step + rows], chip[step + rows :])
    first = [packed] + [swap(packed, y_mask(i), z_mask(i)) for i in range(1, 4)]
    image = jnp.concatenate([keep, swap(send, z_mask(1))], axis=1)
    stack = jnp.stack(first)
    second1, second3 = swap(stack, z_mask(1), y_mask(1)), swap(stack, z_mask(3), y_mask(3))
    images_own = jnp.concatenate([image] + [swap(image, x_mask(k)) for k in range(1, 4)], axis=0)
    images_other = swap(images_own, CORE)
    second2 = swap(after(stack, second1, second3), z_mask(2), y_mask(2))

    info = jnp.stack([core, z_lo]).astype(jnp.int32)
    scales = jnp.stack([scaling, logit_offset_term[0]])
    message = jax.ShapeDtypeStruct((quarter + 16, feats), BF)
    image_part = jax.ShapeDtypeStruct((quarter, feats), F32)
    acc_shape = jax.ShapeDtypeStruct((2 * quarter, feats), F32)
    sums_shape = jax.ShapeDtypeStruct((8, 128), F32)
    scratch = [
        pltpu.VMEM((2, 4, rows, feats), BF),
        pltpu.VMEM((2 * quarter, feats), BF),
        pltpu.VMEM((4 * step, feats), BF),
        pltpu.VMEM((4 * step, 2 * quarter), BF),
        pltpu.VMEM((2, 4, rows, feats), F32),
        pltpu.SemaphoreType.DMA((4,)),
    ]
    cost = pl.CostEstimate(
        flops=3 * 2 * 4 * step * 2 * quarter * feats, bytes_accessed=12 * 4 * step * feats, transcendentals=8 * step * quarter
    )
    text_own, m1, acc, sums = pl.pallas_call(
        functools.partial(tile_kernel, True, rows, half, feats),
        out_shape=(image_part, message, acc_shape, sums_shape),
        in_specs=[SMEM, SMEM] + [HBM] * 4,
        out_specs=(VMEM,) * 4,
        scratch_shapes=scratch,
        compiler_params=grant(40),
        cost_estimate=cost,
        name="tile_first",
    )(info, scales, stack, second1, images_own, images_other)
    m2, m3, img_own, img_other, sums = pl.pallas_call(
        functools.partial(tile_kernel, False, rows, half, feats),
        out_shape=(message, message, image_part, image_part, sums_shape),
        in_specs=[SMEM, SMEM] + [HBM] * 4 + [VMEM] * 2,
        out_specs=(VMEM,) * 5,
        scratch_shapes=scratch,
        compiler_params=grant(40),
        cost_estimate=cost,
        name="tile_second",
    )(info, scales, second2, second3, images_own, images_other, acc, sums)

    message = jax.ShapeDtypeStruct((rows + 16, feats), BF)

    def first_sum(name, coded, *args):
        return pl.pallas_call(
            functools.partial(first_sum_kernel, rows, feats, coded),
            out_shape=(jax.ShapeDtypeStruct((rows, feats), F32), message, message, message),
            in_specs=[VMEM] * len(args),
            out_specs=(VMEM,) * 4,
            compiler_params=grant(20),
            name=name,
        )(*args)

    def last_sum(name, *args):
        return pl.pallas_call(
            functools.partial(last_sum_kernel, rows),
            out_shape=(jax.ShapeDtypeStruct((rows, feats), F32), sums_shape),
            in_specs=[SMEM] + [VMEM] * 5,
            out_specs=(VMEM, VMEM),
            compiler_params=grant(10),
            name=name,
        )(logit_scaler, *args)

    got1 = swap(m1, z_mask(1), y_mask(1))
    m2, m3, img_other, sums, got1 = lax.optimization_barrier((m2, m3, img_other, sums, got1))
    got2, got3 = swap(m2, z_mask(2), y_mask(2)), swap(m3, z_mask(3), y_mask(3))
    img_got, one = swap(img_other, CORE), swap(sums, x_mask(1))
    img, i1, i2, i3 = first_sum("image_first", False, img_own, sums, img_got)
    i1, i2, i3, one = lax.optimization_barrier((i1, i2, i3, one))
    sums = sums + one
    img_got = [swap(m, x_mask(k)) for k, m in ((1, i1), (2, i2), (3, i3))]
    for mask in ((x_mask(2),), (z_mask(1), y_mask(1)), (z_mask(2), y_mask(2))):
        sums = sums + swap(sums, *mask)

    text, n1, n2, n3 = first_sum("text_first", True, text_own, sums, got1, got2, got3)
    got = [swap(m, y_mask(i), z_mask(i)) for i, m in ((1, n1), (2, n2), (3, n3))]

    img, _ = last_sum("image_last", img, sums, *img_got)
    image = jnp.concatenate(by(lo0, img[:, :half], swap(img[:, half:], z_mask(1))), axis=0)
    text, sums = last_sum("text_last", after(text, image), sums, *got)
    whole = jnp.concatenate([text[:, :half], text[:, half:], image], axis=0)
    mine, other = by(on0, whole[:, :width], whole[:, width:])
    tail = jnp.pad(sums, ((0, 0), (0, width - sums.shape[1])))
    other = swap(jnp.concatenate([other, tail], axis=0), CORE)
    text_grad = jnp.concatenate(by(on0, mine[:step], other[:step]), axis=0)
    image_grad = jnp.concatenate(by(on0, mine[step:], other[step : 2 * step]), axis=0)
    sums = sums + other[2 * step :, :128]
    scalar_grads = sums[0, :2]
    return (image_grad, text_grad, scalar_grads)


def solution(mesh):
    placed = (P("batch", "dim"), P("batch", "dim"), P(), P())
    return jax.shard_map(
        body,
        mesh=mesh,
        in_specs=placed,
        out_specs=(P("batch", "dim"), P("batch", "dim"), P()),
        check_vma=False,
    )
```

```python
import functools

import jax
import jax.numpy as jnp
from jax import lax
from jax.experimental import pallas as pl
from jax.experimental.pallas import tpu as pltpu
from jax.sharding import PartitionSpec as P

BF = jnp.bfloat16
F32 = jnp.float32
AXES = ("batch", "dim")
CORE = 1


def x_mask(k):
    return k << 2


def y_mask(k):
    return k << 4


def z_mask(k):
    return ((k >> 1) << 6) | ((k & 1) << 1)


def swap(array, mask0, mask1=None):
    mask1 = mask0 if mask1 is None else mask1
    n = lax.axis_size("batch") * lax.axis_size("dim")
    return lax.ppermute(array, AXES, [(i, i ^ (mask1 if i & 1 else mask0)) for i in range(n)])


LOW = 2.0**-3.5


def encode(v, m):
    a = jnp.abs(v) * (127.0 * LOW / m) + LOW
    for _ in range(5):
        a = a * a
    return jnp.where(v < 0, -a, a)


def decode(code, m):
    c = code.astype(F32)
    a = jnp.exp(jnp.log(jnp.abs(c)) * (1.0 / 32.0)) * (1.0 / LOW) - 1.0
    v = a * (m * (1.0 / 127.0))
    return jnp.where(c < 0, -v, v)


def top_of(largest):
    return (largest * 1.01 + 1e-30).astype(BF).astype(F32)


def tile_kernel(last, rows, half, feats, info_ref, scale_ref, t0_ref, t1_ref, t2_ref, t3_ref, im0_ref, im1_ref, *refs):
    if last:
        before_ref, sums_before, own_ref, m1_ref, m2_ref, m3_ref, img0_ref, img1_ref, sums_ref, *scratch = refs
    else:
        own_ref, m1_ref, m2_ref, m3_ref, acc_ref, sums_ref, *scratch = refs
    texts, images, t_rel, coeff_low, grads, sems = scratch
    core, z_lo = info_ref[0], info_ref[1]
    scaling, offset = scale_ref[0], scale_ref[1]
    quarter, step = 4 * rows, 2 * rows
    copies = [
        pltpu.make_async_copy(src, texts.at[j], sems.at[j]) for j, src in enumerate((t0_ref, t1_ref, t2_ref, t3_ref))
    ] + [
        pltpu.make_async_copy(src, images.at[pl.ds(o * quarter, quarter)], sems.at[4 + o])
        for o, src in enumerate((im0_ref, im1_ref))
    ]
    for copy in copies:
        copy.start()
    for copy in copies:
        copy.wait()

    def place(b, e):
        return jnp.where(core == 0, 2 * (b >> 1) + e, b), jnp.where(core == 0, b & 1, e)

    for b in range(4):
        p0, p1 = (texts[place(b, e)].astype(F32) for e in range(2))
        top = jnp.concatenate([p0[:, :half], p1[:, :half]], axis=1)
        bottom = jnp.concatenate([p0[:, half:], p1[:, half:]], axis=1)
        t_rel[b * step : (b + 1) * step, :] = jnp.concatenate([top, bottom], axis=0).astype(BF)
    similar = lax.dot_general(t_rel[...], images[...], (((1,), (1,)), ((), ())), preferred_element_type=F32)
    temp, bias = jnp.zeros((1, 2 * quarter), F32), jnp.zeros((1, 2 * quarter), F32)
    for b in range(4):
        part = similar[b * step : (b + 1) * step]
        logits = scaling * part + offset
        if last and b == 0:
            row = lax.broadcasted_iota(jnp.int32, part.shape, 0)
            column = lax.broadcasted_iota(jnp.int32, part.shape, 1)
            matched = (row - rows * z_lo == column) & (column < rows)
            sig = 1.0 / (1.0 + jnp.exp(jnp.where(matched, logits, -logits)))
            coeff = jnp.where(matched, -sig, sig)
        else:
            coeff = 1.0 / (1.0 + jnp.exp(-logits))
        coeff_low[b * step : (b + 1) * step, :] = coeff.astype(BF)
        temp = temp + jnp.sum(coeff * part, axis=0, keepdims=True)
        bias = bias + jnp.sum(coeff, axis=0, keepdims=True)
    even = lax.broadcasted_iota(jnp.int32, (8, 128), 1) % 2 == 0
    sums = jnp.where(even, jnp.sum(temp, axis=1, keepdims=True), jnp.sum(bias, axis=1, keepdims=True))
    text_part = jnp.dot(coeff_low[...], images[...], preferred_element_type=F32)
    for b in range(4):
        top = text_part[b * step : b * step + rows]
        bottom = text_part[b * step + rows : (b + 1) * step]
        grads[place(b, 0)] = jnp.concatenate([top[:, :half], bottom[:, :half]], axis=1)
        grads[place(b, 1)] = jnp.concatenate([top[:, half:], bottom[:, half:]], axis=1)
    acc = lax.dot_general(coeff_low[...], t_rel[...], (((0,), (0,)), ((), ())), preferred_element_type=F32)

    own_ref[...] = jnp.concatenate([grads[0, i] for i in range(2)], axis=0)
    for k, m_ref in ((1, m1_ref), (2, m2_ref), (3, m3_ref)):
        m_ref[...] = message([grads[k, i] for i in range(2)], feats)
    if last:
        acc = acc + before_ref[...]
        img0_ref[...] = acc[0:quarter]
        img1_ref[...] = acc[quarter : 2 * quarter]
        sums_ref[...] = sums + sums_before[...]
    else:
        acc_ref[...] = acc
        sums_ref[...] = sums


def message(blocks, feats, extra=()):
    part = jnp.concatenate(blocks, axis=0)
    m = top_of(jnp.max(jnp.max(jnp.abs(part), axis=0, keepdims=True), axis=1, keepdims=True))
    tail = jnp.broadcast_to(m, (8 - len(extra), feats))
    return jnp.concatenate([encode(part, m), *extra, tail], axis=0).astype(BF)


def decoded(ref):
    whole = ref[...].astype(F32)
    n = whole.shape[0] - 8
    return decode(whole[:n], whole[n + 7 : n + 8]), whole[n:]


def split3(v):
    hi = v.astype(BF).astype(F32)
    mid = (v - hi).astype(BF).astype(F32)
    return [hi, mid, v - hi - mid]


def image_first_kernel(rows, feats, own_ref, other_ref, sums_ref, out_ref, *messages):
    total = own_ref[...] + other_ref[...]
    out_ref[...] = total[0:rows]
    scalars = [jnp.concatenate([v] * (feats // 128), axis=1) for v in split3(sums_ref[0:1, :])]
    for i, m_ref in enumerate(messages):
        m_ref[...] = message([total[(i + 1) * rows : (i + 2) * rows]], feats, scalars)


def image_last_kernel(rows, feats, scale_ref, own_ref, sums_ref, r1_ref, r2_ref, r3_ref, out_ref):
    total, tails = own_ref[...], []
    for r in (r1_ref, r2_ref, r3_ref):
        value, tail = decoded(r)
        total = total + value
        tails.append(tail[0:1, :128] + (tail[1:2, :128] + tail[2:3, :128]))
    sums = (sums_ref[0:1, :] + tails[0]) + (tails[1] + tails[2])
    sums = jnp.broadcast_to(jnp.concatenate([sums] * (feats // 128), axis=1), (8, feats))
    out_ref[...] = jnp.concatenate([total * scale_ref[0], sums], axis=0)


def text_first_kernel(rows, feats, keep, own_ref, r1_ref, r2_ref, r3_ref, *out_refs):
    total = own_ref[...]
    for r in (r1_ref, r2_ref, r3_ref):
        total = total + decoded(r)[0]
    for i, out_ref in enumerate(out_refs):
        block = total[i * rows : (i + 1) * rows]
        out_ref[...] = block if keep and i == 0 else message([block], feats)


def text_last_kernel(scale_ref, own_ref, r1_ref, r2_ref, r3_ref, out_ref):
    total = own_ref[...]
    for r in (r1_ref, r2_ref, r3_ref):
        total = total + decoded(r)[0]
    out_ref[...] = total * scale_ref[0]


VMEM = pl.BlockSpec(memory_space=pltpu.VMEM)
SMEM = pl.BlockSpec(memory_space=pltpu.SMEM)
HBM = pl.BlockSpec(memory_space=pl.ANY)


def grant(mib):
    return pltpu.CompilerParams(vmem_limit_bytes=mib * 1024 * 1024)


def after(array, *others):
    return lax.optimization_barrier((array, *others))[0]


def body(picture_embeds, caption_embeds, logit_scaler, logit_offset_term):
    height, width = picture_embeds.shape
    rows, half, feats = height // 4, 2 * width, 4 * width
    step, quarter = 2 * rows, 4 * rows
    index = lax.axis_index("batch") * lax.axis_size("dim") + lax.axis_index("dim")
    core, z_lo = index & 1, (index >> 1) & 1
    on0, lo0 = core == 0, z_lo == 0
    scaling = logit_scaler[0]

    def by(first_one, own, other):
        return [jnp.where(first_one, own, other), jnp.where(first_one, other, own)]

    both = [jnp.concatenate([t[:step], i[:step]]) for t, i in ((caption_embeds, picture_embeds),)]
    both.append(jnp.concatenate([caption_embeds[step:], picture_embeds[step:]]))
    keep, send = by(on0, *both)
    chip = jnp.concatenate(by(on0, keep, swap(send, CORE)), axis=1)
    packed = jnp.concatenate([chip[:rows], chip[rows:step]], axis=1)
    keep, send = by(lo0, chip[step : step + rows], chip[step + rows :])
    first = [packed] + [swap(packed, y_mask(i), z_mask(i)) for i in range(1, 4)]
    image = after(jnp.concatenate([keep, swap(send, z_mask(1))], axis=1), first[1])
    images = [swap(image, x_mask(k)) for k in range(1, 4)]

    def fetch(stack):
        return [stack] + [swap(stack, z_mask(j), y_mask(j)) for j in range(1, 4)]

    texts_a = fetch(jnp.stack(first[2:]))
    images[0] = after(images[0], texts_a[1], texts_a[3])
    images_own = jnp.concatenate([image, *images], axis=0)
    images_other = swap(images_own, CORE)
    texts_b = fetch(after(jnp.stack(first[:2]), texts_a[1], texts_a[3]))

    def small(n, shape, dtype=F32):
        return [jax.ShapeDtypeStruct(shape, dtype)] * n

    def tile(last, *args):
        images = small(2, (quarter, feats)) if last else small(1, (2 * quarter, feats))
        out_shape = small(1, (step, feats)) + small(3, (step + 8, feats), BF) + images + small(1, (8, 128))
        return pl.pallas_call(
            functools.partial(tile_kernel, last, rows, half, feats),
            out_shape=out_shape,
            in_specs=[SMEM, SMEM] + [HBM] * 6 + [VMEM] * (len(args) - 6),
            out_specs=[VMEM] * len(out_shape),
            scratch_shapes=[
                pltpu.VMEM((4, 2, rows, feats), BF),
                pltpu.VMEM((2 * quarter, feats), BF),
                pltpu.VMEM((4 * step, feats), BF),
                pltpu.VMEM((4 * step, 2 * quarter), BF),
                pltpu.VMEM((4, 2, rows, feats), F32),
                pltpu.SemaphoreType.DMA((6,)),
            ],
            compiler_params=grant(40),
            cost_estimate=pl.CostEstimate(
                flops=3 * 2 * 4 * step * 2 * quarter * feats, bytes_accessed=12 * 4 * step * feats, transcendentals=8 * step * quarter
            ),
            name="tile_last" if last else "tile_first",
        )(info, scales, *args)

    def call(kernel, name, out_shape, *args, scale=False):
        return pl.pallas_call(
            kernel,
            out_shape=out_shape,
            in_specs=[SMEM] * scale + [VMEM] * (len(args) - scale),
            out_specs=[VMEM] * len(out_shape),
            compiler_params=grant(20),
            name=name,
        )(*args)

    def give(messages):
        return [swap(m, z_mask(j), y_mask(j)) for j, m in zip((1, 2, 3), messages)]

    info = jnp.stack([core, z_lo]).astype(jnp.int32)
    scales = jnp.stack([scaling, logit_offset_term[0]])
    own_a, *messages, acc, sums = tile(False, *texts_a, images_own, images_other)
    got_a = give(messages)
    own_b, *messages, img_own, img_other, sums = tile(True, *texts_b, images_own, images_other, acc, sums)
    *messages, img_other, sums, _ = lax.optimization_barrier((*messages, img_other, sums, got_a))
    got_b = give(messages)

    img_got = swap(img_other, CORE)
    sums = sums + swap(sums, y_mask(1))
    n2, n3 = call(
        functools.partial(text_first_kernel, rows, feats, False), "text_first_a", small(2, (rows + 8, feats), BF), after(own_a, sums), *got_a
    )
    sums = sums + swap(sums, y_mask(2))
    sums = after(sums, n2, n3)
    sums = sums + swap(sums, z_mask(2))
    img, *messages = call(
        functools.partial(image_first_kernel, rows, feats), "image_first",
        small(1, (rows, feats)) + small(3, (rows + 8, feats), BF), img_own, img_got, sums,
    )
    img_got = [swap(m, x_mask(k)) for k, m in zip((1, 2, 3), messages)]
    got2, got3 = swap(n2, y_mask(2), z_mask(2)), swap(n3, y_mask(3), z_mask(3))
    text, n1 = call(
        functools.partial(text_first_kernel, rows, feats, True), "text_first_b",
        small(1, (rows, feats)) + small(1, (rows + 8, feats), BF), after(own_b, *messages), *got_b,
    )
    got1 = swap(after(n1, got2, got3), y_mask(1), z_mask(1))

    (img,) = call(
        functools.partial(image_last_kernel, rows, feats), "image_last", small(1, (rows + 8, feats)),
        logit_scaler, img, sums, *img_got, scale=True,
    )
    keep, got = img[:, :half], swap(img[:, half:], z_mask(1))
    image = jnp.concatenate(by(lo0, keep[:rows], got[:rows]), axis=0)
    sums = keep[rows:] + got[rows:]
    (text,) = call(text_last_kernel, "text_last", small(1, (rows, feats)), logit_scaler, text, got1, got2, got3, scale=True)
    whole = jnp.concatenate([text[:, :half], text[:, half:], image, sums], axis=0)
    mine, other = by(on0, whole[:, :width], whole[:, width:])
    other = swap(other, CORE)
    text_grad = jnp.concatenate(by(on0, mine[:step], other[:step]), axis=0)
    image_grad = jnp.concatenate(by(on0, mine[step : 2 * step], other[step : 2 * step]), axis=0)
    scalar_grads = mine[2 * step, :2] + other[2 * step, :2]
    return (image_grad, text_grad, scalar_grads)


def solution(mesh):
    placed = (P("batch", "dim"), P("batch", "dim"), P(), P())
    return jax.shard_map(
        body,
        mesh=mesh,
        in_specs=placed,
        out_specs=(P("batch", "dim"), P("batch", "dim"), P()),
        check_vma=False,
    )
```

```python
import functools

import jax
import jax.numpy as jnp
from jax import lax
from jax.experimental import pallas as pl
from jax.experimental.pallas import tpu as pltpu
from jax.sharding import PartitionSpec as P

BF = jnp.bfloat16
F32 = jnp.float32
AXES = ("batch", "dim")
CORE = 1


def x_mask(k):
    return k << 2


def y_mask(k):
    return k << 4


def z_mask(k):
    return ((k >> 1) << 6) | ((k & 1) << 1)


def swap(array, mask0, mask1=None):
    mask1 = mask0 if mask1 is None else mask1
    n = lax.axis_size("batch") * lax.axis_size("dim")
    return lax.ppermute(array, AXES, [(i, i ^ (mask1 if i & 1 else mask0)) for i in range(n)])


LOW = 2.0**-3.5


def encode(v, m):
    a = jnp.abs(v) * (127.0 * LOW / m) + LOW
    for _ in range(5):
        a = a * a
    return jnp.where(v < 0, -a, a)


def decode(code, m):
    c = code.astype(F32)
    a = jnp.exp(jnp.log(jnp.abs(c)) * (1.0 / 32.0)) * (1.0 / LOW) - 1.0
    v = a * (m * (1.0 / 127.0))
    return jnp.where(c < 0, -v, v)


def top_of(largest):
    return (largest * 1.01 + 1e-30).astype(BF).astype(F32)


def pairs(core_ref, rows, half, ta_ref, tb_ref, t_rel):
    on0, step = core_ref[0] == 0, 2 * rows
    for b in range(4):
        other = (ta_ref, tb_ref)[b >> 1]
        p0 = jnp.where(on0, ta_ref[b].astype(F32), other[2 * (b & 1)].astype(F32))
        p1 = jnp.where(on0, tb_ref[b].astype(F32), other[2 * (b & 1) + 1].astype(F32))
        top = jnp.concatenate([p0[:, :half], p1[:, :half]], axis=1)
        bottom = jnp.concatenate([p0[:, half:], p1[:, half:]], axis=1)
        t_rel[b * step : (b + 1) * step, :] = jnp.concatenate([top, bottom], axis=0).astype(BF)


def coefficients(near, rows, info_ref, scale_ref, t_rel, images, coeff_low):
    scaling, offset = scale_ref[0], scale_ref[1]
    step, columns = 2 * rows, images.shape[0]
    similar = lax.dot_general(t_rel[...], images[...], (((1,), (1,)), ((), ())), preferred_element_type=F32)
    temp, bias = jnp.zeros((1, columns), F32), jnp.zeros((1, columns), F32)
    for b in range(4):
        part = similar[b * step : (b + 1) * step]
        logits = scaling * part + offset
        if near and b == 0:
            row = lax.broadcasted_iota(jnp.int32, part.shape, 0)
            column = lax.broadcasted_iota(jnp.int32, part.shape, 1)
            matched = (row - rows * info_ref[1] == column) & (column < rows)
            sig = 1.0 / (1.0 + jnp.exp(jnp.where(matched, logits, -logits)))
            coeff = jnp.where(matched, -sig, sig)
        else:
            coeff = 1.0 / (1.0 + jnp.exp(-logits))
        coeff_low[b * step : (b + 1) * step, :] = coeff.astype(BF)
        temp = temp + jnp.sum(coeff * part, axis=0, keepdims=True)
        bias = bias + jnp.sum(coeff, axis=0, keepdims=True)
    even = lax.broadcasted_iota(jnp.int32, (8, 128), 1) % 2 == 0
    return jnp.where(even, jnp.sum(temp, axis=1, keepdims=True), jnp.sum(bias, axis=1, keepdims=True))


def text_parts(core_ref, rows, half, coeff_low, images, grads):
    on0, step = core_ref[0] == 0, 2 * rows
    part = jnp.dot(coeff_low[...], images[...], preferred_element_type=F32)
    for b in range(4):
        top, bottom = part[b * step : b * step + rows], part[b * step + rows : (b + 1) * step]
        for e, at in ((0, slice(0, half)), (1, slice(half, 2 * half))):
            place = jnp.where(on0, e, b >> 1), jnp.where(on0, b, 2 * (b & 1) + e)
            grads[place] = jnp.concatenate([top[:, at], bottom[:, at]], axis=1)


def image_parts(coeff_low, t_rel):
    return lax.dot_general(coeff_low[...], t_rel[...], (((0,), (0,)), ((), ())), preferred_element_type=F32)


def far_kernel(
    rows, half, feats, info_ref, scale_ref, ta_ref, tb_ref, im0_ref, im1_ref,
    ma_ref, mb_ref, acc_ref, sums_ref, images, t_rel, coeff_low, grads,
):
    quarter = 4 * rows
    images[0:quarter, :] = im0_ref[...]
    images[quarter : 2 * quarter, :] = im1_ref[...]
    pairs(info_ref, rows, half, ta_ref, tb_ref, t_rel)
    sums_ref[...] = coefficients(False, rows, info_ref, scale_ref, t_rel, images, coeff_low)
    text_parts(info_ref, rows, half, coeff_low, images, grads)
    for k, m_ref in ((0, ma_ref), (1, mb_ref)):
        m_ref[...] = message([grads[k, i] for i in range(4)], feats)
    acc_ref[...] = image_parts(coeff_low, t_rel)


def near_first_kernel(
    rows, half, feats, info_ref, scale_ref, ta_ref, tb_ref, im0_ref, im1_ref, sums_before,
    images, t_rel, coeff_low, sums_ref,
):
    quarter = 4 * rows
    images[0:quarter, :] = im0_ref[...]
    images[quarter : 2 * quarter, :] = im1_ref[...]
    pairs(info_ref, rows, half, ta_ref, tb_ref, t_rel)
    sums = coefficients(True, rows, info_ref, scale_ref, t_rel, images, coeff_low)
    sums_ref[...] = sums + sums_before[...]


def near_last_kernel(
    rows, half, feats, info_ref, images, t_rel, coeff_low, before_ref, own_ref, m_ref, img0_ref, *refs,
):
    others, grads = refs[:4], refs[4]
    quarter = 4 * rows
    text_parts(info_ref, rows, half, coeff_low, images, grads)
    own_ref[...] = jnp.concatenate([grads[0, i] for i in range(4)], axis=0)
    m_ref[...] = message([grads[1, i] for i in range(4)], feats)
    acc = image_parts(coeff_low, t_rel) + before_ref[...]
    img0_ref[...] = acc[0:quarter]
    for k, img_ref in enumerate(others):
        img_ref[...] = acc[quarter + k * rows : quarter + (k + 1) * rows]


def message(blocks, feats, extra=()):
    part = jnp.concatenate(blocks, axis=0)
    m = top_of(jnp.max(jnp.max(jnp.abs(part), axis=0, keepdims=True), axis=1, keepdims=True))
    tail = jnp.broadcast_to(m, (8 - len(extra), feats))
    return jnp.concatenate([encode(part, m), *extra, tail], axis=0).astype(BF)


def decoded(ref):
    whole = ref[...].astype(F32)
    n = whole.shape[0] - 8
    return decode(whole[:n], whole[n + 7 : n + 8]), whole[n:]


def split3(v):
    hi = v.astype(BF).astype(F32)
    mid = (v - hi).astype(BF).astype(F32)
    return [hi, mid, v - hi - mid]


def image_first_kernel(rows, feats, own_ref, *refs):
    others, (out_ref, *messages) = refs[:4], refs[4:]
    out_ref[...] = own_ref[0:rows] + others[0][...]
    for i, m_ref in enumerate(messages):
        m_ref[...] = message([own_ref[(i + 1) * rows : (i + 2) * rows] + others[i + 1][...]], feats)


def text_far_kernel(own_ref, r2_ref, out_ref):
    out_ref[...] = own_ref[...] + decoded(r2_ref)[0]


def text_first_kernel(rows, feats, own_ref, r1_ref, r3_ref, sums_ref, out_ref, *messages):
    total = own_ref[...] + decoded(r1_ref)[0] + decoded(r3_ref)[0]
    out_ref[...] = total[0:rows]
    scalars = [jnp.concatenate([v] * (feats // 128), axis=1) for v in split3(sums_ref[0:1, :])]
    for i, m_ref in enumerate(messages):
        m_ref[...] = message([total[(i + 1) * rows : (i + 2) * rows]], feats, scalars)


def image_last_kernel(scale_ref, own_ref, r1_ref, r2_ref, r3_ref, out_ref):
    total = own_ref[...]
    for r in (r1_ref, r2_ref, r3_ref):
        total = total + decoded(r)[0]
    out_ref[...] = total * scale_ref[0]


def text_last_kernel(rows, feats, scale_ref, own_ref, sums_ref, r1_ref, r2_ref, r3_ref, out_ref):
    total, tails = own_ref[...], []
    for r in (r1_ref, r2_ref, r3_ref):
        value, tail = decoded(r)
        total = total + value
        tails.append(tail[0:1, :128] + (tail[1:2, :128] + tail[2:3, :128]))
    sums = (sums_ref[0:1, :] + tails[0]) + (tails[1] + tails[2])
    sums = jnp.broadcast_to(jnp.concatenate([sums] * (feats // 128), axis=1), (8, feats))
    out_ref[...] = jnp.concatenate([total * scale_ref[0], sums], axis=0)


VMEM = pl.BlockSpec(memory_space=pltpu.VMEM)
SMEM = pl.BlockSpec(memory_space=pltpu.SMEM)


def grant(mib):
    return pltpu.CompilerParams(vmem_limit_bytes=mib * 1024 * 1024)


def after(array, *others):
    return lax.optimization_barrier((array, *others))[0]


def body(picture_embeds, caption_embeds, logit_scaler, logit_offset_term):
    height, width = picture_embeds.shape
    rows, half, feats = height // 4, 2 * width, 4 * width
    step, quarter = 2 * rows, 4 * rows
    index = lax.axis_index("batch") * lax.axis_size("dim") + lax.axis_index("dim")
    core, z_lo = index & 1, (index >> 1) & 1
    on0, lo0 = core == 0, z_lo == 0
    scaling = logit_scaler[0]

    def by(first_one, own, other):
        return [jnp.where(first_one, own, other), jnp.where(first_one, other, own)]

    both = [jnp.concatenate([t[:step], i[:step]]) for t, i in ((caption_embeds, picture_embeds),)]
    both.append(jnp.concatenate([caption_embeds[step:], picture_embeds[step:]]))
    keep, send = by(on0, *both)
    chip = jnp.concatenate(by(on0, keep, swap(send, CORE)), axis=1)
    packed = jnp.concatenate([chip[:rows], chip[rows:step]], axis=1)
    keep, send = by(lo0, chip[step : step + rows], chip[step + rows :])
    first = [packed] + [swap(packed, y_mask(i), z_mask(i)) for i in range(1, 4)]
    image = jnp.concatenate([keep, swap(send, z_mask(1))], axis=1)
    stack = jnp.stack(first)
    second = [stack] + [swap(stack, z_mask(j), y_mask(j)) for j in range(1, 4)]
    images_own = jnp.concatenate([image] + [swap(image, x_mask(k)) for k in range(1, 4)], axis=0)
    images_other = swap(images_own, CORE)

    def f32(*shape):
        return jax.ShapeDtypeStruct(shape, F32)

    def bf16(*shape):
        return jax.ShapeDtypeStruct(shape, BF)

    def call(kernel, name, out_shape, *args, scalars=0, scratch=(), mib=20, products=0):
        return pl.pallas_call(
            kernel,
            out_shape=out_shape,
            in_specs=[SMEM] * scalars + [VMEM] * (len(args) - scalars),
            out_specs=[VMEM] * len(out_shape),
            scratch_shapes=scratch,
            compiler_params=grant(mib),
            cost_estimate=pl.CostEstimate(
                flops=products * 2 * quarter * 2 * quarter * 2 * feats,
                bytes_accessed=sum(a.size * a.dtype.itemsize for a in (*args, *out_shape)),
                transcendentals=products * 4 * quarter * quarter,
            ),
            name=name,
        )(*args)

    sizes = (rows, half, feats)
    info = jnp.stack([core, z_lo]).astype(jnp.int32)
    scales = jnp.stack([scaling, logit_offset_term[0]])
    images_shape, coeff_shape = (2 * quarter, feats), (2 * quarter, 2 * quarter)
    grads = pltpu.VMEM((2, 4, rows, feats), F32)
    m2, m3, acc, sums = call(
        functools.partial(far_kernel, *sizes), "tile_far",
        [bf16(quarter + 8, feats), bf16(quarter + 8, feats), f32(*images_shape), f32(8, 128)],
        info, scales, second[2], second[3], images_own, images_other,
        scalars=2, mib=40, products=3,
        scratch=[pltpu.VMEM(images_shape, BF), pltpu.VMEM(images_shape, BF), pltpu.VMEM(coeff_shape, BF), grads],
    )
    images, t_rel, coeff_low, sums = call(
        functools.partial(near_first_kernel, *sizes), "tile_near_first",
        [bf16(*images_shape), bf16(*images_shape), bf16(*coeff_shape), f32(8, 128)],
        info, scales, second[0], second[1], images_own, images_other, sums,
        scalars=2, mib=30, products=1,
    )
    text, m1, img_own, *img_others = call(
        functools.partial(near_last_kernel, *sizes), "tile_near_last",
        [f32(quarter, feats), bf16(quarter + 8, feats), f32(quarter, feats)] + [f32(rows, feats)] * 4,
        info, images, t_rel, coeff_low, acc,
        scalars=1, mib=30, products=2, scratch=[grads],
    )

    one = sums + swap(sums, x_mask(1))
    got2 = swap(m2, z_mask(2), y_mask(2))
    m1, m3, img_others, one, got2 = lax.optimization_barrier((m1, m3, img_others, one, got2))
    got1, got3 = swap(m1, z_mask(1), y_mask(1)), swap(m3, z_mask(3), y_mask(3))
    img, *messages = call(
        functools.partial(image_first_kernel, rows, feats), "image_first",
        [f32(rows, feats)] + [bf16(rows + 8, feats)] * 3, img_own, *[swap(part, CORE) for part in img_others],
    )
    sums = one
    for mask in ((x_mask(3),), (z_mask(1), y_mask(1)), (z_mask(3), y_mask(3))):
        sums = sums + swap(sums, *mask)
    img_got = [swap(m, x_mask(k)) for k, m in zip((1, 2, 3), messages)]
    (far,) = call(text_far_kernel, "text_far", [f32(quarter, feats)], after(text, *messages), got2)
    text, *messages = call(
        functools.partial(text_first_kernel, rows, feats), "text_first",
        [f32(rows, feats)] + [bf16(rows + 8, feats)] * 3, far, got1, got3, sums,
    )
    got = [swap(m, y_mask(i), z_mask(i)) for i, m in zip((1, 2, 3), messages)]

    (img,) = call(image_last_kernel, "image_last", [f32(rows, feats)], logit_scaler, img, *img_got, scalars=1)
    image = jnp.concatenate(by(lo0, img[:, :half], swap(img[:, half:], z_mask(1))), axis=0)
    (text,) = call(
        functools.partial(text_last_kernel, rows, feats), "text_last", [f32(rows + 8, feats)],
        logit_scaler, after(text, image), sums, *got, scalars=1,
    )
    whole = jnp.concatenate([text[:rows, :half], text[:rows, half:], image, text[rows:, :half]], axis=0)
    mine, other = by(on0, whole[:, :width], whole[:, width:])
    other = swap(other, CORE)
    text_grad = jnp.concatenate(by(on0, mine[:step], other[:step]), axis=0)
    image_grad = jnp.concatenate(by(on0, mine[step : 2 * step], other[step : 2 * step]), axis=0)
    scalar_grads = mine[2 * step, :2] + other[2 * step, :2]
    return (image_grad, text_grad, scalar_grads)


def solution(mesh):
    placed = (P("batch", "dim"), P("batch", "dim"), P(), P())
    return jax.shard_map(
        body,
        mesh=mesh,
        in_specs=placed,
        out_specs=(P("batch", "dim"), P("batch", "dim"), P()),
        check_vma=False,
    )
```

```python
import functools

import jax
import jax.numpy as jnp
from jax import lax
from jax.experimental import pallas as pl
from jax.experimental.pallas import tpu as pltpu
from jax.sharding import PartitionSpec as P

BF = jnp.bfloat16
F32 = jnp.float32
AXES = ("batch", "dim")
CORE = 1


def x_mask(k):
    return k << 2


def y_mask(k):
    return k << 4


def z_mask(k):
    return ((k >> 1) << 6) | ((k & 1) << 1)


def swap(array, mask0, mask1=None):
    mask1 = mask0 if mask1 is None else mask1
    n = lax.axis_size("batch") * lax.axis_size("dim")
    return lax.ppermute(array, AXES, [(i, i ^ (mask1 if i & 1 else mask0)) for i in range(n)])


LOW = 2.0**-3.5


def encode(v, m):
    a = jnp.abs(v) * (127.0 * LOW / m) + LOW
    for _ in range(5):
        a = a * a
    return jnp.where(v < 0, -a, a)


def decode(code, m):
    c = code.astype(F32)
    a = jnp.exp(jnp.log(jnp.abs(c)) * (1.0 / 32.0)) * (1.0 / LOW) - 1.0
    v = a * (m * (1.0 / 127.0))
    return jnp.where(c < 0, -v, v)


def top_of(largest):
    return (largest * 1.01 + 1e-30).astype(BF).astype(F32)


def pairs(core_ref, rows, half, ta_ref, tb_ref, t_rel):
    on0, step = core_ref[0] == 0, 2 * rows
    for b in range(4):
        other = (ta_ref, tb_ref)[b >> 1]
        p0 = jnp.where(on0, ta_ref[b].astype(F32), other[2 * (b & 1)].astype(F32))
        p1 = jnp.where(on0, tb_ref[b].astype(F32), other[2 * (b & 1) + 1].astype(F32))
        top = jnp.concatenate([p0[:, :half], p1[:, :half]], axis=1)
        bottom = jnp.concatenate([p0[:, half:], p1[:, half:]], axis=1)
        t_rel[b * step : (b + 1) * step, :] = jnp.concatenate([top, bottom], axis=0).astype(BF)


def coefficients(near, rows, info_ref, scale_ref, t_rel, images, coeff_low):
    scaling, offset = scale_ref[0], scale_ref[1]
    step, columns = 2 * rows, images.shape[0]
    similar = lax.dot_general(t_rel[...], images[...], (((1,), (1,)), ((), ())), preferred_element_type=F32)
    temp, bias = jnp.zeros((1, columns), F32), jnp.zeros((1, columns), F32)
    for b in range(4):
        part = similar[b * step : (b + 1) * step]
        logits = scaling * part + offset
        if near and b == 0:
            row = lax.broadcasted_iota(jnp.int32, part.shape, 0)
            column = lax.broadcasted_iota(jnp.int32, part.shape, 1)
            matched = (row - rows * info_ref[1] == column) & (column < rows)
            sig = 1.0 / (1.0 + jnp.exp(jnp.where(matched, logits, -logits)))
            coeff = jnp.where(matched, -sig, sig)
        else:
            coeff = 1.0 / (1.0 + jnp.exp(-logits))
        coeff_low[b * step : (b + 1) * step, :] = coeff.astype(BF)
        temp = temp + jnp.sum(coeff * part, axis=0, keepdims=True)
        bias = bias + jnp.sum(coeff, axis=0, keepdims=True)
    even = lax.broadcasted_iota(jnp.int32, (8, 128), 1) % 2 == 0
    return jnp.where(even, jnp.sum(temp, axis=1, keepdims=True), jnp.sum(bias, axis=1, keepdims=True))


def text_parts(core_ref, rows, half, coeff_low, images, grads):
    on0, step = core_ref[0] == 0, 2 * rows
    part = jnp.dot(coeff_low[...], images[...], preferred_element_type=F32)
    for b in range(4):
        top, bottom = part[b * step : b * step + rows], part[b * step + rows : (b + 1) * step]
        for e, at in ((0, slice(0, half)), (1, slice(half, 2 * half))):
            place = jnp.where(on0, e, b >> 1), jnp.where(on0, b, 2 * (b & 1) + e)
            grads[place] = jnp.concatenate([top[:, at], bottom[:, at]], axis=1)


def image_parts(coeff_low, t_rel):
    return lax.dot_general(coeff_low[...], t_rel[...], (((0,), (0,)), ((), ())), preferred_element_type=F32)


def far_kernel(
    rows, half, feats, info_ref, scale_ref, ta_ref, tb_ref, im0_ref, im1_ref,
    ma_ref, mb_ref, acc_ref, sums_ref, images, t_rel, coeff_low, grads,
):
    quarter = 4 * rows
    images[0:quarter, :] = im0_ref[...]
    images[quarter : 2 * quarter, :] = im1_ref[...]
    pairs(info_ref, rows, half, ta_ref, tb_ref, t_rel)
    sums_ref[...] = coefficients(False, rows, info_ref, scale_ref, t_rel, images, coeff_low)
    text_parts(info_ref, rows, half, coeff_low, images, grads)
    for k, m_ref in ((0, ma_ref), (1, mb_ref)):
        m_ref[...] = message([grads[k, i] for i in range(4)], feats)
    acc_ref[...] = image_parts(coeff_low, t_rel)


def near_first_kernel(
    rows, half, feats, info_ref, scale_ref, ta_ref, tb_ref, im0_ref, im1_ref, sums_before,
    images, t_rel, coeff_low, sums_ref,
):
    quarter = 4 * rows
    images[0:quarter, :] = im0_ref[...]
    images[quarter : 2 * quarter, :] = im1_ref[...]
    pairs(info_ref, rows, half, ta_ref, tb_ref, t_rel)
    sums = coefficients(True, rows, info_ref, scale_ref, t_rel, images, coeff_low)
    sums_ref[...] = sums + sums_before[...]


def near_last_kernel(
    rows, half, feats, info_ref, images, t_rel, coeff_low, before_ref, own_ref, m_ref, img0_ref, *refs,
):
    others, grads = refs[:4], refs[4]
    quarter = 4 * rows
    text_parts(info_ref, rows, half, coeff_low, images, grads)
    own_ref[...] = jnp.concatenate([grads[0, i] for i in range(4)], axis=0)
    m_ref[...] = message([grads[1, i] for i in range(4)], feats)
    acc = image_parts(coeff_low, t_rel) + before_ref[...]
    img0_ref[...] = acc[0:quarter]
    for k, img_ref in enumerate(others):
        img_ref[...] = acc[quarter + k * rows : quarter + (k + 1) * rows]


def message(blocks, feats, extra=()):
    part = jnp.concatenate(blocks, axis=0)
    m = top_of(jnp.max(jnp.max(jnp.abs(part), axis=0, keepdims=True), axis=1, keepdims=True))
    tail = jnp.broadcast_to(m, (8 - len(extra), feats))
    return jnp.concatenate([encode(part, m), *extra, tail], axis=0).astype(BF)


def decoded(ref):
    whole = ref[...].astype(F32)
    n = whole.shape[0] - 8
    return decode(whole[:n], whole[n + 7 : n + 8]), whole[n:]


def split3(v):
    hi = v.astype(BF).astype(F32)
    mid = (v - hi).astype(BF).astype(F32)
    return [hi, mid, v - hi - mid]


def image_first_kernel(rows, feats, own_ref, sums_ref, *refs):
    others, (out_ref, *messages) = refs[:4], refs[4:]
    out_ref[...] = own_ref[0:rows] + others[0][...]
    scalars = [jnp.concatenate([v] * (feats // 128), axis=1) for v in split3(sums_ref[0:1, :])]
    for i, m_ref in enumerate(messages):
        m_ref[...] = message([own_ref[(i + 1) * rows : (i + 2) * rows] + others[i + 1][...]], feats, scalars)


def image_last_kernel(feats, scale_ref, own_ref, sums_ref, r1_ref, r2_ref, r3_ref, out_ref):
    total, tails = own_ref[...], []
    for r in (r1_ref, r2_ref, r3_ref):
        value, tail = decoded(r)
        total = total + value
        tails.append(tail[0:1, :128] + (tail[1:2, :128] + tail[2:3, :128]))
    sums = (sums_ref[0:1, :] + tails[0]) + (tails[1] + tails[2])
    sums = jnp.broadcast_to(jnp.concatenate([sums] * (feats // 128), axis=1), (8, feats))
    out_ref[...] = jnp.concatenate([total * scale_ref[0], sums], axis=0)


def text_far_kernel(own_ref, r2_ref, out_ref):
    out_ref[...] = own_ref[...] + decoded(r2_ref)[0]


def text_first_kernel(rows, feats, own_ref, r1_ref, r3_ref, out_ref, *messages):
    total = own_ref[...] + decoded(r1_ref)[0] + decoded(r3_ref)[0]
    out_ref[...] = total[0:rows]
    for i, m_ref in enumerate(messages):
        m_ref[...] = message([total[(i + 1) * rows : (i + 2) * rows]], feats)


def text_last_kernel(scale_ref, own_ref, r1_ref, r2_ref, r3_ref, out_ref):
    total = own_ref[...]
    for r in (r1_ref, r2_ref, r3_ref):
        total = total + decoded(r)[0]
    out_ref[...] = total * scale_ref[0]


VMEM = pl.BlockSpec(memory_space=pltpu.VMEM)
SMEM = pl.BlockSpec(memory_space=pltpu.SMEM)


def grant(mib):
    return pltpu.CompilerParams(vmem_limit_bytes=mib * 1024 * 1024)


def after(array, *others):
    return lax.optimization_barrier((array, *others))[0]


def body(picture_embeds, caption_embeds, logit_scaler, logit_offset_term):
    height, width = picture_embeds.shape
    rows, half, feats = height // 4, 2 * width, 4 * width
    step, quarter = 2 * rows, 4 * rows
    index = lax.axis_index("batch") * lax.axis_size("dim") + lax.axis_index("dim")
    core, z_lo = index & 1, (index >> 1) & 1
    on0, lo0 = core == 0, z_lo == 0
    scaling = logit_scaler[0]

    def by(first_one, own, other):
        return [jnp.where(first_one, own, other), jnp.where(first_one, other, own)]

    both = [jnp.concatenate([t[:step], i[:step]]) for t, i in ((caption_embeds, picture_embeds),)]
    both.append(jnp.concatenate([caption_embeds[step:], picture_embeds[step:]]))
    keep, send = by(on0, *both)
    chip = jnp.concatenate(by(on0, keep, swap(send, CORE)), axis=1)
    packed = jnp.concatenate([chip[:rows], chip[rows:step]], axis=1)
    keep, send = by(lo0, chip[step : step + rows], chip[step + rows :])
    first = [packed] + [swap(packed, y_mask(i), z_mask(i)) for i in range(1, 4)]
    image = jnp.concatenate([keep, swap(send, z_mask(1))], axis=1)
    stack = jnp.stack(first)
    second = [stack] + [swap(stack, z_mask(j), y_mask(j)) for j in range(1, 4)]
    images_own = jnp.concatenate([image] + [swap(image, x_mask(k)) for k in range(1, 4)], axis=0)
    images_other = swap(images_own, CORE)

    def f32(*shape):
        return jax.ShapeDtypeStruct(shape, F32)

    def bf16(*shape):
        return jax.ShapeDtypeStruct(shape, BF)

    def call(kernel, name, out_shape, *args, scalars=0, scratch=(), mib=20, products=0):
        return pl.pallas_call(
            kernel,
            out_shape=out_shape,
            in_specs=[SMEM] * scalars + [VMEM] * (len(args) - scalars),
            out_specs=[VMEM] * len(out_shape),
            scratch_shapes=scratch,
            compiler_params=grant(mib),
            cost_estimate=pl.CostEstimate(
                flops=products * 2 * quarter * 2 * quarter * 2 * feats,
                bytes_accessed=sum(a.size * a.dtype.itemsize for a in (*args, *out_shape)),
                transcendentals=products * 4 * quarter * quarter,
            ),
            name=name,
        )(*args)

    sizes = (rows, half, feats)
    info = jnp.stack([core, z_lo]).astype(jnp.int32)
    scales = jnp.stack([scaling, logit_offset_term[0]])
    images_shape, coeff_shape = (2 * quarter, feats), (2 * quarter, 2 * quarter)
    grads = pltpu.VMEM((2, 4, rows, feats), F32)
    m2, m3, acc, sums = call(
        functools.partial(far_kernel, *sizes), "tile_far",
        [bf16(quarter + 8, feats), bf16(quarter + 8, feats), f32(*images_shape), f32(8, 128)],
        info, scales, second[2], second[3], images_own, images_other,
        scalars=2, mib=40, products=3,
        scratch=[pltpu.VMEM(images_shape, BF), pltpu.VMEM(images_shape, BF), pltpu.VMEM(coeff_shape, BF), grads],
    )
    images, t_rel, coeff_low, sums = call(
        functools.partial(near_first_kernel, *sizes), "tile_near_first",
        [bf16(*images_shape), bf16(*images_shape), bf16(*coeff_shape), f32(8, 128)],
        info, scales, second[0], second[1], images_own, images_other, sums,
        scalars=2, mib=30, products=1,
    )
    text, m1, img_own, *img_others = call(
        functools.partial(near_last_kernel, *sizes), "tile_near_last",
        [f32(quarter, feats), bf16(quarter + 8, feats), f32(quarter, feats)] + [f32(rows, feats)] * 4,
        info, images, t_rel, coeff_low, acc,
        scalars=1, mib=30, products=2, scratch=[grads],
    )

    one = sums + swap(sums, y_mask(1))
    got2 = swap(m2, z_mask(2), y_mask(2))
    m1, m3, img_others, one, got2 = lax.optimization_barrier((m1, m3, img_others, one, got2))
    got1, got3 = swap(m1, z_mask(1), y_mask(1)), swap(m3, z_mask(3), y_mask(3))
    sums = one + swap(one, y_mask(3))
    img, *messages = call(
        functools.partial(image_first_kernel, rows, feats), "image_first",
        [f32(rows, feats)] + [bf16(rows + 8, feats)] * 3, img_own, sums, *[swap(part, CORE) for part in img_others],
    )
    img_got = [swap(m, x_mask(k)) for k, m in zip((1, 2, 3), messages)]
    (far,) = call(text_far_kernel, "text_far", [f32(quarter, feats)], after(text, *messages), got2)
    text, *messages = call(
        functools.partial(text_first_kernel, rows, feats), "text_first",
        [f32(rows, feats)] + [bf16(rows + 8, feats)] * 3, far, got1, got3,
    )
    got = [swap(m, y_mask(i), z_mask(i)) for i, m in zip((1, 2, 3), messages)]

    img_got[0] = after(img_got[0], text)
    (img,) = call(
        functools.partial(image_last_kernel, feats), "image_last", [f32(rows + 8, feats)], logit_scaler, img, sums, *img_got, scalars=1
    )
    keep, back = img[:, :half], swap(img[:, half:], z_mask(1))
    image = jnp.concatenate(by(lo0, keep[:rows], back[:rows]), axis=0)
    sums = keep[rows:]
    sums = (sums + back[rows:]) + (swap(sums, z_mask(2)) + swap(sums, z_mask(3)))
    (text,) = call(text_last_kernel, "text_last", [f32(rows, feats)], logit_scaler, after(text, img, sums), *got, scalars=1)
    whole = jnp.concatenate([text[:, :half], text[:, half:], image, sums], axis=0)
    mine, other = by(on0, whole[:, :width], whole[:, width:])
    other = swap(other, CORE)
    text_grad = jnp.concatenate(by(on0, mine[:step], other[:step]), axis=0)
    image_grad = jnp.concatenate(by(on0, mine[step : 2 * step], other[step : 2 * step]), axis=0)
    return (image_grad, text_grad, mine[2 * step, :2] + other[2 * step, :2])


def solution(mesh):
    placed = (P("batch", "dim"), P("batch", "dim"), P(), P())
    return jax.shard_map(
        body,
        mesh=mesh,
        in_specs=placed,
        out_specs=(P("batch", "dim"), P("batch", "dim"), P()),
        check_vma=False,
    )
```

```python
import functools

import jax
import jax.numpy as jnp
from jax import lax
from jax.experimental import pallas as pl
from jax.experimental.pallas import tpu as pltpu
from jax.sharding import PartitionSpec as P

BF = jnp.bfloat16
F32 = jnp.float32
AXES = ("batch", "dim")
CORE = 1


def x_mask(k):
    return k << 2


def y_mask(k):
    return k << 4


def z_mask(k):
    return ((k >> 1) << 6) | ((k & 1) << 1)


def swap(array, mask0, mask1=None):
    mask1 = mask0 if mask1 is None else mask1
    n = lax.axis_size("batch") * lax.axis_size("dim")
    return lax.ppermute(array, AXES, [(i, i ^ (mask1 if i & 1 else mask0)) for i in range(n)])


LOW = 2.0**-3.5


def encode(v, m):
    a = jnp.abs(v) * (127.0 * LOW / m) + LOW
    for _ in range(5):
        a = a * a
    return jnp.where(v < 0, -a, a)


def decode(code, m):
    c = code.astype(F32)
    a = jnp.exp(jnp.log(jnp.abs(c)) * (1.0 / 32.0)) * (1.0 / LOW) - 1.0
    v = a * (m * (1.0 / 127.0))
    return jnp.where(c < 0, -v, v)


def top_of(largest):
    return (largest * 1.01 + 1e-30).astype(BF).astype(F32)


def pairs(core_ref, rows, half, ta_ref, tb_ref, t_rel):
    on0, step = core_ref[0] == 0, 2 * rows
    for b in range(4):
        other = (ta_ref, tb_ref)[b >> 1]
        p0 = jnp.where(on0, ta_ref[b].astype(F32), other[2 * (b & 1)].astype(F32))
        p1 = jnp.where(on0, tb_ref[b].astype(F32), other[2 * (b & 1) + 1].astype(F32))
        top = jnp.concatenate([p0[:, :half], p1[:, :half]], axis=1)
        bottom = jnp.concatenate([p0[:, half:], p1[:, half:]], axis=1)
        t_rel[b * step : (b + 1) * step, :] = jnp.concatenate([top, bottom], axis=0).astype(BF)


def coefficients(near, rows, info_ref, scale_ref, t_rel, images, coeff_low):
    scaling, offset = scale_ref[0], scale_ref[1]
    step, columns = 2 * rows, images.shape[0]
    similar = lax.dot_general(t_rel[...], images[...], (((1,), (1,)), ((), ())), preferred_element_type=F32)
    temp, bias = jnp.zeros((1, columns), F32), jnp.zeros((1, columns), F32)
    for b in range(4):
        part = similar[b * step : (b + 1) * step]
        logits = scaling * part + offset
        if near and b == 0:
            row = lax.broadcasted_iota(jnp.int32, part.shape, 0)
            column = lax.broadcasted_iota(jnp.int32, part.shape, 1)
            matched = (row - rows * info_ref[1] == column) & (column < rows)
            sig = 1.0 / (1.0 + jnp.exp(jnp.where(matched, logits, -logits)))
            coeff = jnp.where(matched, -sig, sig)
        else:
            coeff = 1.0 / (1.0 + jnp.exp(-logits))
        coeff_low[b * step : (b + 1) * step, :] = coeff.astype(BF)
        temp = temp + jnp.sum(coeff * part, axis=0, keepdims=True)
        bias = bias + jnp.sum(coeff, axis=0, keepdims=True)
    even = lax.broadcasted_iota(jnp.int32, (8, 128), 1) % 2 == 0
    return jnp.where(even, jnp.sum(temp, axis=1, keepdims=True), jnp.sum(bias, axis=1, keepdims=True))


def text_parts(core_ref, rows, half, coeff_low, images, grads):
    on0, step = core_ref[0] == 0, 2 * rows
    part = jnp.dot(coeff_low[...], images[...], preferred_element_type=F32)
    for b in range(4):
        top, bottom = part[b * step : b * step + rows], part[b * step + rows : (b + 1) * step]
        for e, at in ((0, slice(0, half)), (1, slice(half, 2 * half))):
            place = jnp.where(on0, e, b >> 1), jnp.where(on0, b, 2 * (b & 1) + e)
            grads[place] = jnp.concatenate([top[:, at], bottom[:, at]], axis=1)


def image_parts(coeff_low, t_rel):
    return lax.dot_general(coeff_low[...], t_rel[...], (((0,), (0,)), ((), ())), preferred_element_type=F32)


def far_kernel(
    rows, half, feats, info_ref, scale_ref, ta_ref, tb_ref, im0_ref, im1_ref,
    ma_ref, mb_ref, acc_ref, sums_ref, images, t_rel, coeff_low, grads,
):
    quarter = 4 * rows
    images[0:quarter, :] = im0_ref[...]
    images[quarter : 2 * quarter, :] = im1_ref[...]
    pairs(info_ref, rows, half, ta_ref, tb_ref, t_rel)
    sums_ref[...] = coefficients(False, rows, info_ref, scale_ref, t_rel, images, coeff_low)
    text_parts(info_ref, rows, half, coeff_low, images, grads)
    for k, m_ref in ((0, ma_ref), (1, mb_ref)):
        m_ref[...] = message([grads[k, i] for i in range(4)], feats)
    acc_ref[...] = image_parts(coeff_low, t_rel)


def near_first_kernel(
    rows, half, feats, info_ref, scale_ref, ta_ref, tb_ref, im0_ref, im1_ref, sums_before,
    images, t_rel, coeff_low, sums_ref,
):
    quarter = 4 * rows
    images[0:quarter, :] = im0_ref[...]
    images[quarter : 2 * quarter, :] = im1_ref[...]
    pairs(info_ref, rows, half, ta_ref, tb_ref, t_rel)
    sums = coefficients(True, rows, info_ref, scale_ref, t_rel, images, coeff_low)
    sums_ref[...] = sums + sums_before[...]


def near_text_kernel(rows, half, feats, info_ref, images, coeff_low, own_ref, m_ref, grads):
    text_parts(info_ref, rows, half, coeff_low, images, grads)
    own_ref[...] = jnp.concatenate([grads[0, i] for i in range(4)], axis=0)
    m_ref[...] = message([grads[1, i] for i in range(4)], feats)


def near_image_kernel(rows, t_rel, coeff_low, before_ref, own_ref, *others):
    quarter = 4 * rows
    acc = image_parts(coeff_low, t_rel) + before_ref[...]
    own_ref[...] = acc[0:quarter]
    for k, img_ref in enumerate(others):
        img_ref[...] = acc[quarter + k * rows : quarter + (k + 1) * rows]


def message(blocks, feats, extra=()):
    part = jnp.concatenate(blocks, axis=0)
    m = top_of(jnp.max(jnp.max(jnp.abs(part), axis=0, keepdims=True), axis=1, keepdims=True))
    tail = jnp.broadcast_to(m, (8 - len(extra), feats))
    return jnp.concatenate([encode(part, m), *extra, tail], axis=0).astype(BF)


def decoded(ref):
    whole = ref[...].astype(F32)
    n = whole.shape[0] - 8
    return decode(whole[:n], whole[n + 7 : n + 8]), whole[n:]


def split3(v):
    hi = v.astype(BF).astype(F32)
    mid = (v - hi).astype(BF).astype(F32)
    return [hi, mid, v - hi - mid]


def image_first_kernel(rows, feats, own_ref, sums_ref, *refs):
    others, (out_ref, *messages) = refs[:4], refs[4:]
    out_ref[...] = own_ref[0:rows] + others[0][...]
    scalars = [jnp.concatenate([v] * (feats // 128), axis=1) for v in split3(sums_ref[0:1, :])]
    for i, m_ref in enumerate(messages):
        m_ref[...] = message([own_ref[(i + 1) * rows : (i + 2) * rows] + others[i + 1][...]], feats, scalars)


def image_last_kernel(feats, scale_ref, own_ref, sums_ref, r1_ref, r2_ref, r3_ref, out_ref):
    total, tails = own_ref[...], []
    for r in (r1_ref, r2_ref, r3_ref):
        value, tail = decoded(r)
        total = total + value
        tails.append(tail[0:1, :128] + (tail[1:2, :128] + tail[2:3, :128]))
    sums = (sums_ref[0:1, :] + tails[0]) + (tails[1] + tails[2])
    sums = jnp.broadcast_to(jnp.concatenate([sums] * (feats // 128), axis=1), (8, feats))
    out_ref[...] = jnp.concatenate([total * scale_ref[0], sums], axis=0)


def text_far_kernel(own_ref, r2_ref, out_ref):
    out_ref[...] = own_ref[...] + decoded(r2_ref)[0]


def text_first_kernel(rows, feats, own_ref, r1_ref, r3_ref, out_ref, *messages):
    total = own_ref[...] + decoded(r1_ref)[0] + decoded(r3_ref)[0]
    out_ref[...] = total[0:rows]
    for i, m_ref in enumerate(messages):
        m_ref[...] = message([total[(i + 1) * rows : (i + 2) * rows]], feats)


def text_last_kernel(scale_ref, own_ref, r1_ref, r2_ref, r3_ref, out_ref):
    total = own_ref[...]
    for r in (r1_ref, r2_ref, r3_ref):
        total = total + decoded(r)[0]
    out_ref[...] = total * scale_ref[0]


VMEM = pl.BlockSpec(memory_space=pltpu.VMEM)
SMEM = pl.BlockSpec(memory_space=pltpu.SMEM)


def grant(mib):
    return pltpu.CompilerParams(vmem_limit_bytes=mib * 1024 * 1024)


def after(array, *others):
    return lax.optimization_barrier((array, *others))[0]


def body(picture_embeds, caption_embeds, logit_scaler, logit_offset_term):
    height, width = picture_embeds.shape
    rows, half, feats = height // 4, 2 * width, 4 * width
    step, quarter = 2 * rows, 4 * rows
    index = lax.axis_index("batch") * lax.axis_size("dim") + lax.axis_index("dim")
    core, z_lo = index & 1, (index >> 1) & 1
    on0, lo0 = core == 0, z_lo == 0
    scaling = logit_scaler[0]

    def by(first_one, own, other):
        return [jnp.where(first_one, own, other), jnp.where(first_one, other, own)]

    both = [jnp.concatenate([t[:step], i[:step]]) for t, i in ((caption_embeds, picture_embeds),)]
    both.append(jnp.concatenate([caption_embeds[step:], picture_embeds[step:]]))
    keep, send = by(on0, *both)
    chip = jnp.concatenate(by(on0, keep, swap(send, CORE)), axis=1)
    packed = jnp.concatenate([chip[:rows], chip[rows:step]], axis=1)
    keep, send = by(lo0, chip[step : step + rows], chip[step + rows :])
    first = [packed] + [swap(packed, y_mask(i), z_mask(i)) for i in range(1, 4)]
    image = jnp.concatenate([keep, swap(send, z_mask(1))], axis=1)
    stack = jnp.stack(first)
    second = [stack] + [swap(stack, z_mask(j), y_mask(j)) for j in range(1, 4)]
    images_own = jnp.concatenate([image] + [swap(image, x_mask(k)) for k in range(1, 4)], axis=0)
    images_other = swap(images_own, CORE)

    def f32(*shape):
        return jax.ShapeDtypeStruct(shape, F32)

    def bf16(*shape):
        return jax.ShapeDtypeStruct(shape, BF)

    def call(kernel, name, out_shape, *args, scalars=0, scratch=(), mib=20, products=0):
        return pl.pallas_call(
            kernel,
            out_shape=out_shape,
            in_specs=[SMEM] * scalars + [VMEM] * (len(args) - scalars),
            out_specs=[VMEM] * len(out_shape),
            scratch_shapes=scratch,
            compiler_params=grant(mib),
            cost_estimate=pl.CostEstimate(
                flops=products * 2 * quarter * 2 * quarter * 2 * feats,
                bytes_accessed=sum(a.size * a.dtype.itemsize for a in (*args, *out_shape)),
                transcendentals=products * 4 * quarter * quarter,
            ),
            name=name,
        )(*args)

    sizes = (rows, half, feats)
    info = jnp.stack([core, z_lo]).astype(jnp.int32)
    scales = jnp.stack([scaling, logit_offset_term[0]])
    images_shape, coeff_shape = (2 * quarter, feats), (2 * quarter, 2 * quarter)
    grads = pltpu.VMEM((2, 4, rows, feats), F32)
    m2, m3, acc, sums = call(
        functools.partial(far_kernel, *sizes), "tile_far",
        [bf16(quarter + 8, feats), bf16(quarter + 8, feats), f32(*images_shape), f32(8, 128)],
        info, scales, second[2], second[3], images_own, images_other,
        scalars=2, mib=40, products=3,
        scratch=[pltpu.VMEM(images_shape, BF), pltpu.VMEM(images_shape, BF), pltpu.VMEM(coeff_shape, BF), grads],
    )
    images, t_rel, coeff_low, sums = call(
        functools.partial(near_first_kernel, *sizes), "tile_near_first",
        [bf16(*images_shape), bf16(*images_shape), bf16(*coeff_shape), f32(8, 128)],
        info, scales, second[0], second[1], images_own, images_other, sums,
        scalars=2, mib=30, products=1,
    )
    two = sums + swap(sums, y_mask(1))
    img_own, *img_others = call(
        functools.partial(near_image_kernel, rows), "tile_near_image", [f32(quarter, feats)] + [f32(rows, feats)] * 4,
        t_rel, coeff_low, acc, mib=30, products=1,
    )
    coeff_low, two, img_own, img_others = lax.optimization_barrier((coeff_low, two, img_own, img_others))
    img_others = [swap(part, CORE) for part in img_others]
    sums = two + swap(two, y_mask(3))
    text, m1 = call(
        functools.partial(near_text_kernel, *sizes), "tile_near_text", [f32(quarter, feats), bf16(quarter + 8, feats)],
        info, images, coeff_low, scalars=1, mib=30, products=1, scratch=[grads],
    )
    got2 = swap(m2, z_mask(2), y_mask(2))
    m1, m3, sums, got2, img_others = lax.optimization_barrier((m1, m3, sums, got2, img_others))
    got1, got3 = swap(m1, z_mask(1), y_mask(1)), swap(m3, z_mask(3), y_mask(3))
    img, *messages = call(
        functools.partial(image_first_kernel, rows, feats), "image_first",
        [f32(rows, feats)] + [bf16(rows + 8, feats)] * 3, img_own, sums, *img_others,
    )
    img_got = [swap(m, x_mask(k)) for k, m in zip((1, 2, 3), messages)]
    (far,) = call(text_far_kernel, "text_far", [f32(quarter, feats)], after(text, *messages), got2)
    text, *messages = call(
        functools.partial(text_first_kernel, rows, feats), "text_first",
        [f32(rows, feats)] + [bf16(rows + 8, feats)] * 3, far, got1, got3,
    )
    got = [swap(m, y_mask(i), z_mask(i)) for i, m in zip((1, 2, 3), messages)]

    img_got[0] = after(img_got[0], text)
    (img,) = call(
        functools.partial(image_last_kernel, feats), "image_last", [f32(rows + 8, feats)], logit_scaler, img, sums, *img_got, scalars=1, products=1
    )
    (text,) = call(text_last_kernel, "text_last", [f32(rows, feats)], logit_scaler, text, *got, scalars=1, products=2)
    keep, back = img[:, :half], after(swap(img[:, half:], z_mask(1)), text)
    image = jnp.concatenate(by(lo0, keep[:rows], back[:rows]), axis=0)
    sums = keep[rows:]
    sums = (sums + back[rows:]) + (swap(sums, z_mask(2)) + swap(sums, z_mask(3)))
    whole = jnp.concatenate([text[:, :half], text[:, half:], image, sums], axis=0)
    mine, other = by(on0, whole[:, :width], whole[:, width:])
    other = swap(other, CORE)
    text_grad = jnp.concatenate(by(on0, mine[:step], other[:step]), axis=0)
    image_grad = jnp.concatenate(by(on0, mine[step : 2 * step], other[step : 2 * step]), axis=0)
    return (image_grad, text_grad, mine[2 * step, :2] + other[2 * step, :2])


def solution(mesh):
    placed = (P("batch", "dim"), P("batch", "dim"), P(), P())
    return jax.shard_map(
        body,
        mesh=mesh,
        in_specs=placed,
        out_specs=(P("batch", "dim"), P("batch", "dim"), P()),
        check_vma=False,
    )
```

```python
import functools

import jax
import jax.numpy as jnp
from jax import lax
from jax.experimental import pallas as pl
from jax.experimental.pallas import tpu as pltpu
from jax.sharding import PartitionSpec as P

BF = jnp.bfloat16
F32 = jnp.float32
AXES = ("batch", "dim")
CORE = 1


def x_mask(k):
    return k << 2


def y_mask(k):
    return k << 4


def z_mask(k):
    return ((k >> 1) << 6) | ((k & 1) << 1)


def swap(array, mask0, mask1=None):
    mask1 = mask0 if mask1 is None else mask1
    n = lax.axis_size("batch") * lax.axis_size("dim")
    return lax.ppermute(array, AXES, [(i, i ^ (mask1 if i & 1 else mask0)) for i in range(n)])


LOW = 2.0**-3.5


def encode(v, m):
    a = jnp.abs(v) * (127.0 * LOW / m) + LOW
    for _ in range(5):
        a = a * a
    return jnp.where(v < 0, -a, a)


def decode(code, m):
    c = code.astype(F32)
    a = jnp.exp(jnp.log(jnp.abs(c)) * (1.0 / 32.0)) * (1.0 / LOW) - 1.0
    v = a * (m * (1.0 / 127.0))
    return jnp.where(c < 0, -v, v)


def top_of(largest):
    return (largest * 1.01 + 1e-30).astype(BF).astype(F32)


def pairs(core_ref, rows, half, ta_ref, tb_ref, t_rel):
    on0, step = core_ref[0] == 0, 2 * rows
    for b in range(4):
        other = (ta_ref, tb_ref)[b >> 1]
        p0 = jnp.where(on0, ta_ref[b].astype(F32), other[2 * (b & 1)].astype(F32))
        p1 = jnp.where(on0, tb_ref[b].astype(F32), other[2 * (b & 1) + 1].astype(F32))
        top = jnp.concatenate([p0[:, :half], p1[:, :half]], axis=1)
        bottom = jnp.concatenate([p0[:, half:], p1[:, half:]], axis=1)
        t_rel[b * step : (b + 1) * step, :] = jnp.concatenate([top, bottom], axis=0).astype(BF)


def coefficients(near, rows, info_ref, scale_ref, t_rel, images, coeff_low):
    scaling, offset = scale_ref[0], scale_ref[1]
    step, columns = 2 * rows, images.shape[0]
    similar = lax.dot_general(t_rel[...], images[...], (((1,), (1,)), ((), ())), preferred_element_type=F32)
    temp, bias = jnp.zeros((1, columns), F32), jnp.zeros((1, columns), F32)
    for b in range(4):
        part = similar[b * step : (b + 1) * step]
        logits = scaling * part + offset
        if near and b == 0:
            row = lax.broadcasted_iota(jnp.int32, part.shape, 0)
            column = lax.broadcasted_iota(jnp.int32, part.shape, 1)
            matched = (row - rows * info_ref[1] == column) & (column < rows)
            sig = 1.0 / (1.0 + jnp.exp(jnp.where(matched, logits, -logits)))
            coeff = jnp.where(matched, -sig, sig)
        else:
            coeff = 1.0 / (1.0 + jnp.exp(-logits))
        coeff_low[b * step : (b + 1) * step, :] = coeff.astype(BF)
        temp = temp + jnp.sum(coeff * part, axis=0, keepdims=True)
        bias = bias + jnp.sum(coeff, axis=0, keepdims=True)
    even = lax.broadcasted_iota(jnp.int32, (8, 128), 1) % 2 == 0
    return jnp.where(even, jnp.sum(temp, axis=1, keepdims=True), jnp.sum(bias, axis=1, keepdims=True))


def text_parts(core_ref, rows, half, coeff_low, images, grads):
    on0, step = core_ref[0] == 0, 2 * rows
    part = jnp.dot(coeff_low[...], images[...], preferred_element_type=F32)
    for b in range(4):
        top, bottom = part[b * step : b * step + rows], part[b * step + rows : (b + 1) * step]
        for e, at in ((0, slice(0, half)), (1, slice(half, 2 * half))):
            place = jnp.where(on0, e, b >> 1), jnp.where(on0, b, 2 * (b & 1) + e)
            grads[place] = jnp.concatenate([top[:, at], bottom[:, at]], axis=1)


def image_parts(coeff_low, t_rel):
    return lax.dot_general(coeff_low[...], t_rel[...], (((0,), (0,)), ((), ())), preferred_element_type=F32)


def near_kernel(
    rows, half, feats, info_ref, scale_ref, ta_ref, tb_ref, im0_ref, im1_ref,
    own_ref, m_ref, acc_ref, sums_ref, images, t_rel, coeff_low, grads,
):
    quarter = 4 * rows
    images[0:quarter, :] = im0_ref[...]
    images[quarter : 2 * quarter, :] = im1_ref[...]
    pairs(info_ref, rows, half, ta_ref, tb_ref, t_rel)
    sums_ref[...] = coefficients(True, rows, info_ref, scale_ref, t_rel, images, coeff_low)
    text_parts(info_ref, rows, half, coeff_low, images, grads)
    own_ref[...] = jnp.concatenate([grads[0, i] for i in range(4)], axis=0)
    m_ref[...] = message([grads[1, i] for i in range(4)], feats)
    acc_ref[...] = image_parts(coeff_low, t_rel)


def far_kernel(
    rows, half, feats, info_ref, scale_ref, ta_ref, tb_ref, im0_ref, im1_ref, before_ref, sums_before,
    ma_ref, mb_ref, own_ref, other_ref, sums_ref, images, t_rel, coeff_low, grads,
):
    quarter = 4 * rows
    images[0:quarter, :] = im0_ref[...]
    images[quarter : 2 * quarter, :] = im1_ref[...]
    pairs(info_ref, rows, half, ta_ref, tb_ref, t_rel)
    sums_ref[...] = coefficients(False, rows, info_ref, scale_ref, t_rel, images, coeff_low) + sums_before[...]
    text_parts(info_ref, rows, half, coeff_low, images, grads)
    for k, m_ref in ((0, ma_ref), (1, mb_ref)):
        m_ref[...] = message([grads[k, i] for i in range(4)], feats)
    acc = image_parts(coeff_low, t_rel) + before_ref[...]
    own_ref[...] = acc[0:quarter]
    other_ref[...] = acc[quarter : 2 * quarter]


def message(blocks, feats, extra=()):
    part = jnp.concatenate(blocks, axis=0)
    m = top_of(jnp.max(jnp.max(jnp.abs(part), axis=0, keepdims=True), axis=1, keepdims=True))
    tail = jnp.broadcast_to(m, (8 - len(extra), feats))
    return jnp.concatenate([encode(part, m), *extra, tail], axis=0).astype(BF)


def decoded(ref):
    whole = ref[...].astype(F32)
    n = whole.shape[0] - 8
    return decode(whole[:n], whole[n + 7 : n + 8]), whole[n:]


def split3(v):
    hi = v.astype(BF).astype(F32)
    mid = (v - hi).astype(BF).astype(F32)
    return [hi, mid, v - hi - mid]


def image_first_kernel(rows, feats, own_ref, other_ref, out_ref, *messages):
    total = own_ref[...] + other_ref[...]
    out_ref[...] = total[0:rows]
    for i, m_ref in enumerate(messages):
        m_ref[...] = message([total[(i + 1) * rows : (i + 2) * rows]], feats)


def image_last_kernel(scale_ref, own_ref, r1_ref, r2_ref, r3_ref, out_ref):
    total = own_ref[...]
    for r in (r1_ref, r2_ref, r3_ref):
        total = total + decoded(r)[0]
    out_ref[...] = total * scale_ref[0]


def text_near_kernel(own_ref, r1_ref, out_ref):
    out_ref[...] = own_ref[...] + decoded(r1_ref)[0]


def text_first_kernel(rows, feats, own_ref, r2_ref, r3_ref, sums_ref, out_ref, *messages):
    total = own_ref[...] + decoded(r2_ref)[0] + decoded(r3_ref)[0]
    out_ref[...] = total[0:rows]
    scalars = [jnp.concatenate([v] * (feats // 128), axis=1) for v in split3(sums_ref[0:1, :])]
    for i, m_ref in enumerate(messages):
        m_ref[...] = message([total[(i + 1) * rows : (i + 2) * rows]], feats, scalars)


def text_last_kernel(feats, scale_ref, own_ref, sums_ref, r1_ref, r2_ref, r3_ref, out_ref):
    total, tails = own_ref[...], []
    for r in (r1_ref, r2_ref, r3_ref):
        value, tail = decoded(r)
        total = total + value
        tails.append(tail[0:1, :128] + (tail[1:2, :128] + tail[2:3, :128]))
    sums = (sums_ref[0:1, :] + tails[0]) + (tails[1] + tails[2])
    sums = jnp.broadcast_to(jnp.concatenate([sums] * (feats // 128), axis=1), (8, feats))
    out_ref[...] = jnp.concatenate([total * scale_ref[0], sums], axis=0)


VMEM = pl.BlockSpec(memory_space=pltpu.VMEM)
SMEM = pl.BlockSpec(memory_space=pltpu.SMEM)


def grant(mib):
    return pltpu.CompilerParams(vmem_limit_bytes=mib * 1024 * 1024)


def after(array, *others):
    return lax.optimization_barrier((array, *others))[0]


def body(picture_embeds, caption_embeds, logit_scaler, logit_offset_term):
    height, width = picture_embeds.shape
    rows, half, feats = height // 4, 2 * width, 4 * width
    step, quarter = 2 * rows, 4 * rows
    index = lax.axis_index("batch") * lax.axis_size("dim") + lax.axis_index("dim")
    core, z_lo = index & 1, (index >> 1) & 1
    on0, lo0 = core == 0, z_lo == 0
    scaling = logit_scaler[0]

    def by(first_one, own, other):
        return [jnp.where(first_one, own, other), jnp.where(first_one, other, own)]

    both = [jnp.concatenate([t[:step], i[:step]]) for t, i in ((caption_embeds, picture_embeds),)]
    both.append(jnp.concatenate([caption_embeds[step:], picture_embeds[step:]]))
    keep, send = by(on0, *both)
    chip = jnp.concatenate(by(on0, keep, swap(send, CORE)), axis=1)
    packed = jnp.concatenate([chip[:rows], chip[rows:step]], axis=1)
    keep, send = by(lo0, chip[step : step + rows], chip[step + rows :])
    first = [packed] + [swap(packed, y_mask(i), z_mask(i)) for i in range(1, 4)]
    image = jnp.concatenate([keep, swap(send, z_mask(1))], axis=1)
    stack = jnp.stack(first)
    second1, second3 = (swap(stack, z_mask(j), y_mask(j)) for j in (1, 3))
    images_own = jnp.concatenate([image] + [swap(image, x_mask(k)) for k in range(1, 4)], axis=0)
    images_other = swap(images_own, CORE)
    second2 = swap(after(stack, images_own), z_mask(2), y_mask(2))

    def f32(*shape):
        return jax.ShapeDtypeStruct(shape, F32)

    def bf16(*shape):
        return jax.ShapeDtypeStruct(shape, BF)

    def call(kernel, name, out_shape, *args, scalars=0, scratch=(), mib=20, products=0, brief=False):
        return pl.pallas_call(
            kernel,
            out_shape=out_shape,
            in_specs=[SMEM] * scalars + [VMEM] * (len(args) - scalars),
            out_specs=[VMEM] * len(out_shape),
            scratch_shapes=scratch,
            compiler_params=grant(mib),
            cost_estimate=pl.CostEstimate(
                flops=products * 2 * quarter * 2 * quarter * 2 * feats,
                bytes_accessed=0 if brief else sum(a.size * a.dtype.itemsize for a in (*args, *out_shape)),
                transcendentals=products * 4 * quarter * quarter,
            ),
            name=name,
        )(*args)

    sizes = (rows, half, feats)
    info = jnp.stack([core, z_lo]).astype(jnp.int32)
    scales = jnp.stack([scaling, logit_offset_term[0]])
    images_shape, coeff_shape = (2 * quarter, feats), (2 * quarter, 2 * quarter)
    grads = pltpu.VMEM((2, 4, rows, feats), F32)
    scratch = [pltpu.VMEM(images_shape, BF), pltpu.VMEM(images_shape, BF), pltpu.VMEM(coeff_shape, BF), grads]
    text, m1, acc, sums = call(
        functools.partial(near_kernel, *sizes), "tile_near",
        [f32(quarter, feats), bf16(quarter + 8, feats), f32(*images_shape), f32(8, 128)],
        info, scales, stack, second1, images_own, images_other,
        scalars=2, mib=40, products=3, scratch=scratch,
    )
    m2, m3, img_own, img_other, sums = call(
        functools.partial(far_kernel, *sizes), "tile_far",
        [bf16(quarter + 8, feats), bf16(quarter + 8, feats), f32(quarter, feats), f32(quarter, feats), f32(8, 128)],
        info, scales, second2, second3, images_own, images_other, acc, sums,
        scalars=2, mib=40, products=3, scratch=scratch,
    )
    got1 = swap(m1, z_mask(1), y_mask(1))
    m2, m3, img_other, sums, got1 = lax.optimization_barrier((m2, m3, img_other, sums, got1))
    got2, got3 = swap(m2, z_mask(2), y_mask(2)), swap(m3, z_mask(3), y_mask(3))
    one = swap(sums, x_mask(1))
    img, *messages = call(
        functools.partial(image_first_kernel, rows, feats), "image_first",
        [f32(rows, feats)] + [bf16(rows + 8, feats)] * 3, img_own, swap(img_other, CORE),
    )
    *messages, one = lax.optimization_barrier((*messages, one))
    two = sums + one
    four = two + swap(two, x_mask(3))
    img_got = [swap(m, x_mask(k)) for k, m in zip((1, 2, 3), messages)]
    (text,) = call(text_near_kernel, "text_near", [f32(quarter, feats)], after(text, *messages, four), got1, products=3)
    s1, s2, s3 = (after(swap(four, z_mask(k), y_mask(k)), got2, got3) for k in (1, 2, 3))
    sums = (four + s1) + (s2 + s3)
    text, *messages = call(
        functools.partial(text_first_kernel, rows, feats), "text_first",
        [f32(rows, feats)] + [bf16(rows + 8, feats)] * 3, text, got2, got3, sums, brief=True,
    )
    got = [swap(m, y_mask(i), z_mask(i)) for i, m in zip((1, 2, 3), messages)]

    img_got[0] = after(img_got[0], text)
    (img,) = call(image_last_kernel, "image_last", [f32(rows, feats)], logit_scaler, img, *img_got, scalars=1, products=3)
    (text,) = call(
        functools.partial(text_last_kernel, feats), "text_last", [f32(rows + 8, feats)],
        logit_scaler, text, sums, *got, scalars=1, products=4,
    )
    image = jnp.concatenate(by(lo0, img[:, :half], after(swap(img[:, half:], z_mask(1)), text)), axis=0)
    whole = jnp.concatenate([text[:rows, :half], text[:rows, half:], image, text[rows:, :half]], axis=0)
    mine, other = by(on0, whole[:, :width], whole[:, width:])
    other = swap(other, CORE)
    text_grad = jnp.concatenate(by(on0, mine[:step], other[:step]), axis=0)
    image_grad = jnp.concatenate(by(on0, mine[step : 2 * step], other[step : 2 * step]), axis=0)
    return (image_grad, text_grad, mine[2 * step, :2] + other[2 * step, :2])


def solution(mesh):
    placed = (P("batch", "dim"), P("batch", "dim"), P(), P())
    return jax.shard_map(
        body,
        mesh=mesh,
        in_specs=placed,
        out_specs=(P("batch", "dim"), P("batch", "dim"), P()),
        check_vma=False,
    )
```

```python
import functools

import jax
import jax.numpy as jnp
from jax import lax
from jax.experimental import pallas as pl
from jax.experimental.pallas import tpu as pltpu
from jax.sharding import PartitionSpec as P

BF = jnp.bfloat16
F32 = jnp.float32
AXES = ("batch", "dim")
CORE = 1


def x_mask(k):
    return k << 2


def y_mask(k):
    return k << 4


def z_mask(k):
    return ((k >> 1) << 6) | ((k & 1) << 1)


def swap(array, mask0, mask1=None):
    mask1 = mask0 if mask1 is None else mask1
    n = lax.axis_size("batch") * lax.axis_size("dim")
    return lax.ppermute(array, AXES, [(i, i ^ (mask1 if i & 1 else mask0)) for i in range(n)])


LOW = 2.0**-3.5


def encode(v, m):
    a = jnp.abs(v) * (127.0 * LOW / m) + LOW
    for _ in range(5):
        a = a * a
    return jnp.where(v < 0, -a, a)


def decode(code, m):
    c = code.astype(F32)
    a = jnp.exp(jnp.log(jnp.abs(c)) * (1.0 / 32.0)) * (1.0 / LOW) - 1.0
    v = a * (m * (1.0 / 127.0))
    return jnp.where(c < 0, -v, v)


def top_of(largest):
    return (largest * 1.01 + 1e-30).astype(BF).astype(F32)


def pairs(core_ref, rows, half, ta_ref, tb_ref, t_rel):
    on0, step = core_ref[0] == 0, 2 * rows
    for b in range(4):
        other = (ta_ref, tb_ref)[b >> 1]
        p0 = jnp.where(on0, ta_ref[b].astype(F32), other[2 * (b & 1)].astype(F32))
        p1 = jnp.where(on0, tb_ref[b].astype(F32), other[2 * (b & 1) + 1].astype(F32))
        top = jnp.concatenate([p0[:, :half], p1[:, :half]], axis=1)
        bottom = jnp.concatenate([p0[:, half:], p1[:, half:]], axis=1)
        t_rel[b * step : (b + 1) * step, :] = jnp.concatenate([top, bottom], axis=0).astype(BF)


def coefficients(near, rows, info_ref, scale_ref, t_rel, images, coeff_low):
    scaling, offset = scale_ref[0], scale_ref[1]
    step, columns = 2 * rows, images.shape[0]
    similar = lax.dot_general(t_rel[...], images[...], (((1,), (1,)), ((), ())), preferred_element_type=F32)
    temp, bias = jnp.zeros((1, columns), F32), jnp.zeros((1, columns), F32)
    for b in range(4):
        part = similar[b * step : (b + 1) * step]
        logits = scaling * part + offset
        if near and b == 0:
            row = lax.broadcasted_iota(jnp.int32, part.shape, 0)
            column = lax.broadcasted_iota(jnp.int32, part.shape, 1)
            matched = (row - rows * info_ref[1] == column) & (column < rows)
            sig = 1.0 / (1.0 + jnp.exp(jnp.where(matched, logits, -logits)))
            coeff = jnp.where(matched, -sig, sig)
        else:
            coeff = 1.0 / (1.0 + jnp.exp(-logits))
        coeff_low[b * step : (b + 1) * step, :] = coeff.astype(BF)
        temp = temp + jnp.sum(coeff * part, axis=0, keepdims=True)
        bias = bias + jnp.sum(coeff, axis=0, keepdims=True)
    even = lax.broadcasted_iota(jnp.int32, (8, 128), 1) % 2 == 0
    return jnp.where(even, jnp.sum(temp, axis=1, keepdims=True), jnp.sum(bias, axis=1, keepdims=True))


def text_parts(core_ref, rows, half, coeff_low, images, grads):
    on0, step = core_ref[0] == 0, 2 * rows
    part = jnp.dot(coeff_low[...], images[...], preferred_element_type=F32)
    for b in range(4):
        top, bottom = part[b * step : b * step + rows], part[b * step + rows : (b + 1) * step]
        for e, at in ((0, slice(0, half)), (1, slice(half, 2 * half))):
            place = jnp.where(on0, e, b >> 1), jnp.where(on0, b, 2 * (b & 1) + e)
            grads[place] = jnp.concatenate([top[:, at], bottom[:, at]], axis=1)


def image_parts(coeff_low, t_rel):
    return lax.dot_general(coeff_low[...], t_rel[...], (((0,), (0,)), ((), ())), preferred_element_type=F32)


def near_kernel(
    rows, half, feats, info_ref, scale_ref, ta_ref, tb_ref, im0_ref, im1_ref,
    own_ref, m_ref, acc_ref, sums_ref, images, t_rel, coeff_low, grads,
):
    quarter = 4 * rows
    images[0:quarter, :] = im0_ref[...]
    images[quarter : 2 * quarter, :] = im1_ref[...]
    pairs(info_ref, rows, half, ta_ref, tb_ref, t_rel)
    sums_ref[...] = coefficients(True, rows, info_ref, scale_ref, t_rel, images, coeff_low)
    text_parts(info_ref, rows, half, coeff_low, images, grads)
    own_ref[...] = jnp.concatenate([grads[0, i] for i in range(4)], axis=0)
    m_ref[...] = message([grads[1, i] for i in range(4)], feats)
    acc_ref[...] = image_parts(coeff_low, t_rel)


def far_kernel(
    rows, half, feats, info_ref, scale_ref, ta_ref, tb_ref, im0_ref, im1_ref, before_ref, sums_before,
    ma_ref, mb_ref, own_ref, other_ref, images, t_rel, coeff_low, grads,
):
    quarter = 4 * rows
    images[0:quarter, :] = im0_ref[...]
    images[quarter : 2 * quarter, :] = im1_ref[...]
    pairs(info_ref, rows, half, ta_ref, tb_ref, t_rel)
    sums = coefficients(False, rows, info_ref, scale_ref, t_rel, images, coeff_low) + sums_before[...]
    text_parts(info_ref, rows, half, coeff_low, images, grads)
    for k, m_ref in ((0, ma_ref), (1, mb_ref)):
        m_ref[...] = message([grads[k, i] for i in range(4)], feats)
    acc = image_parts(coeff_low, t_rel) + before_ref[...]
    wide = jnp.concatenate([sums] * (feats // 128), axis=1)
    own_ref[...] = jnp.concatenate([acc[0:quarter], wide], axis=0)
    other_ref[...] = jnp.concatenate([acc[quarter : 2 * quarter], wide], axis=0)


def message(blocks, feats, extra=()):
    part = jnp.concatenate(blocks, axis=0)
    m = top_of(jnp.max(jnp.max(jnp.abs(part), axis=0, keepdims=True), axis=1, keepdims=True))
    tail = jnp.broadcast_to(m, (8 - len(extra), feats))
    return jnp.concatenate([encode(part, m), *extra, tail], axis=0).astype(BF)


def decoded(ref):
    whole = ref[...].astype(F32)
    n = whole.shape[0] - 8
    return decode(whole[:n], whole[n + 7 : n + 8]), whole[n:]


def split3(v):
    hi = v.astype(BF).astype(F32)
    mid = (v - hi).astype(BF).astype(F32)
    return [hi, mid, v - hi - mid]


def image_first_kernel(rows, feats, own_ref, other_ref, out_ref, *messages):
    total = own_ref[...] + other_ref[...]
    sums = total[4 * rows :]
    out_ref[...] = jnp.concatenate([total[0:rows], sums], axis=0)
    for i, m_ref in enumerate(messages):
        m_ref[...] = message([total[(i + 1) * rows : (i + 2) * rows]], feats, split3(sums[0:1]))


def with_scalars(own_ref, refs):
    n = own_ref.shape[0] - 8
    total, tails = own_ref[0:n, :], []
    for r in refs:
        value, tail = decoded(r)
        total = total + value
        tails.append(tail[0:1] + (tail[1:2] + tail[2:3]))
    return total, (own_ref[n : n + 1, :] + tails[0]) + (tails[1] + tails[2])


def image_last_kernel(feats, scale_ref, own_ref, r1_ref, r2_ref, r3_ref, out_ref, sums_ref):
    total, sums = with_scalars(own_ref, (r1_ref, r2_ref, r3_ref))
    out_ref[...] = total * scale_ref[0]
    sums_ref[...] = jnp.broadcast_to(sums, (8, feats))


def text_near_kernel(own_ref, r1_ref, out_ref):
    out_ref[...] = own_ref[...] + decoded(r1_ref)[0]


def text_first_kernel(rows, feats, own_ref, r2_ref, r3_ref, sums_ref, out_ref, *messages):
    total = own_ref[...] + decoded(r2_ref)[0] + decoded(r3_ref)[0]
    out_ref[...] = jnp.concatenate([total[0:rows], sums_ref[...]], axis=0)
    for i, m_ref in enumerate(messages):
        m_ref[...] = message([total[(i + 1) * rows : (i + 2) * rows]], feats, split3(sums_ref[0:1, :]))


def text_last_kernel(scale_ref, own_ref, r1_ref, r2_ref, r3_ref, out_ref, sums_ref):
    total, sums = with_scalars(own_ref, (r1_ref, r2_ref, r3_ref))
    out_ref[...] = total * scale_ref[0]
    sums_ref[...] = jnp.broadcast_to(sums[:, :128], (8, 128))


VMEM = pl.BlockSpec(memory_space=pltpu.VMEM)
SMEM = pl.BlockSpec(memory_space=pltpu.SMEM)


def grant(mib):
    return pltpu.CompilerParams(vmem_limit_bytes=mib * 1024 * 1024)


def after(array, *others):
    return lax.optimization_barrier((array, *others))[0]


def body(picture_embeds, caption_embeds, logit_scaler, logit_offset_term):
    height, width = picture_embeds.shape
    rows, half, feats = height // 4, 2 * width, 4 * width
    step, quarter = 2 * rows, 4 * rows
    index = lax.axis_index("batch") * lax.axis_size("dim") + lax.axis_index("dim")
    core, z_lo = index & 1, (index >> 1) & 1
    on0, lo0 = core == 0, z_lo == 0
    scaling = logit_scaler[0]

    def by(first_one, own, other):
        return [jnp.where(first_one, own, other), jnp.where(first_one, other, own)]

    both = [jnp.concatenate([t[:step], i[:step]]) for t, i in ((caption_embeds, picture_embeds),)]
    both.append(jnp.concatenate([caption_embeds[step:], picture_embeds[step:]]))
    keep, send = by(on0, *both)
    chip = jnp.concatenate(by(on0, keep, swap(send, CORE)), axis=1)
    packed = jnp.concatenate([chip[:rows], chip[rows:step]], axis=1)
    keep, send = by(lo0, chip[step : step + rows], chip[step + rows :])
    first = [packed] + [swap(packed, y_mask(i), z_mask(i)) for i in range(1, 4)]
    image = jnp.concatenate([keep, swap(send, z_mask(1))], axis=1)
    stack = jnp.stack(first)
    second1, second3 = (swap(stack, z_mask(j), y_mask(j)) for j in (1, 3))
    images_own = jnp.concatenate([image] + [swap(image, x_mask(k)) for k in range(1, 4)], axis=0)
    images_other = swap(images_own, CORE)
    second2 = swap(after(stack, images_own), z_mask(2), y_mask(2))
    second1, second3 = lax.optimization_barrier((second1, second3))

    def f32(*shape):
        return jax.ShapeDtypeStruct(shape, F32)

    def bf16(*shape):
        return jax.ShapeDtypeStruct(shape, BF)

    def call(kernel, name, out_shape, *args, scalars=0, scratch=(), mib=20, products=0, brief=False):
        return pl.pallas_call(
            kernel,
            out_shape=out_shape,
            in_specs=[SMEM] * scalars + [VMEM] * (len(args) - scalars),
            out_specs=[VMEM] * len(out_shape),
            scratch_shapes=scratch,
            compiler_params=grant(mib),
            cost_estimate=pl.CostEstimate(
                flops=products * 2 * quarter * 2 * quarter * 2 * feats,
                bytes_accessed=0 if brief else sum(a.size * a.dtype.itemsize for a in (*args, *out_shape)),
                transcendentals=products * 4 * quarter * quarter,
            ),
            name=name,
        )(*args)

    sizes = (rows, half, feats)
    info = jnp.stack([core, z_lo]).astype(jnp.int32)
    scales = jnp.stack([scaling, logit_offset_term[0]])
    images_shape, coeff_shape = (2 * quarter, feats), (2 * quarter, 2 * quarter)
    grads = pltpu.VMEM((2, 4, rows, feats), F32)
    scratch = [pltpu.VMEM(images_shape, BF), pltpu.VMEM(images_shape, BF), pltpu.VMEM(coeff_shape, BF), grads]
    text, m1, acc, sums = call(
        functools.partial(near_kernel, *sizes), "tile_near",
        [f32(quarter, feats), bf16(quarter + 8, feats), f32(*images_shape), f32(8, 128)],
        info, scales, stack, second1, images_own, images_other,
        scalars=2, mib=40, products=3, scratch=scratch,
    )
    m2, m3, img_own, img_other = call(
        functools.partial(far_kernel, *sizes), "tile_far",
        [bf16(quarter + 8, feats), bf16(quarter + 8, feats), f32(quarter + 8, feats), f32(quarter + 8, feats)],
        info, scales, second2, second3, images_own, images_other, acc, sums,
        scalars=2, mib=40, products=3, scratch=scratch,
    )
    got1 = swap(m1, z_mask(1), y_mask(1))
    m2, m3, img_other, got1 = lax.optimization_barrier((m2, m3, img_other, got1))
    got2, got3 = swap(m2, z_mask(2), y_mask(2)), swap(m3, z_mask(3), y_mask(3))
    img, *messages = call(
        functools.partial(image_first_kernel, rows, feats), "image_first",
        [f32(rows + 8, feats)] + [bf16(rows + 8, feats)] * 3, img_own, swap(img_other, CORE),
    )
    img_got = [swap(m, x_mask(k)) for k, m in zip((1, 2, 3), messages)]
    (text,) = call(text_near_kernel, "text_near", [f32(quarter, feats)], after(text, *messages), got1)
    img, sums = call(
        functools.partial(image_last_kernel, feats), "image_last", [f32(rows, feats), f32(8, feats)],
        logit_scaler, img, *img_got, scalars=1,
    )
    text, *messages = call(
        functools.partial(text_first_kernel, rows, feats), "text_first",
        [f32(rows + 8, feats)] + [bf16(rows + 8, feats)] * 3, text, got2, got3, sums,
    )
    got = [swap(m, y_mask(i), z_mask(i)) for i, m in zip((1, 2, 3), messages)]
    text, sums = call(
        text_last_kernel, "text_last", [f32(rows, feats), f32(8, 128)], logit_scaler, text, *got, scalars=1, products=2
    )
    image = jnp.concatenate(by(lo0, img[:, :half], after(swap(img[:, half:], z_mask(1)), text)), axis=0)
    whole = jnp.concatenate([text[:, :half], text[:, half:], image], axis=0)
    mine, other = by(on0, whole[:, :width], whole[:, width:])
    sums = after(sums, other)
    other = swap(other, CORE)
    text_grad = jnp.concatenate(by(on0, mine[:step], other[:step]), axis=0)
    image_grad = jnp.concatenate(by(on0, mine[step:], other[step:]), axis=0)
    s1, s2, s3 = (swap(sums, z_mask(k), y_mask(k)) for k in (1, 2, 3))
    sums = (sums + s1) + (s2 + s3)
    return (image_grad, text_grad, sums[0, :2])


def solution(mesh):
    placed = (P("batch", "dim"), P("batch", "dim"), P(), P())
    return jax.shard_map(
        body,
        mesh=mesh,
        in_specs=placed,
        out_specs=(P("batch", "dim"), P("batch", "dim"), P()),
        check_vma=False,
    )
```

```python
import functools

import jax
import jax.numpy as jnp
from jax import lax
from jax.experimental import pallas as pl
from jax.experimental.pallas import tpu as pltpu
from jax.sharding import PartitionSpec as P

BF = jnp.bfloat16
F32 = jnp.float32
AXES = ("batch", "dim")
CORE = 1


def x_mask(k):
    return k << 2


def y_mask(k):
    return k << 4


def z_mask(k):
    return ((k >> 1) << 6) | ((k & 1) << 1)


def swap(array, mask0, mask1=None):
    mask1 = mask0 if mask1 is None else mask1
    n = lax.axis_size("batch") * lax.axis_size("dim")
    return lax.ppermute(array, AXES, [(i, i ^ (mask1 if i & 1 else mask0)) for i in range(n)])


LOW = 2.0**-3.5


def encode(v, m):
    a = jnp.abs(v) * (127.0 * LOW / m) + LOW
    for _ in range(5):
        a = a * a
    return jnp.where(v < 0, -a, a)


def decode(code, m):
    c = code.astype(F32)
    a = jnp.exp(jnp.log(jnp.abs(c)) * (1.0 / 32.0)) * (1.0 / LOW) - 1.0
    v = a * (m * (1.0 / 127.0))
    return jnp.where(c < 0, -v, v)


def top_of(largest):
    return (largest * 1.01 + 1e-30).astype(BF).astype(F32)


def pairs(core_ref, rows, half, ta_ref, tb_ref, t_rel):
    on0, step = core_ref[0] == 0, 2 * rows
    for b in range(4):
        other = (ta_ref, tb_ref)[b >> 1]
        p0 = jnp.where(on0, ta_ref[b].astype(F32), other[2 * (b & 1)].astype(F32))
        p1 = jnp.where(on0, tb_ref[b].astype(F32), other[2 * (b & 1) + 1].astype(F32))
        top = jnp.concatenate([p0[:, :half], p1[:, :half]], axis=1)
        bottom = jnp.concatenate([p0[:, half:], p1[:, half:]], axis=1)
        t_rel[b * step : (b + 1) * step, :] = jnp.concatenate([top, bottom], axis=0).astype(BF)


def coefficients(near, rows, info_ref, scale_ref, t_rel, images, coeff_low):
    scaling, offset = scale_ref[0], scale_ref[1]
    step, columns = 2 * rows, images.shape[0]
    similar = lax.dot_general(t_rel[...], images[...], (((1,), (1,)), ((), ())), preferred_element_type=F32)
    temp, bias = jnp.zeros((1, columns), F32), jnp.zeros((1, columns), F32)
    for b in range(4):
        part = similar[b * step : (b + 1) * step]
        logits = scaling * part + offset
        if near and b == 0:
            row = lax.broadcasted_iota(jnp.int32, part.shape, 0)
            column = lax.broadcasted_iota(jnp.int32, part.shape, 1)
            matched = (row - rows * info_ref[1] == column) & (column < rows)
            sig = 1.0 / (1.0 + jnp.exp(jnp.where(matched, logits, -logits)))
            coeff = jnp.where(matched, -sig, sig)
        else:
            coeff = 1.0 / (1.0 + jnp.exp(-logits))
        coeff_low[b * step : (b + 1) * step, :] = coeff.astype(BF)
        temp = temp + jnp.sum(coeff * part, axis=0, keepdims=True)
        bias = bias + jnp.sum(coeff, axis=0, keepdims=True)
    even = lax.broadcasted_iota(jnp.int32, (8, 128), 1) % 2 == 0
    return jnp.where(even, jnp.sum(temp, axis=1, keepdims=True), jnp.sum(bias, axis=1, keepdims=True))


def text_parts(core_ref, rows, half, coeff_low, images, grads):
    on0, step = core_ref[0] == 0, 2 * rows
    part = jnp.dot(coeff_low[...], images[...], preferred_element_type=F32)
    for b in range(4):
        top, bottom = part[b * step : b * step + rows], part[b * step + rows : (b + 1) * step]
        for e, at in ((0, slice(0, half)), (1, slice(half, 2 * half))):
            place = jnp.where(on0, e, b >> 1), jnp.where(on0, b, 2 * (b & 1) + e)
            grads[place] = jnp.concatenate([top[:, at], bottom[:, at]], axis=1)


def image_parts(coeff_low, t_rel):
    return lax.dot_general(coeff_low[...], t_rel[...], (((0,), (0,)), ((), ())), preferred_element_type=F32)


def split_kernel(rows, info_ref, texts_ref, images_ref, keep_ref, send_ref):
    on0, step = info_ref[0] == 0, 2 * rows
    for at, ref in ((0, texts_ref), (step, images_ref)):
        whole = ref[...].astype(F32).T
        first, second = whole[:step], whole[step:]
        keep_ref[at : at + step, :] = jnp.where(on0, first, second).astype(BF)
        send_ref[at : at + step, :] = jnp.where(on0, second, first).astype(BF)


def join_kernel(rows, info_ref, own_ref, got_ref, texts_ref, images_ref):
    on0, step = info_ref[0] == 0, 2 * rows
    for at, ref in ((0, texts_ref), (step, images_ref)):
        own, got = own_ref[at : at + step, :], got_ref[at : at + step, :]
        ref[...] = jnp.concatenate([jnp.where(on0, own, got), jnp.where(on0, got, own)], axis=0).T


def near_kernel(
    rows, half, feats, info_ref, scale_ref, ta_ref, tb_ref, im0_ref, im1_ref,
    own_ref, m_ref, acc_ref, sums_ref, images, t_rel, coeff_low, grads,
):
    quarter = 4 * rows
    images[0:quarter, :] = im0_ref[...]
    images[quarter : 2 * quarter, :] = im1_ref[...]
    pairs(info_ref, rows, half, ta_ref, tb_ref, t_rel)
    sums_ref[...] = coefficients(True, rows, info_ref, scale_ref, t_rel, images, coeff_low)
    text_parts(info_ref, rows, half, coeff_low, images, grads)
    own_ref[...] = jnp.concatenate([grads[0, i] for i in range(4)], axis=0)
    m_ref[...] = message([grads[1, i] for i in range(4)], feats)
    acc_ref[...] = image_parts(coeff_low, t_rel)


def far_kernel(
    rows, half, feats, info_ref, scale_ref, ta_ref, tb_ref, im0_ref, im1_ref, before_ref, sums_before,
    ma_ref, mb_ref, own_ref, other_ref, images, t_rel, coeff_low, grads,
):
    quarter = 4 * rows
    images[0:quarter, :] = im0_ref[...]
    images[quarter : 2 * quarter, :] = im1_ref[...]
    pairs(info_ref, rows, half, ta_ref, tb_ref, t_rel)
    sums = coefficients(False, rows, info_ref, scale_ref, t_rel, images, coeff_low) + sums_before[...]
    text_parts(info_ref, rows, half, coeff_low, images, grads)
    for k, m_ref in ((0, ma_ref), (1, mb_ref)):
        m_ref[...] = message([grads[k, i] for i in range(4)], feats)
    acc = image_parts(coeff_low, t_rel) + before_ref[...]
    wide = jnp.concatenate([sums] * (feats // 128), axis=1)
    own_ref[...] = jnp.concatenate([acc[0:quarter], wide], axis=0)
    other_ref[...] = jnp.concatenate([acc[quarter : 2 * quarter], wide], axis=0)


def message(blocks, feats, extra=()):
    part = jnp.concatenate(blocks, axis=0)
    m = top_of(jnp.max(jnp.max(jnp.abs(part), axis=0, keepdims=True), axis=1, keepdims=True))
    tail = jnp.broadcast_to(m, (8 - len(extra), feats))
    return jnp.concatenate([encode(part, m), *extra, tail], axis=0).astype(BF)


def decoded(ref):
    whole = ref[...].astype(F32)
    n = whole.shape[0] - 8
    return decode(whole[:n], whole[n + 7 : n + 8]), whole[n:]


def split3(v):
    hi = v.astype(BF).astype(F32)
    mid = (v - hi).astype(BF).astype(F32)
    return [hi, mid, v - hi - mid]


def image_first_kernel(rows, feats, own_ref, other_ref, out_ref, *messages):
    total = own_ref[...] + other_ref[...]
    sums = total[4 * rows :]
    out_ref[...] = jnp.concatenate([total[0:rows], sums], axis=0)
    for i, m_ref in enumerate(messages):
        m_ref[...] = message([total[(i + 1) * rows : (i + 2) * rows]], feats, split3(sums[0:1]))


def with_scalars(own_ref, refs):
    n = own_ref.shape[0] - 8
    total, tails = own_ref[0:n, :], []
    for r in refs:
        value, tail = decoded(r)
        total = total + value
        tails.append(tail[0:1] + (tail[1:2] + tail[2:3]))
    return total, (own_ref[n : n + 1, :] + tails[0]) + (tails[1] + tails[2])


def image_last_kernel(feats, scale_ref, own_ref, r1_ref, r2_ref, r3_ref, out_ref, sums_ref):
    total, sums = with_scalars(own_ref, (r1_ref, r2_ref, r3_ref))
    out_ref[...] = total * scale_ref[0]
    sums_ref[...] = jnp.broadcast_to(sums, (8, feats))


def text_near_kernel(own_ref, r1_ref, out_ref):
    out_ref[...] = own_ref[...] + decoded(r1_ref)[0]


def text_first_kernel(rows, feats, own_ref, r2_ref, r3_ref, sums_ref, out_ref, *messages):
    total = own_ref[...] + decoded(r2_ref)[0] + decoded(r3_ref)[0]
    out_ref[...] = jnp.concatenate([total[0:rows], sums_ref[...]], axis=0)
    for i, m_ref in enumerate(messages):
        m_ref[...] = message([total[(i + 1) * rows : (i + 2) * rows]], feats, split3(sums_ref[0:1, :]))


def text_last_kernel(scale_ref, own_ref, r1_ref, r2_ref, r3_ref, out_ref, sums_ref):
    total, sums = with_scalars(own_ref, (r1_ref, r2_ref, r3_ref))
    out_ref[...] = total * scale_ref[0]
    sums_ref[...] = jnp.broadcast_to(sums[:, :128], (8, 128))


VMEM = pl.BlockSpec(memory_space=pltpu.VMEM)
SMEM = pl.BlockSpec(memory_space=pltpu.SMEM)


def grant(mib):
    return pltpu.CompilerParams(vmem_limit_bytes=mib * 1024 * 1024)


def after(array, *others):
    return lax.optimization_barrier((array, *others))[0]


def body(picture_embeds, caption_embeds, logit_scaler, logit_offset_term):
    height, width = picture_embeds.shape
    rows, half, feats = height // 4, 2 * width, 4 * width
    step, quarter = 2 * rows, 4 * rows
    index = lax.axis_index("batch") * lax.axis_size("dim") + lax.axis_index("dim")
    core, z_lo = index & 1, (index >> 1) & 1
    on0, lo0 = core == 0, z_lo == 0
    scaling = logit_scaler[0]

    def by(first_one, own, other):
        return [jnp.where(first_one, own, other), jnp.where(first_one, other, own)]

    def f32(*shape):
        return jax.ShapeDtypeStruct(shape, F32)

    def bf16(*shape):
        return jax.ShapeDtypeStruct(shape, BF)

    def call(kernel, name, out_shape, *args, scalars=0, scratch=(), mib=20, products=0, brief=False):
        return pl.pallas_call(
            kernel,
            out_shape=out_shape,
            in_specs=[SMEM] * scalars + [VMEM] * (len(args) - scalars),
            out_specs=[VMEM] * len(out_shape),
            scratch_shapes=scratch,
            compiler_params=grant(mib),
            cost_estimate=pl.CostEstimate(
                flops=products * 2 * quarter * 2 * quarter * 2 * feats,
                bytes_accessed=0 if brief else sum(a.size * a.dtype.itemsize for a in (*args, *out_shape)),
                transcendentals=products * 4 * quarter * quarter,
            ),
            name=name,
        )(*args)

    info = jnp.stack([core, z_lo]).astype(jnp.int32)
    keep, send = call(
        functools.partial(split_kernel, rows), "split", [bf16(height, width)] * 2, info, caption_embeds.T, picture_embeds.T, scalars=1
    )
    chip = jnp.concatenate(by(on0, keep, swap(send, CORE)), axis=1)
    packed = jnp.concatenate([chip[:rows], chip[rows:step]], axis=1)
    keep, send = by(lo0, chip[step : step + rows], chip[step + rows :])
    first = [packed] + [swap(packed, y_mask(i), z_mask(i)) for i in range(1, 4)]
    image = jnp.concatenate([keep, swap(send, z_mask(1))], axis=1)
    stack = jnp.stack(first)
    second1, second3 = (swap(stack, z_mask(j), y_mask(j)) for j in (1, 3))
    images_own = jnp.concatenate([image] + [swap(image, x_mask(k)) for k in range(1, 4)], axis=0)
    images_other = swap(images_own, CORE)
    second2 = swap(after(stack, images_own), z_mask(2), y_mask(2))
    second1, second3 = lax.optimization_barrier((second1, second3))

    sizes = (rows, half, feats)
    scales = jnp.stack([scaling, logit_offset_term[0]])
    images_shape, coeff_shape = (2 * quarter, feats), (2 * quarter, 2 * quarter)
    grads = pltpu.VMEM((2, 4, rows, feats), F32)
    scratch = [pltpu.VMEM(images_shape, BF), pltpu.VMEM(images_shape, BF), pltpu.VMEM(coeff_shape, BF), grads]
    text, m1, acc, sums = call(
        functools.partial(near_kernel, *sizes), "tile_near",
        [f32(quarter, feats), bf16(quarter + 8, feats), f32(*images_shape), f32(8, 128)],
        info, scales, stack, second1, images_own, images_other,
        scalars=2, mib=40, products=3, scratch=scratch,
    )
    m2, m3, img_own, img_other = call(
        functools.partial(far_kernel, *sizes), "tile_far",
        [bf16(quarter + 8, feats), bf16(quarter + 8, feats), f32(quarter + 8, feats), f32(quarter + 8, feats)],
        info, scales, second2, second3, images_own, images_other, acc, sums,
        scalars=2, mib=40, products=3, scratch=scratch,
    )
    got1 = swap(m1, z_mask(1), y_mask(1))
    img_other, got1 = lax.optimization_barrier((img_other, got1))
    got2, got3 = swap(m2, z_mask(2), y_mask(2)), swap(m3, z_mask(3), y_mask(3))
    img, *messages = call(
        functools.partial(image_first_kernel, rows, feats), "image_first",
        [f32(rows + 8, feats)] + [bf16(rows + 8, feats)] * 3, img_own, swap(img_other, CORE),
    )
    img_got = [swap(m, x_mask(k)) for k, m in zip((1, 2, 3), messages)]
    (text,) = call(text_near_kernel, "text_near", [f32(quarter, feats)], after(text, *messages), got1)
    img, sums = call(
        functools.partial(image_last_kernel, feats), "image_last", [f32(rows, feats), f32(8, feats)],
        logit_scaler, img, *img_got, scalars=1,
    )
    text, *messages = call(
        functools.partial(text_first_kernel, rows, feats), "text_first",
        [f32(rows + 8, feats)] + [bf16(rows + 8, feats)] * 3, text, got2, got3, sums,
    )
    got = [swap(m, y_mask(i), z_mask(i)) for i, m in zip((1, 2, 3), messages)]
    text, sums = call(
        text_last_kernel, "text_last", [f32(rows, feats), f32(8, 128)], logit_scaler, text, *got, scalars=1, products=2
    )
    image = jnp.concatenate(by(lo0, img[:, :half], after(swap(img[:, half:], z_mask(1)), text)), axis=0)
    whole = jnp.concatenate([text[:, :half], text[:, half:], image], axis=0)
    mine, other = by(on0, whole[:, :width], whole[:, width:])
    sums = after(sums, other)
    other = swap(other, CORE)
    sums = sums + swap(sums, z_mask(1), y_mask(1))
    mine = after(mine, sums)
    text_grad, image_grad = call(
        functools.partial(join_kernel, rows), "join", [f32(width, height)] * 2, info, mine, other, scalars=1
    )
    sums = sums + after(swap(sums, z_mask(3), y_mask(3)), text_grad, image_grad)
    return (image_grad.T, text_grad.T, sums[0, :2])


def solution(mesh):
    placed = (P("batch", "dim"), P("batch", "dim"), P(), P())
    return jax.shard_map(
        body,
        mesh=mesh,
        in_specs=placed,
        out_specs=(P("batch", "dim"), P("batch", "dim"), P()),
        check_vma=False,
    )
```

```python
import functools

import jax
import jax.numpy as jnp
from jax import lax
from jax.experimental import pallas as pl
from jax.experimental.pallas import tpu as pltpu
from jax.sharding import PartitionSpec as P

BF = jnp.bfloat16
F32 = jnp.float32
AXES = ("batch", "dim")
CORE = 1


def x_mask(k):
    return k << 2


def y_mask(k):
    return k << 4


def z_mask(k):
    return ((k >> 1) << 6) | ((k & 1) << 1)


def swap(array, mask0, mask1=None):
    mask1 = mask0 if mask1 is None else mask1
    n = lax.axis_size("batch") * lax.axis_size("dim")
    return lax.ppermute(array, AXES, [(i, i ^ (mask1 if i & 1 else mask0)) for i in range(n)])


LOW = 2.0**-3.5


def encode(v, m):
    a = jnp.abs(v) * (127.0 * LOW / m) + LOW
    for _ in range(5):
        a = a * a
    return jnp.where(v < 0, -a, a)


def decode(code, m):
    c = code.astype(F32)
    a = jnp.exp(jnp.log(jnp.abs(c)) * (1.0 / 32.0)) * (1.0 / LOW) - 1.0
    v = a * (m * (1.0 / 127.0))
    return jnp.where(c < 0, -v, v)


def top_of(largest):
    return (largest * 1.01 + 1e-30).astype(BF).astype(F32)


def pairs(core_ref, rows, half, ta_ref, tb_ref, t_rel):
    on0, step = core_ref[0] == 0, 2 * rows
    for b in range(4):
        other = (ta_ref, tb_ref)[b >> 1]
        p0 = jnp.where(on0, ta_ref[b].astype(F32), other[2 * (b & 1)].astype(F32))
        p1 = jnp.where(on0, tb_ref[b].astype(F32), other[2 * (b & 1) + 1].astype(F32))
        top = jnp.concatenate([p0[:, :half], p1[:, :half]], axis=1)
        bottom = jnp.concatenate([p0[:, half:], p1[:, half:]], axis=1)
        t_rel[b * step : (b + 1) * step, :] = jnp.concatenate([top, bottom], axis=0).astype(BF)


def coefficients(near, rows, info_ref, scale_ref, t_rel, images, coeff_low):
    scaling, offset = scale_ref[0], scale_ref[1]
    step, columns = 2 * rows, images.shape[0]
    similar = lax.dot_general(t_rel[...], images[...], (((1,), (1,)), ((), ())), preferred_element_type=F32)
    temp, bias = jnp.zeros((1, columns), F32), jnp.zeros((1, columns), F32)
    for b in range(4):
        part = similar[b * step : (b + 1) * step]
        logits = scaling * part + offset
        if near and b == 0:
            row = lax.broadcasted_iota(jnp.int32, part.shape, 0)
            column = lax.broadcasted_iota(jnp.int32, part.shape, 1)
            matched = (row - rows * info_ref[1] == column) & (column < rows)
            sig = 1.0 / (1.0 + jnp.exp(jnp.where(matched, logits, -logits)))
            coeff = jnp.where(matched, -sig, sig)
        else:
            coeff = 1.0 / (1.0 + jnp.exp(-logits))
        coeff_low[b * step : (b + 1) * step, :] = coeff.astype(BF)
        temp = temp + jnp.sum(coeff * part, axis=0, keepdims=True)
        bias = bias + jnp.sum(coeff, axis=0, keepdims=True)
    even = lax.broadcasted_iota(jnp.int32, (8, 128), 1) % 2 == 0
    return jnp.where(even, jnp.sum(temp, axis=1, keepdims=True), jnp.sum(bias, axis=1, keepdims=True))


def text_parts(core_ref, rows, half, coeff_low, images, grads):
    on0, step = core_ref[0] == 0, 2 * rows
    part = jnp.dot(coeff_low[...], images[...], preferred_element_type=F32)
    for b in range(4):
        top, bottom = part[b * step : b * step + rows], part[b * step + rows : (b + 1) * step]
        for e, at in ((0, slice(0, half)), (1, slice(half, 2 * half))):
            place = jnp.where(on0, e, b >> 1), jnp.where(on0, b, 2 * (b & 1) + e)
            grads[place] = jnp.concatenate([top[:, at], bottom[:, at]], axis=1)


def image_parts(coeff_low, t_rel):
    return lax.dot_general(coeff_low[...], t_rel[...], (((0,), (0,)), ((), ())), preferred_element_type=F32)


def split_kernel(rows, info_ref, texts_ref, images_ref, keep_ref, send_ref):
    on0, step = info_ref[0] == 0, 2 * rows
    for at, ref in ((0, texts_ref), (step, images_ref)):
        whole = ref[...].astype(F32).T
        first, second = whole[:step], whole[step:]
        keep_ref[at : at + step, :] = jnp.where(on0, first, second).astype(BF)
        send_ref[at : at + step, :] = jnp.where(on0, second, first).astype(BF)


def join_kernel(rows, info_ref, own_ref, got_ref, texts_ref, images_ref):
    on0, step = info_ref[0] == 0, 2 * rows
    for at, ref in ((0, texts_ref), (step, images_ref)):
        own, got = own_ref[at : at + step, :], got_ref[at : at + step, :]
        ref[...] = jnp.concatenate([jnp.where(on0, own, got), jnp.where(on0, got, own)], axis=0).T


def near_kernel(
    rows, half, feats, info_ref, scale_ref, ta_ref, tb_ref, im0_ref, im1_ref,
    own_ref, m_ref, t_rel, coeff_low, sums_ref, images, grads,
):
    quarter = 4 * rows
    images[0:quarter, :] = im0_ref[...]
    images[quarter : 2 * quarter, :] = im1_ref[...]
    pairs(info_ref, rows, half, ta_ref, tb_ref, t_rel)
    sums_ref[...] = coefficients(True, rows, info_ref, scale_ref, t_rel, images, coeff_low)
    text_parts(info_ref, rows, half, coeff_low, images, grads)
    own_ref[...] = jnp.concatenate([grads[0, i] for i in range(4)], axis=0)
    m_ref[...] = message([grads[1, i] for i in range(4)], feats)


def near_image_kernel(t_rel, coeff_low, acc_ref):
    acc_ref[...] = image_parts(coeff_low, t_rel)


def far_kernel(
    rows, half, feats, info_ref, scale_ref, ta_ref, tb_ref, im0_ref, im1_ref, before_ref, sums_before,
    ma_ref, mb_ref, own_ref, other_ref, images, t_rel, coeff_low, grads,
):
    quarter = 4 * rows
    images[0:quarter, :] = im0_ref[...]
    images[quarter : 2 * quarter, :] = im1_ref[...]
    pairs(info_ref, rows, half, ta_ref, tb_ref, t_rel)
    sums = coefficients(False, rows, info_ref, scale_ref, t_rel, images, coeff_low) + sums_before[...]
    text_parts(info_ref, rows, half, coeff_low, images, grads)
    for k, m_ref in ((0, ma_ref), (1, mb_ref)):
        m_ref[...] = message([grads[k, i] for i in range(4)], feats)
    acc = image_parts(coeff_low, t_rel) + before_ref[...]
    wide = jnp.concatenate([sums] * (feats // 128), axis=1)
    own_ref[...] = jnp.concatenate([acc[0:quarter], wide], axis=0)
    other_ref[...] = jnp.concatenate([acc[quarter : 2 * quarter], wide], axis=0)


def message(blocks, feats, extra=()):
    part = jnp.concatenate(blocks, axis=0)
    m = top_of(jnp.max(jnp.max(jnp.abs(part), axis=0, keepdims=True), axis=1, keepdims=True))
    tail = jnp.broadcast_to(m, (8 - len(extra), feats))
    return jnp.concatenate([encode(part, m), *extra, tail], axis=0).astype(BF)


def decoded(ref):
    whole = ref[...].astype(F32)
    n = whole.shape[0] - 8
    return decode(whole[:n], whole[n + 7 : n + 8]), whole[n:]


def split3(v):
    hi = v.astype(BF).astype(F32)
    mid = (v - hi).astype(BF).astype(F32)
    return [hi, mid, v - hi - mid]


def image_first_kernel(rows, feats, own_ref, other_ref, out_ref, *messages):
    total = own_ref[...] + other_ref[...]
    sums = total[4 * rows :]
    out_ref[...] = jnp.concatenate([total[0:rows], sums], axis=0)
    for i, m_ref in enumerate(messages):
        m_ref[...] = message([total[(i + 1) * rows : (i + 2) * rows]], feats, split3(sums[0:1]))


def with_scalars(own_ref, refs):
    n = own_ref.shape[0] - 8
    total, tails = own_ref[0:n, :], []
    for r in refs:
        value, tail = decoded(r)
        total = total + value
        tails.append(tail[0:1] + (tail[1:2] + tail[2:3]))
    return total, (own_ref[n : n + 1, :] + tails[0]) + (tails[1] + tails[2])


def image_last_kernel(feats, scale_ref, own_ref, r1_ref, r2_ref, r3_ref, out_ref, sums_ref):
    total, sums = with_scalars(own_ref, (r1_ref, r2_ref, r3_ref))
    out_ref[...] = total * scale_ref[0]
    sums_ref[...] = jnp.broadcast_to(sums, (8, feats))


def text_near_kernel(own_ref, r1_ref, out_ref):
    out_ref[...] = own_ref[...] + decoded(r1_ref)[0]


def text_first_kernel(rows, feats, own_ref, r2_ref, r3_ref, sums_ref, out_ref, *messages):
    total = own_ref[...] + decoded(r2_ref)[0] + decoded(r3_ref)[0]
    out_ref[...] = jnp.concatenate([total[0:rows], sums_ref[...]], axis=0)
    for i, m_ref in enumerate(messages):
        m_ref[...] = message([total[(i + 1) * rows : (i + 2) * rows]], feats, split3(sums_ref[0:1, :]))


def text_last_kernel(scale_ref, own_ref, r1_ref, r2_ref, r3_ref, out_ref, sums_ref):
    total, sums = with_scalars(own_ref, (r1_ref, r2_ref, r3_ref))
    out_ref[...] = total * scale_ref[0]
    sums_ref[...] = jnp.broadcast_to(sums[:, :128], (8, 128))


VMEM = pl.BlockSpec(memory_space=pltpu.VMEM)
SMEM = pl.BlockSpec(memory_space=pltpu.SMEM)


def grant(mib):
    return pltpu.CompilerParams(vmem_limit_bytes=mib * 1024 * 1024)


def after(array, *others):
    return lax.optimization_barrier((array, *others))[0]


def body(picture_embeds, caption_embeds, logit_scaler, logit_offset_term):
    height, width = picture_embeds.shape
    rows, half, feats = height // 4, 2 * width, 4 * width
    step, quarter = 2 * rows, 4 * rows
    index = lax.axis_index("batch") * lax.axis_size("dim") + lax.axis_index("dim")
    core, z_lo = index & 1, (index >> 1) & 1
    on0, lo0 = core == 0, z_lo == 0
    scaling = logit_scaler[0]

    def by(first_one, own, other):
        return [jnp.where(first_one, own, other), jnp.where(first_one, other, own)]

    def f32(*shape):
        return jax.ShapeDtypeStruct(shape, F32)

    def bf16(*shape):
        return jax.ShapeDtypeStruct(shape, BF)

    def call(kernel, name, out_shape, *args, scalars=0, scratch=(), mib=20, products=0, brief=False):
        return pl.pallas_call(
            kernel,
            out_shape=out_shape,
            in_specs=[SMEM] * scalars + [VMEM] * (len(args) - scalars),
            out_specs=[VMEM] * len(out_shape),
            scratch_shapes=scratch,
            compiler_params=grant(mib),
            cost_estimate=pl.CostEstimate(
                flops=products * 2 * quarter * 2 * quarter * 2 * feats,
                bytes_accessed=0 if brief else sum(a.size * a.dtype.itemsize for a in (*args, *out_shape)),
                transcendentals=products * 4 * quarter * quarter,
            ),
            name=name,
        )(*args)

    info = jnp.stack([core, z_lo]).astype(jnp.int32)
    keep, send = call(
        functools.partial(split_kernel, rows), "split", [bf16(height, width)] * 2, info, caption_embeds.T, picture_embeds.T, scalars=1
    )
    chip = jnp.concatenate(by(on0, keep, swap(send, CORE)), axis=1)
    packed = jnp.concatenate([chip[:rows], chip[rows:step]], axis=1)
    keep, send = by(lo0, chip[step : step + rows], chip[step + rows :])
    first = [packed] + [swap(packed, y_mask(i), z_mask(i)) for i in range(1, 4)]
    image = jnp.concatenate([keep, swap(send, z_mask(1))], axis=1)
    stack = jnp.stack(first)
    second1, second3 = (swap(stack, z_mask(j), y_mask(j)) for j in (1, 3))
    images_own = jnp.concatenate([image] + [swap(image, x_mask(k)) for k in range(1, 4)], axis=0)
    images_other = swap(images_own, CORE)
    second2 = swap(after(stack, images_own), z_mask(2), y_mask(2))
    second1, second3 = lax.optimization_barrier((second1, second3))

    sizes = (rows, half, feats)
    scales = jnp.stack([scaling, logit_offset_term[0]])
    images_shape, coeff_shape = (2 * quarter, feats), (2 * quarter, 2 * quarter)
    grads = pltpu.VMEM((2, 4, rows, feats), F32)
    scratch = [pltpu.VMEM(images_shape, BF), pltpu.VMEM(images_shape, BF), pltpu.VMEM(coeff_shape, BF), grads]
    text, m1, t_near, c_near, sums = call(
        functools.partial(near_kernel, *sizes), "tile_near",
        [f32(quarter, feats), bf16(quarter + 8, feats), bf16(*images_shape), bf16(*coeff_shape), f32(8, 128)],
        info, scales, stack, second1, images_own, images_other,
        scalars=2, mib=36, products=2, scratch=[scratch[0], grads],
    )
    got1 = swap(m1, z_mask(1), y_mask(1))
    (acc,) = call(near_image_kernel, "image_near", [f32(*images_shape)], t_near, c_near, mib=30, products=1)
    second2 = after(second2, acc)
    m2, m3, img_own, img_other = call(
        functools.partial(far_kernel, *sizes), "tile_far",
        [bf16(quarter + 8, feats), bf16(quarter + 8, feats), f32(quarter + 8, feats), f32(quarter + 8, feats)],
        info, scales, second2, second3, images_own, images_other, acc, sums,
        scalars=2, mib=40, products=3, scratch=scratch,
    )
    img_other, got1 = lax.optimization_barrier((img_other, got1))
    got2, got3 = swap(m2, z_mask(2), y_mask(2)), swap(m3, z_mask(3), y_mask(3))
    img, *messages = call(
        functools.partial(image_first_kernel, rows, feats), "image_first",
        [f32(rows + 8, feats)] + [bf16(rows + 8, feats)] * 3, img_own, swap(img_other, CORE),
    )
    img_got = [swap(m, x_mask(k)) for k, m in zip((1, 2, 3), messages)]
    (text,) = call(text_near_kernel, "text_near", [f32(quarter, feats)], after(text, *messages), got1)
    img, sums = call(
        functools.partial(image_last_kernel, feats), "image_last", [f32(rows, feats), f32(8, feats)],
        logit_scaler, img, *img_got, scalars=1,
    )
    text, *messages = call(
        functools.partial(text_first_kernel, rows, feats), "text_first",
        [f32(rows + 8, feats)] + [bf16(rows + 8, feats)] * 3, text, got2, got3, sums,
    )
    got = [swap(m, y_mask(i), z_mask(i)) for i, m in zip((1, 2, 3), messages)]
    text, sums = call(
        text_last_kernel, "text_last", [f32(rows, feats), f32(8, 128)], logit_scaler, text, *got, scalars=1, products=2
    )
    image = jnp.concatenate(by(lo0, img[:, :half], after(swap(img[:, half:], z_mask(1)), text)), axis=0)
    whole = jnp.concatenate([text[:, :half], text[:, half:], image], axis=0)
    mine, other = by(on0, whole[:, :width], whole[:, width:])
    sums = after(sums, other)
    other = swap(other, CORE)
    text_grad, image_grad = call(
        functools.partial(join_kernel, rows), "join", [f32(width, height)] * 2, info, mine, other, scalars=1
    )
    s1, s2, s3 = (after(swap(sums, z_mask(k), y_mask(k)), text_grad, image_grad) for k in (1, 2, 3))
    sums = (sums + s1) + (s2 + s3)
    return (image_grad.T, text_grad.T, sums[0, :2])


def solution(mesh):
    placed = (P("batch", "dim"), P("batch", "dim"), P(), P())
    return jax.shard_map(
        body,
        mesh=mesh,
        in_specs=placed,
        out_specs=(P("batch", "dim"), P("batch", "dim"), P()),
        check_vma=False,
    )
```

```python
import functools

import jax
import jax.numpy as jnp
from jax import lax
from jax.experimental import pallas as pl
from jax.experimental.pallas import tpu as pltpu
from jax.sharding import PartitionSpec as P

BF = jnp.bfloat16
F32 = jnp.float32
AXES = ("batch", "dim")
CORE = 1


def x_mask(k):
    return k << 2


def y_mask(k):
    return k << 4


def z_mask(k):
    return ((k >> 1) << 6) | ((k & 1) << 1)


def swap(array, mask0, mask1=None):
    mask1 = mask0 if mask1 is None else mask1
    n = lax.axis_size("batch") * lax.axis_size("dim")
    return lax.ppermute(array, AXES, [(i, i ^ (mask1 if i & 1 else mask0)) for i in range(n)])


LOW = 2.0**-3.5


def encode(v, m):
    a = jnp.abs(v) * (127.0 * LOW / m) + LOW
    for _ in range(5):
        a = a * a
    return jnp.where(v < 0, -a, a)


def decode(code, m):
    c = code.astype(F32)
    a = jnp.exp(jnp.log(jnp.abs(c)) * (1.0 / 32.0)) * (1.0 / LOW) - 1.0
    v = a * (m * (1.0 / 127.0))
    return jnp.where(c < 0, -v, v)


def top_of(largest):
    return (largest * 1.01 + 1e-30).astype(BF).astype(F32)


def pairs(core_ref, rows, half, ta_ref, tb_ref, t_rel):
    on0, step = core_ref[0] == 0, 2 * rows
    for b in range(4):
        other = (ta_ref, tb_ref)[b >> 1]
        p0 = jnp.where(on0, ta_ref[b].astype(F32), other[2 * (b & 1)].astype(F32))
        p1 = jnp.where(on0, tb_ref[b].astype(F32), other[2 * (b & 1) + 1].astype(F32))
        top = jnp.concatenate([p0[:, :half], p1[:, :half]], axis=1)
        bottom = jnp.concatenate([p0[:, half:], p1[:, half:]], axis=1)
        t_rel[b * step : (b + 1) * step, :] = jnp.concatenate([top, bottom], axis=0).astype(BF)


def coefficients(near, rows, info_ref, scale_ref, t_rel, images, coeff_low):
    scaling, offset = scale_ref[0], scale_ref[1]
    step, columns = 2 * rows, images.shape[0]
    similar = lax.dot_general(t_rel[...], images[...], (((1,), (1,)), ((), ())), preferred_element_type=F32)
    temp, bias = jnp.zeros((1, columns), F32), jnp.zeros((1, columns), F32)
    for b in range(4):
        part = similar[b * step : (b + 1) * step]
        logits = scaling * part + offset
        if near and b == 0:
            row = lax.broadcasted_iota(jnp.int32, part.shape, 0)
            column = lax.broadcasted_iota(jnp.int32, part.shape, 1)
            matched = (row - rows * info_ref[1] == column) & (column < rows)
            sig = 1.0 / (1.0 + jnp.exp(jnp.where(matched, logits, -logits)))
            coeff = jnp.where(matched, -sig, sig)
        else:
            coeff = 1.0 / (1.0 + jnp.exp(-logits))
        coeff_low[b * step : (b + 1) * step, :] = coeff.astype(BF)
        temp = temp + jnp.sum(coeff * part, axis=0, keepdims=True)
        bias = bias + jnp.sum(coeff, axis=0, keepdims=True)
    even = lax.broadcasted_iota(jnp.int32, (8, 128), 1) % 2 == 0
    return jnp.where(even, jnp.sum(temp, axis=1, keepdims=True), jnp.sum(bias, axis=1, keepdims=True))


def text_parts(core_ref, rows, half, coeff_low, images, grads):
    on0, step = core_ref[0] == 0, 2 * rows
    part = jnp.dot(coeff_low[...], images[...], preferred_element_type=F32)
    for b in range(4):
        top, bottom = part[b * step : b * step + rows], part[b * step + rows : (b + 1) * step]
        for e, at in ((0, slice(0, half)), (1, slice(half, 2 * half))):
            place = jnp.where(on0, e, b >> 1), jnp.where(on0, b, 2 * (b & 1) + e)
            grads[place] = jnp.concatenate([top[:, at], bottom[:, at]], axis=1)


def image_parts(coeff_low, t_rel):
    return lax.dot_general(coeff_low[...], t_rel[...], (((0,), (0,)), ((), ())), preferred_element_type=F32)


def split_kernel(rows, info_ref, texts_ref, images_ref, keep_ref, send_ref, both, sems):
    on0, step = info_ref[0] == 0, 2 * rows
    copies = [pltpu.make_async_copy(ref, both.at[k], sems.at[k]) for k, ref in enumerate((texts_ref, images_ref))]
    for copy in copies:
        copy.start()
    for k, at in ((0, 0), (1, step)):
        copies[k].wait()
        whole = both[k].astype(F32).T
        first, second = whole[:step], whole[step:]
        keep_ref[at : at + step, :] = jnp.where(on0, first, second).astype(BF)
        send_ref[at : at + step, :] = jnp.where(on0, second, first).astype(BF)


def join_kernel(rows, info_ref, own_ref, got_ref, texts_ref, images_ref):
    on0, step = info_ref[0] == 0, 2 * rows
    for at, ref in ((0, texts_ref), (step, images_ref)):
        own, got = own_ref[:, at : at + step], got_ref[:, at : at + step]
        ref[...] = jnp.concatenate([jnp.where(on0, own, got), jnp.where(on0, got, own)], axis=1)


def near_kernel(
    rows, half, feats, info_ref, scale_ref, ta_ref, tb_ref, im0_ref, im1_ref,
    own_ref, m_ref, t_rel, coeff_low, sums_ref, images, grads,
):
    quarter = 4 * rows
    images[0:quarter, :] = im0_ref[...]
    images[quarter : 2 * quarter, :] = im1_ref[...]
    pairs(info_ref, rows, half, ta_ref, tb_ref, t_rel)
    sums_ref[...] = coefficients(True, rows, info_ref, scale_ref, t_rel, images, coeff_low)
    text_parts(info_ref, rows, half, coeff_low, images, grads)
    own_ref[...] = jnp.concatenate([grads[0, i] for i in range(4)], axis=0)
    m_ref[...] = message([grads[1, i] for i in range(4)], feats)


def near_image_kernel(t_rel, coeff_low, acc_ref):
    acc_ref[...] = image_parts(coeff_low, t_rel)


def far_kernel(
    rows, half, feats, info_ref, scale_ref, ta_ref, tb_ref, im0_ref, im1_ref, before_ref, sums_before,
    ma_ref, mb_ref, own_ref, other_ref, images, t_rel, coeff_low, grads,
):
    quarter = 4 * rows
    images[0:quarter, :] = im0_ref[...]
    images[quarter : 2 * quarter, :] = im1_ref[...]
    pairs(info_ref, rows, half, ta_ref, tb_ref, t_rel)
    sums = coefficients(False, rows, info_ref, scale_ref, t_rel, images, coeff_low) + sums_before[...]
    text_parts(info_ref, rows, half, coeff_low, images, grads)
    for k, m_ref in ((0, ma_ref), (1, mb_ref)):
        m_ref[...] = message([grads[k, i] for i in range(4)], feats)
    acc = image_parts(coeff_low, t_rel) + before_ref[...]
    wide = jnp.concatenate([sums] * (feats // 128), axis=1)
    own_ref[...] = jnp.concatenate([acc[0:quarter], wide], axis=0)
    other_ref[...] = jnp.concatenate([acc[quarter : 2 * quarter], wide], axis=0)


def message(blocks, feats, extra=()):
    part = jnp.concatenate(blocks, axis=0)
    m = top_of(jnp.max(jnp.max(jnp.abs(part), axis=0, keepdims=True), axis=1, keepdims=True))
    tail = jnp.broadcast_to(m, (8 - len(extra), feats))
    return jnp.concatenate([encode(part, m), *extra, tail], axis=0).astype(BF)


def decoded(ref):
    whole = ref[...].astype(F32)
    n = whole.shape[0] - 8
    return decode(whole[:n], whole[n + 7 : n + 8]), whole[n:]


def split3(v):
    hi = v.astype(BF).astype(F32)
    mid = (v - hi).astype(BF).astype(F32)
    return [hi, mid, v - hi - mid]


def image_first_kernel(rows, feats, own_ref, other_ref, out_ref, *messages):
    total = own_ref[...] + other_ref[...]
    sums = total[4 * rows :]
    out_ref[...] = jnp.concatenate([total[0:rows], sums], axis=0)
    for i, m_ref in enumerate(messages):
        m_ref[...] = message([total[(i + 1) * rows : (i + 2) * rows]], feats, split3(sums[0:1]))


def with_scalars(own_ref, refs):
    n = own_ref.shape[0] - 8
    total, tails = own_ref[0:n, :], []
    for r in refs:
        value, tail = decoded(r)
        total = total + value
        tails.append(tail[0:1] + (tail[1:2] + tail[2:3]))
    return total, (own_ref[n : n + 1, :] + tails[0]) + (tails[1] + tails[2])


def image_last_kernel(feats, scale_ref, own_ref, r1_ref, r2_ref, r3_ref, out_ref, sums_ref):
    total, sums = with_scalars(own_ref, (r1_ref, r2_ref, r3_ref))
    out_ref[...] = total * scale_ref[0]
    sums_ref[...] = jnp.broadcast_to(sums, (8, feats))


def text_near_kernel(own_ref, r1_ref, out_ref):
    out_ref[...] = own_ref[...] + decoded(r1_ref)[0]


def text_first_kernel(rows, feats, own_ref, r2_ref, r3_ref, sums_ref, out_ref, m1_ref, m2_ref, m3_ref, total):
    tops = [r[4 * rows :, :].astype(F32)[7:8] for r in (r2_ref, r3_ref)]

    def add(step, carry):
        at = pl.ds(pl.multiple_of(step * 32, 32), 32)
        total[at, :] = own_ref[at, :] + decode(r2_ref[at, :], tops[0]) + decode(r3_ref[at, :], tops[1])
        return carry

    lax.fori_loop(0, 4 * rows // 32, add, 0)
    out_ref[...] = jnp.concatenate([total[0:rows, :], sums_ref[...]], axis=0)
    for i, m_ref in enumerate((m1_ref, m2_ref, m3_ref)):
        m_ref[...] = message([total[(i + 1) * rows : (i + 2) * rows, :]], feats, split3(sums_ref[0:1, :]))


def close_kernel(rows, width, info_ref, scale_ref, own_ref, r1_ref, r2_ref, r3_ref, img_ref, back_ref, mine_ref, other_ref, sums_ref):
    half = 2 * width
    on0, lo0 = info_ref[0] == 0, info_ref[1] == 0
    total, sums = with_scalars(own_ref, (r1_ref, r2_ref, r3_ref))
    text = total * scale_ref[0]
    sums_ref[...] = jnp.broadcast_to(sums[:, :128], (8, 128))
    keep, back = img_ref[:, :half], back_ref[...]
    parts = (text[:, :half], text[:, half:], jnp.where(lo0, keep, back), jnp.where(lo0, back, keep))
    whole = jnp.concatenate(parts, axis=0)
    left, right = whole[:, :width], whole[:, width:]
    mine_ref[...] = jnp.where(on0, left, right).T
    other_ref[...] = jnp.where(on0, right, left).T


VMEM = pl.BlockSpec(memory_space=pltpu.VMEM)
HBM = pl.BlockSpec(memory_space=pltpu.HBM)
SMEM = pl.BlockSpec(memory_space=pltpu.SMEM)


def grant(mib):
    return pltpu.CompilerParams(vmem_limit_bytes=mib * 1024 * 1024)


def after(array, *others):
    return lax.optimization_barrier((array, *others))[0]


def body(picture_embeds, caption_embeds, logit_scaler, logit_offset_term):
    height, width = picture_embeds.shape
    rows, half, feats = height // 4, 2 * width, 4 * width
    step, quarter = 2 * rows, 4 * rows
    index = lax.axis_index("batch") * lax.axis_size("dim") + lax.axis_index("dim")
    core, z_lo = index & 1, (index >> 1) & 1
    on0, lo0 = core == 0, z_lo == 0
    scaling = logit_scaler[0]

    def by(first_one, own, other):
        return [jnp.where(first_one, own, other), jnp.where(first_one, other, own)]

    def f32(*shape):
        return jax.ShapeDtypeStruct(shape, F32)

    def bf16(*shape):
        return jax.ShapeDtypeStruct(shape, BF)

    def call(kernel, name, out_shape, *args, scalars=0, scratch=(), mib=20, products=0, where=VMEM):
        return pl.pallas_call(
            kernel,
            out_shape=out_shape,
            in_specs=[SMEM] * scalars + [where] * (len(args) - scalars),
            out_specs=[VMEM] * len(out_shape),
            scratch_shapes=scratch,
            compiler_params=grant(mib),
            cost_estimate=pl.CostEstimate(
                flops=products * 2 * quarter * 2 * quarter * 2 * feats,
                bytes_accessed=sum(a.size * a.dtype.itemsize for a in (*args, *out_shape)),
                transcendentals=products * 4 * quarter * quarter,
            ),
            name=name,
        )(*args)

    info = jnp.stack([core, z_lo]).astype(jnp.int32)
    keep, send = call(
        functools.partial(split_kernel, rows), "split", [bf16(height, width)] * 2, info, caption_embeds.T, picture_embeds.T, scalars=1,
        where=HBM, mib=62, scratch=[pltpu.VMEM((2, width, height), BF), pltpu.SemaphoreType.DMA((2,))],
    )
    chip = jnp.concatenate(by(on0, keep, swap(send, CORE)), axis=1)
    packed = jnp.concatenate([chip[:rows], chip[rows:step]], axis=1)
    keep, send = by(lo0, chip[step : step + rows], chip[step + rows :])
    first = [packed] + [swap(packed, y_mask(i), z_mask(i)) for i in range(1, 4)]
    image = jnp.concatenate([keep, swap(send, z_mask(1))], axis=1)
    stack = jnp.stack(first)
    second1, second3 = (swap(stack, z_mask(j), y_mask(j)) for j in (1, 3))
    images_own = jnp.concatenate([image] + [swap(image, x_mask(k)) for k in range(1, 4)], axis=0)
    images_other = swap(images_own, CORE)
    second2 = swap(after(stack, images_own), z_mask(2), y_mask(2))
    second1, second3 = lax.optimization_barrier((second1, second3))

    sizes = (rows, half, feats)
    scales = jnp.stack([scaling, logit_offset_term[0]])
    images_shape, coeff_shape = (2 * quarter, feats), (2 * quarter, 2 * quarter)
    grads = pltpu.VMEM((2, 4, rows, feats), F32)
    scratch = [pltpu.VMEM(images_shape, BF), pltpu.VMEM(images_shape, BF), pltpu.VMEM(coeff_shape, BF), grads]
    text, m1, t_near, c_near, sums = call(
        functools.partial(near_kernel, *sizes), "tile_near",
        [f32(quarter, feats), bf16(quarter + 8, feats), bf16(*images_shape), bf16(*coeff_shape), f32(8, 128)],
        info, scales, stack, second1, images_own, images_other,
        scalars=2, mib=36, products=2, scratch=[scratch[0], grads],
    )
    got1 = swap(m1, z_mask(1), y_mask(1))
    (acc,) = call(near_image_kernel, "image_near", [f32(*images_shape)], t_near, c_near, mib=30, products=1)
    second2 = after(second2, acc)
    m2, m3, img_own, img_other = call(
        functools.partial(far_kernel, *sizes), "tile_far",
        [bf16(quarter + 8, feats), bf16(quarter + 8, feats), f32(quarter + 8, feats), f32(quarter + 8, feats)],
        info, scales, second2, second3, images_own, images_other, acc, sums,
        scalars=2, mib=40, products=3, scratch=scratch,
    )
    img_other, got1 = lax.optimization_barrier((img_other, got1))
    got2, got3 = swap(m2, z_mask(2), y_mask(2)), swap(m3, z_mask(3), y_mask(3))
    img, *messages = call(
        functools.partial(image_first_kernel, rows, feats), "image_first",
        [f32(rows + 8, feats)] + [bf16(rows + 8, feats)] * 3, img_own, swap(img_other, CORE),
    )
    img_got = [swap(m, x_mask(k)) for k, m in zip((1, 2, 3), messages)]
    (text,) = call(text_near_kernel, "text_near", [f32(quarter, feats)], after(text, *messages), got1)
    img, sums = call(
        functools.partial(image_last_kernel, feats), "image_last", [f32(rows, feats), f32(8, feats)],
        logit_scaler, img, *img_got, scalars=1,
    )
    text, *messages = call(
        functools.partial(text_first_kernel, rows, feats), "text_first",
        [f32(rows + 8, feats)] + [bf16(rows + 8, feats)] * 3, text, got2, got3, sums,
        scratch=[pltpu.VMEM((quarter, feats), F32)],
    )
    got = [swap(m, y_mask(i), z_mask(i)) for i, m in zip((1, 2, 3), messages)]
    back = swap(img[:, half:], z_mask(1))
    mine, other, sums = call(
        functools.partial(close_kernel, rows, width), "close", [f32(width, height), f32(width, height), f32(8, 128)],
        info, logit_scaler, text, *got, img, back, scalars=2,
    )
    sums = after(sums, other)
    other = swap(other, CORE)
    text_grad, image_grad = call(
        functools.partial(join_kernel, rows), "join", [f32(width, height)] * 2, info, mine, other, scalars=1
    )
    s1, s2, s3 = (after(swap(sums, z_mask(k), y_mask(k)), text_grad, image_grad) for k in (1, 2, 3))
    sums = (sums + s1) + (s2 + s3)
    return (image_grad.T, text_grad.T, sums[0, :2])


def solution(mesh):
    placed = (P("batch", "dim"), P("batch", "dim"), P(), P())
    return jax.shard_map(
        body,
        mesh=mesh,
        in_specs=placed,
        out_specs=(P("batch", "dim"), P("batch", "dim"), P()),
        check_vma=False,
    )
```

```python
import functools

import jax
import jax.numpy as jnp
from jax import lax
from jax.experimental import pallas as pl
from jax.experimental.pallas import tpu as pltpu
from jax.sharding import PartitionSpec as P

BF = jnp.bfloat16
F32 = jnp.float32
AXES = ("batch", "dim")
CORE = 1


def x_mask(k):
    return k << 2


def y_mask(k):
    return k << 4


def z_mask(k):
    return ((k >> 1) << 6) | ((k & 1) << 1)


def swap(array, mask0, mask1=None):
    mask1 = mask0 if mask1 is None else mask1
    n = lax.axis_size("batch") * lax.axis_size("dim")
    return lax.ppermute(array, AXES, [(i, i ^ (mask1 if i & 1 else mask0)) for i in range(n)])


LOW = 2.0**-3.5


def encode(v, m):
    a = jnp.abs(v) * (127.0 * LOW / m) + LOW
    for _ in range(5):
        a = a * a
    return jnp.where(v < 0, -a, a)


def decode(code, m):
    c = code.astype(F32)
    a = jnp.exp(jnp.log(jnp.abs(c)) * (1.0 / 32.0)) * (1.0 / LOW) - 1.0
    v = a * (m * (1.0 / 127.0))
    return jnp.where(c < 0, -v, v)


def top_of(largest):
    return (largest * 1.01 + 1e-30).astype(BF).astype(F32)


def pairs(core_ref, rows, half, ta_ref, tb_ref, t_rel):
    on0, step = core_ref[0] == 0, 2 * rows
    for b in range(4):
        other = (ta_ref, tb_ref)[b >> 1]
        p0 = jnp.where(on0, ta_ref[b].astype(F32), other[2 * (b & 1)].astype(F32))
        p1 = jnp.where(on0, tb_ref[b].astype(F32), other[2 * (b & 1) + 1].astype(F32))
        top = jnp.concatenate([p0[:, :half], p1[:, :half]], axis=1)
        bottom = jnp.concatenate([p0[:, half:], p1[:, half:]], axis=1)
        t_rel[b * step : (b + 1) * step, :] = jnp.concatenate([top, bottom], axis=0).astype(BF)


def coefficients(near, rows, info_ref, scale_ref, t_rel, images, coeff_low):
    scaling, offset = scale_ref[0], scale_ref[1]
    step, columns = 2 * rows, images.shape[0]
    similar = lax.dot_general(t_rel[...], images[...], (((1,), (1,)), ((), ())), preferred_element_type=F32)
    temp, bias = jnp.zeros((1, columns), F32), jnp.zeros((1, columns), F32)
    for b in range(4):
        part = similar[b * step : (b + 1) * step]
        logits = scaling * part + offset
        if near and b == 0:
            row = lax.broadcasted_iota(jnp.int32, part.shape, 0)
            column = lax.broadcasted_iota(jnp.int32, part.shape, 1)
            matched = (row - rows * info_ref[1] == column) & (column < rows)
            sig = 1.0 / (1.0 + jnp.exp(jnp.where(matched, logits, -logits)))
            coeff = jnp.where(matched, -sig, sig)
        else:
            coeff = 1.0 / (1.0 + jnp.exp(-logits))
        coeff_low[b * step : (b + 1) * step, :] = coeff.astype(BF)
        temp = temp + jnp.sum(coeff * part, axis=0, keepdims=True)
        bias = bias + jnp.sum(coeff, axis=0, keepdims=True)
    even = lax.broadcasted_iota(jnp.int32, (8, 128), 1) % 2 == 0
    return jnp.where(even, jnp.sum(temp, axis=1, keepdims=True), jnp.sum(bias, axis=1, keepdims=True))


def text_parts(core_ref, rows, half, coeff_low, images, grads):
    on0, step = core_ref[0] == 0, 2 * rows
    part = jnp.dot(coeff_low[...], images[...], preferred_element_type=F32)
    for b in range(4):
        top, bottom = part[b * step : b * step + rows], part[b * step + rows : (b + 1) * step]
        for e, at in ((0, slice(0, half)), (1, slice(half, 2 * half))):
            place = jnp.where(on0, e, b >> 1), jnp.where(on0, b, 2 * (b & 1) + e)
            grads[place] = jnp.concatenate([top[:, at], bottom[:, at]], axis=1)


def image_parts(coeff_low, t_rel):
    return lax.dot_general(coeff_low[...], t_rel[...], (((0,), (0,)), ((), ())), preferred_element_type=F32)


def split_kernel(rows, info_ref, texts_ref, images_ref, keep_ref, send_ref):
    on0, step = info_ref[0] == 0, 2 * rows
    for at, ref in ((0, texts_ref), (step, images_ref)):
        whole = ref[...].astype(F32).T
        first, second = whole[:step], whole[step:]
        keep_ref[at : at + step, :] = jnp.where(on0, first, second).astype(BF)
        send_ref[at : at + step, :] = jnp.where(on0, second, first).astype(BF)


def join_kernel(rows, info_ref, own_ref, got_ref, sums_ref, s1_ref, s2_ref, s3_ref, texts_ref, images_ref, scalars_ref):
    on0, step = info_ref[0] == 0, 2 * rows
    sums = (sums_ref[0:1, :] + s1_ref[0:1, :]) + (s2_ref[0:1, :] + s3_ref[0:1, :])
    scalars_ref[0] = jnp.sum(sums[:, 0:1])
    scalars_ref[1] = jnp.sum(sums[:, 1:2])
    for at, ref in ((0, texts_ref), (step, images_ref)):
        own, got = own_ref[at : at + step, :], got_ref[at : at + step, :]
        ref[...] = jnp.concatenate([jnp.where(on0, own, got), jnp.where(on0, got, own)], axis=0).T


def near_kernel(
    rows, half, feats, info_ref, scale_ref, ta_ref, tb_ref, im0_ref, im1_ref,
    own_ref, m_ref, t_rel, coeff_low, sums_ref, images, grads,
):
    quarter = 4 * rows
    images[0:quarter, :] = im0_ref[...]
    images[quarter : 2 * quarter, :] = im1_ref[...]
    pairs(info_ref, rows, half, ta_ref, tb_ref, t_rel)
    sums_ref[...] = coefficients(True, rows, info_ref, scale_ref, t_rel, images, coeff_low)
    text_parts(info_ref, rows, half, coeff_low, images, grads)
    own_ref[...] = jnp.concatenate([grads[0, i] for i in range(4)], axis=0)
    m_ref[...] = message([grads[1, i] for i in range(4)], feats)


def near_image_kernel(t_rel, coeff_low, acc_ref):
    acc_ref[...] = image_parts(coeff_low, t_rel)


def far_kernel(
    rows, half, feats, info_ref, scale_ref, ta_ref, tb_ref, im0_ref, im1_ref, before_ref, sums_before,
    ma_ref, mb_ref, own_ref, other_ref, images, t_rel, coeff_low, grads,
):
    quarter = 4 * rows
    images[0:quarter, :] = im0_ref[...]
    images[quarter : 2 * quarter, :] = im1_ref[...]
    pairs(info_ref, rows, half, ta_ref, tb_ref, t_rel)
    sums = coefficients(False, rows, info_ref, scale_ref, t_rel, images, coeff_low) + sums_before[...]
    text_parts(info_ref, rows, half, coeff_low, images, grads)
    for k, m_ref in ((0, ma_ref), (1, mb_ref)):
        m_ref[...] = message([grads[k, i] for i in range(4)], feats)
    acc = image_parts(coeff_low, t_rel) + before_ref[...]
    wide = jnp.concatenate([sums] * (feats // 128), axis=1)
    own_ref[...] = jnp.concatenate([acc[0:quarter], wide], axis=0)
    other_ref[...] = jnp.concatenate([acc[quarter : 2 * quarter], wide], axis=0)


def message(blocks, feats, extra=()):
    part = jnp.concatenate(blocks, axis=0)
    m = top_of(jnp.max(jnp.max(jnp.abs(part), axis=0, keepdims=True), axis=1, keepdims=True))
    tail = jnp.broadcast_to(m, (8 - len(extra), feats))
    return jnp.concatenate([encode(part, m), *extra, tail], axis=0).astype(BF)


def decoded(ref):
    whole = ref[...].astype(F32)
    n = whole.shape[0] - 8
    return decode(whole[:n], whole[n + 7 : n + 8]), whole[n:]


def split3(v):
    hi = v.astype(BF).astype(F32)
    mid = (v - hi).astype(BF).astype(F32)
    return [hi, mid, v - hi - mid]


def image_first_kernel(rows, feats, own_ref, other_ref, out_ref, *messages):
    total = own_ref[...] + other_ref[...]
    sums = total[4 * rows :]
    out_ref[...] = jnp.concatenate([total[0:rows], sums], axis=0)
    for i, m_ref in enumerate(messages):
        m_ref[...] = message([total[(i + 1) * rows : (i + 2) * rows]], feats, split3(sums[0:1]))


def with_scalars(own_ref, refs):
    n = own_ref.shape[0] - 8
    total, tails = own_ref[0:n, :], []
    for r in refs:
        value, tail = decoded(r)
        total = total + value
        tails.append(tail[0:1] + (tail[1:2] + tail[2:3]))
    return total, (own_ref[n : n + 1, :] + tails[0]) + (tails[1] + tails[2])


def image_last_kernel(feats, scale_ref, own_ref, r1_ref, r2_ref, r3_ref, out_ref, sums_ref):
    total, sums = with_scalars(own_ref, (r1_ref, r2_ref, r3_ref))
    out_ref[...] = total * scale_ref[0]
    sums_ref[...] = jnp.broadcast_to(sums, (8, feats))


def text_near_kernel(own_ref, r1_ref, out_ref):
    out_ref[...] = own_ref[...] + decoded(r1_ref)[0]


def text_first_kernel(rows, feats, own_ref, r2_ref, r3_ref, sums_ref, out_ref, m1_ref, m2_ref, m3_ref, total):
    tops = [r[4 * rows :, :].astype(F32)[7:8] for r in (r2_ref, r3_ref)]

    def add(step, carry):
        at = pl.ds(pl.multiple_of(step * 32, 32), 32)
        total[at, :] = own_ref[at, :] + decode(r2_ref[at, :], tops[0]) + decode(r3_ref[at, :], tops[1])
        return carry

    lax.fori_loop(0, 4 * rows // 32, add, 0)
    out_ref[...] = jnp.concatenate([total[0:rows, :], sums_ref[...]], axis=0)
    for i, m_ref in enumerate((m1_ref, m2_ref, m3_ref)):
        m_ref[...] = message([total[(i + 1) * rows : (i + 2) * rows, :]], feats, split3(sums_ref[0:1, :]))


def text_last_kernel(scale_ref, own_ref, r1_ref, r2_ref, r3_ref, out_ref, sums_ref):
    total, sums = with_scalars(own_ref, (r1_ref, r2_ref, r3_ref))
    out_ref[...] = total * scale_ref[0]
    sums_ref[...] = jnp.broadcast_to(sums[:, :128], (8, 128))


VMEM = pl.BlockSpec(memory_space=pltpu.VMEM)
SMEM = pl.BlockSpec(memory_space=pltpu.SMEM)


def grant(mib):
    return pltpu.CompilerParams(vmem_limit_bytes=mib * 1024 * 1024)


def after(array, *others):
    return lax.optimization_barrier((array, *others))[0]


def body(picture_embeds, caption_embeds, logit_scaler, logit_offset_term):
    height, width = picture_embeds.shape
    rows, half, feats = height // 4, 2 * width, 4 * width
    step, quarter = 2 * rows, 4 * rows
    index = lax.axis_index("batch") * lax.axis_size("dim") + lax.axis_index("dim")
    core, z_lo = index & 1, (index >> 1) & 1
    on0, lo0 = core == 0, z_lo == 0
    scaling = logit_scaler[0]

    def by(first_one, own, other):
        return [jnp.where(first_one, own, other), jnp.where(first_one, other, own)]

    def f32(*shape):
        return jax.ShapeDtypeStruct(shape, F32)

    def bf16(*shape):
        return jax.ShapeDtypeStruct(shape, BF)

    def call(kernel, name, out_shape, *args, scalars=0, scratch=(), mib=20, products=0, out_specs=None):
        return pl.pallas_call(
            kernel,
            out_shape=out_shape,
            in_specs=[SMEM] * scalars + [VMEM] * (len(args) - scalars),
            out_specs=out_specs or [VMEM] * len(out_shape),
            scratch_shapes=scratch,
            compiler_params=grant(mib),
            cost_estimate=pl.CostEstimate(
                flops=products * 2 * quarter * 2 * quarter * 2 * feats,
                bytes_accessed=sum(a.size * a.dtype.itemsize for a in (*args, *out_shape)),
                transcendentals=products * 4 * quarter * quarter,
            ),
            name=name,
        )(*args)

    info = jnp.stack([core, z_lo]).astype(jnp.int32)
    keep, send = call(
        functools.partial(split_kernel, rows), "split", [bf16(height, width)] * 2, info, caption_embeds.T, picture_embeds.T, scalars=1
    )
    chip = jnp.concatenate(by(on0, keep, swap(send, CORE)), axis=1)
    packed = jnp.concatenate([chip[:rows], chip[rows:step]], axis=1)
    keep, send = by(lo0, chip[step : step + rows], chip[step + rows :])
    first = [packed] + [swap(packed, y_mask(i), z_mask(i)) for i in range(1, 4)]
    image = jnp.concatenate([keep, swap(send, z_mask(1))], axis=1)
    stack = jnp.stack(first)
    second1, second3 = (swap(stack, z_mask(j), y_mask(j)) for j in (1, 3))
    images_own = jnp.concatenate([image] + [swap(image, x_mask(k)) for k in range(1, 4)], axis=0)
    images_other = swap(images_own, CORE)
    second2 = swap(after(stack, images_own), z_mask(2), y_mask(2))
    second1, second3 = lax.optimization_barrier((second1, second3))

    sizes = (rows, half, feats)
    scales = jnp.stack([scaling, logit_offset_term[0]])
    images_shape, coeff_shape = (2 * quarter, feats), (2 * quarter, 2 * quarter)
    grads = pltpu.VMEM((2, 4, rows, feats), F32)
    scratch = [pltpu.VMEM(images_shape, BF), pltpu.VMEM(images_shape, BF), pltpu.VMEM(coeff_shape, BF), grads]
    text, m1, t_near, c_near, sums = call(
        functools.partial(near_kernel, *sizes), "tile_near",
        [f32(quarter, feats), bf16(quarter + 8, feats), bf16(*images_shape), bf16(*coeff_shape), f32(8, 128)],
        info, scales, stack, second1, images_own, images_other,
        scalars=2, mib=36, products=2, scratch=[scratch[0], grads],
    )
    got1 = swap(m1, z_mask(1), y_mask(1))
    (acc,) = call(near_image_kernel, "image_near", [f32(*images_shape)], t_near, c_near, mib=30, products=1)
    second2 = after(second2, acc)
    m2, m3, img_own, img_other = call(
        functools.partial(far_kernel, *sizes), "tile_far",
        [bf16(quarter + 8, feats), bf16(quarter + 8, feats), f32(quarter + 8, feats), f32(quarter + 8, feats)],
        info, scales, second2, second3, images_own, images_other, acc, sums,
        scalars=2, mib=40, products=3, scratch=scratch,
    )
    img_other, got1 = lax.optimization_barrier((img_other, got1))
    got2, got3 = swap(m2, z_mask(2), y_mask(2)), swap(m3, z_mask(3), y_mask(3))
    img, *messages = call(
        functools.partial(image_first_kernel, rows, feats), "image_first",
        [f32(rows + 8, feats)] + [bf16(rows + 8, feats)] * 3, img_own, swap(img_other, CORE),
    )
    img_got = [swap(m, x_mask(k)) for k, m in zip((1, 2, 3), messages)]
    (text,) = call(text_near_kernel, "text_near", [f32(quarter, feats)], after(text, *messages), got1)
    img, sums = call(
        functools.partial(image_last_kernel, feats), "image_last", [f32(rows, feats), f32(8, feats)],
        logit_scaler, img, *img_got, scalars=1,
    )
    text, *messages = call(
        functools.partial(text_first_kernel, rows, feats), "text_first",
        [f32(rows + 8, feats)] + [bf16(rows + 8, feats)] * 3, text, got2, got3, sums,
        scratch=[pltpu.VMEM((quarter, feats), F32)],
    )
    got = [swap(m, y_mask(i), z_mask(i)) for i, m in zip((1, 2, 3), messages)]
    text, sums = call(
        text_last_kernel, "text_last", [f32(rows, feats), f32(8, 128)], logit_scaler, text, *got, scalars=1, products=2
    )
    image = jnp.concatenate(by(lo0, img[:, :half], after(swap(img[:, half:], z_mask(1)), text)), axis=0)
    whole = jnp.concatenate([text[:, :half], text[:, half:], image], axis=0)
    mine, other = by(on0, whole[:, :width], whole[:, width:])
    sums = after(sums, other)
    other = swap(other, CORE)
    lasts = [swap(sums, z_mask(k), y_mask(k)) for k in (1, 2, 3)]
    text_grad, image_grad, scalar_grads = call(
        functools.partial(join_kernel, rows), "join", [f32(width, height), f32(width, height), f32(2)],
        info, mine, other, sums, *lasts, scalars=1, out_specs=[VMEM, VMEM, SMEM],
    )
    return (image_grad.T, text_grad.T, scalar_grads)


def solution(mesh):
    placed = (P("batch", "dim"), P("batch", "dim"), P(), P())
    return jax.shard_map(
        body,
        mesh=mesh,
        in_specs=placed,
        out_specs=(P("batch", "dim"), P("batch", "dim"), P()),
        check_vma=False,
    )
```

```python
import functools

import jax
import jax.numpy as jnp
from jax import lax
from jax.experimental import pallas as pl
from jax.experimental.pallas import tpu as pltpu
from jax.sharding import PartitionSpec as P

BF = jnp.bfloat16
F32 = jnp.float32
AXES = ("batch", "dim")
CORE = 1


def x_mask(k):
    return k << 2


def y_mask(k):
    return k << 4


def z_mask(k):
    return ((k >> 1) << 6) | ((k & 1) << 1)


def swap(array, mask0, mask1=None):
    mask1 = mask0 if mask1 is None else mask1
    n = lax.axis_size("batch") * lax.axis_size("dim")
    return lax.ppermute(array, AXES, [(i, i ^ (mask1 if i & 1 else mask0)) for i in range(n)])


LOW = 2.0**-3.5


def encode(v, m):
    a = jnp.abs(v) * (127.0 * LOW / m) + LOW
    for _ in range(5):
        a = a * a
    return jnp.where(v < 0, -a, a)


def decode(code, m):
    c = code.astype(F32)
    a = jnp.exp(jnp.log(jnp.abs(c)) * (1.0 / 32.0)) * (1.0 / LOW) - 1.0
    v = a * (m * (1.0 / 127.0))
    return jnp.where(c < 0, -v, v)


def top_of(largest):
    return (largest * 1.01 + 1e-30).astype(BF).astype(F32)


def pairs(core_ref, rows, half, texts, t_rel):
    on0, step = core_ref[0] == 0, 2 * rows
    for b in range(4):
        p0, p1 = (
            jnp.where(on0, texts[2 * (b >> 1) + e][b & 1].astype(F32), texts[b][e].astype(F32)) for e in range(2)
        )
        top = jnp.concatenate([p0[:, :half], p1[:, :half]], axis=1)
        bottom = jnp.concatenate([p0[:, half:], p1[:, half:]], axis=1)
        t_rel[b * step : (b + 1) * step, :] = jnp.concatenate([top, bottom], axis=0).astype(BF)


def coefficients(near, rows, info_ref, scale_ref, t_rel, images, coeff_low):
    scaling, offset = scale_ref[0], scale_ref[1]
    step, columns = 2 * rows, images.shape[0]
    similar = lax.dot_general(t_rel[...], images[...], (((1,), (1,)), ((), ())), preferred_element_type=F32)
    temp, bias = jnp.zeros((1, columns), F32), jnp.zeros((1, columns), F32)
    for b in range(4):
        part = similar[b * step : (b + 1) * step]
        logits = scaling * part + offset
        if near and b == 0:
            row = lax.broadcasted_iota(jnp.int32, part.shape, 0)
            column = lax.broadcasted_iota(jnp.int32, part.shape, 1)
            matched = (row - rows * info_ref[1] == column) & (column < rows)
            sig = 1.0 / (1.0 + jnp.exp(jnp.where(matched, logits, -logits)))
            coeff = jnp.where(matched, -sig, sig)
        else:
            coeff = 1.0 / (1.0 + jnp.exp(-logits))
        coeff_low[b * step : (b + 1) * step, :] = coeff.astype(BF)
        temp = temp + jnp.sum(coeff * part, axis=0, keepdims=True)
        bias = bias + jnp.sum(coeff, axis=0, keepdims=True)
    even = lax.broadcasted_iota(jnp.int32, (8, 128), 1) % 2 == 0
    return jnp.where(even, jnp.sum(temp, axis=1, keepdims=True), jnp.sum(bias, axis=1, keepdims=True))


def text_parts(core_ref, rows, half, coeff_low, images, grads):
    on0, step = core_ref[0] == 0, 2 * rows
    part = jnp.dot(coeff_low[...], images[...], preferred_element_type=F32)
    for b in range(4):
        top, bottom = part[b * step : b * step + rows], part[b * step + rows : (b + 1) * step]
        for e, at in ((0, slice(0, half)), (1, slice(half, 2 * half))):
            place = jnp.where(on0, 2 * (b >> 1) + e, b), jnp.where(on0, b & 1, e)
            grads[place] = jnp.concatenate([top[:, at], bottom[:, at]], axis=1)


def image_parts(coeff_low, t_rel):
    return lax.dot_general(coeff_low[...], t_rel[...], (((0,), (0,)), ((), ())), preferred_element_type=F32)


def split_kernel(rows, info_ref, texts_ref, images_ref, keep_ref, send_ref):
    on0, step = info_ref[0] == 0, 2 * rows
    for at, ref in ((0, texts_ref), (step, images_ref)):
        whole = ref[...].astype(F32).T
        first, second = whole[:step], whole[step:]
        keep_ref[at : at + step, :] = jnp.where(on0, first, second).astype(BF)
        send_ref[at : at + step, :] = jnp.where(on0, second, first).astype(BF)


def join_kernel(rows, info_ref, own_ref, got_ref, texts_ref, images_ref):
    on0, step = info_ref[0] == 0, 2 * rows
    for at, ref in ((0, texts_ref), (step, images_ref)):
        own, got = own_ref[at : at + step, :], got_ref[at : at + step, :]
        ref[...] = jnp.concatenate([jnp.where(on0, own, got), jnp.where(on0, got, own)], axis=0).T


def tile_kernel(last, rows, half, feats, info_ref, scale_ref, *refs):
    texts, (im0_ref, im1_ref), refs = refs[:4], refs[4:6], refs[6:]
    if last:
        acc_ref, sums_before, own_ref, *refs = refs
        messages, (mine_ref, *others), (images, t_rel, coeff_low, grads) = refs[:3], refs[3:8], refs[8:]
    else:
        own_ref, *refs = refs
        messages, (t_rel, coeff_low, sums_ref), (images, grads) = refs[:3], refs[3:6], refs[6:]
    quarter = 4 * rows
    images[0:quarter, :] = im0_ref[...]
    images[quarter : 2 * quarter, :] = im1_ref[...]
    pairs(info_ref, rows, half, texts, t_rel)
    sums = coefficients(last, rows, info_ref, scale_ref, t_rel, images, coeff_low)
    text_parts(info_ref, rows, half, coeff_low, images, grads)
    own_ref[...] = jnp.concatenate([grads[0, i] for i in range(2)], axis=0)
    for k, m_ref in enumerate(messages):
        m_ref[...] = message([grads[k + 1, i] for i in range(2)], feats)
    if last:
        acc = image_parts(coeff_low, t_rel) + acc_ref[...]
        wide = jnp.concatenate([sums + sums_before[...]] * (feats // 128), axis=1)
        mine_ref[...] = jnp.concatenate([acc[0:quarter], wide], axis=0)
        for k, ref in enumerate(others):
            value = acc[quarter + k * rows : quarter + (k + 1) * rows]
            ref[...] = jnp.concatenate([value, wide], axis=0) if k == 0 else value
    else:
        sums_ref[...] = sums


def image_kernel(t_rel, coeff_low, acc_ref):
    acc_ref[...] = image_parts(coeff_low, t_rel)


def message(blocks, feats, extra=()):
    part = jnp.concatenate(blocks, axis=0)
    m = top_of(jnp.max(jnp.max(jnp.abs(part), axis=0, keepdims=True), axis=1, keepdims=True))
    tail = jnp.broadcast_to(m, (8 - len(extra), feats))
    return jnp.concatenate([encode(part, m), *extra, tail], axis=0).astype(BF)


def decoded(ref):
    whole = ref[...].astype(F32)
    n = whole.shape[0] - 8
    return decode(whole[:n], whole[n + 7 : n + 8]), whole[n:]


def split3(v):
    hi = v.astype(BF).astype(F32)
    mid = (v - hi).astype(BF).astype(F32)
    return [hi, mid, v - hi - mid]


def image_first_kernel(rows, feats, own_ref, *refs):
    others, (out_ref, *messages) = refs[:4], refs[4:]
    sums = own_ref[4 * rows :, :] + others[0][rows:, :]
    out_ref[...] = jnp.concatenate([own_ref[0:rows, :] + others[0][0:rows, :], sums], axis=0)
    for i, m_ref in enumerate(messages):
        m_ref[...] = message([own_ref[(i + 1) * rows : (i + 2) * rows, :] + others[i + 1][...]], feats, split3(sums[0:1]))


def with_scalars(own_ref, refs):
    n = own_ref.shape[0] - 8
    total, tails = own_ref[0:n, :], []
    for r in refs:
        value, tail = decoded(r)
        total = total + value
        tails.append(tail[0:1] + (tail[1:2] + tail[2:3]))
    return total, (own_ref[n : n + 1, :] + tails[0]) + (tails[1] + tails[2])


def image_last_kernel(feats, scale_ref, own_ref, r1_ref, r2_ref, r3_ref, out_ref):
    total, sums = with_scalars(own_ref, (r1_ref, r2_ref, r3_ref))
    out_ref[...] = jnp.concatenate([total * scale_ref[0], jnp.broadcast_to(sums, (8, feats))], axis=0)


def text_first_kernel(rows, feats, owna_ref, ownb_ref, a1_ref, a2_ref, a3_ref, b1_ref, b2_ref, b3_ref, out_ref, m1_ref, m2_ref, m3_ref, total):
    step = 2 * rows
    for at, own_ref, refs in ((step, owna_ref, (a1_ref, a2_ref, a3_ref)), (0, ownb_ref, (b1_ref, b2_ref, b3_ref))):
        tops = [r[...].astype(F32)[step + 7 : step + 8] for r in refs]

        def add(k, carry):
            part = pl.ds(pl.multiple_of(k * 16, 16), 16)
            value = own_ref[part, :]
            for r, top in zip(refs, tops):
                value = value + decode(r[part, :], top)
            total[pl.ds(pl.multiple_of(at + k * 16, 16), 16), :] = value
            return carry

        lax.fori_loop(0, step // 16, add, 0, unroll=2)
    out_ref[...] = total[0:rows, :]
    for i, m_ref in enumerate((m1_ref, m2_ref, m3_ref)):
        m_ref[...] = message([total[(i + 1) * rows : (i + 2) * rows, :]], feats)


def text_last_kernel(scale_ref, own_ref, r1_ref, r2_ref, r3_ref, out_ref):
    total = own_ref[...]
    for r in (r1_ref, r2_ref, r3_ref):
        total = total + decoded(r)[0]
    out_ref[...] = total * scale_ref[0]


VMEM = pl.BlockSpec(memory_space=pltpu.VMEM)
SMEM = pl.BlockSpec(memory_space=pltpu.SMEM)


def grant(mib):
    return pltpu.CompilerParams(vmem_limit_bytes=mib * 1024 * 1024)


def after(array, *others):
    return lax.optimization_barrier((array, *others))[0]


def body(picture_embeds, caption_embeds, logit_scaler, logit_offset_term):
    height, width = picture_embeds.shape
    rows, half, feats = height // 4, 2 * width, 4 * width
    step, quarter = 2 * rows, 4 * rows
    index = lax.axis_index("batch") * lax.axis_size("dim") + lax.axis_index("dim")
    core, z_lo = index & 1, (index >> 1) & 1
    on0, lo0 = core == 0, z_lo == 0
    scaling = logit_scaler[0]

    def by(first_one, own, other):
        return [jnp.where(first_one, own, other), jnp.where(first_one, other, own)]

    def f32(*shape):
        return jax.ShapeDtypeStruct(shape, F32)

    def bf16(*shape):
        return jax.ShapeDtypeStruct(shape, BF)

    def call(kernel, name, out_shape, *args, scalars=0, scratch=(), mib=20, products=0):
        return pl.pallas_call(
            kernel,
            out_shape=out_shape,
            in_specs=[SMEM] * scalars + [VMEM] * (len(args) - scalars),
            out_specs=[VMEM] * len(out_shape),
            scratch_shapes=scratch,
            compiler_params=grant(mib),
            cost_estimate=pl.CostEstimate(
                flops=products * 2 * quarter * 2 * quarter * 2 * feats,
                bytes_accessed=sum(a.size * a.dtype.itemsize for a in (*args, *out_shape)),
                transcendentals=products * 4 * quarter * quarter,
            ),
            name=name,
        )(*args)

    info = jnp.stack([core, z_lo]).astype(jnp.int32)
    keep, send = call(
        functools.partial(split_kernel, rows), "split", [bf16(height, width)] * 2, info, caption_embeds.T, picture_embeds.T, scalars=1
    )
    chip = jnp.concatenate(by(on0, keep, swap(send, CORE)), axis=1)
    packed = jnp.concatenate([chip[:rows], chip[rows:step]], axis=1)
    keep, send = by(lo0, chip[step : step + rows], chip[step + rows :])
    first = [packed] + [swap(packed, y_mask(i), z_mask(i)) for i in range(1, 4)]
    image = jnp.concatenate([keep, swap(send, z_mask(1))], axis=1)
    pieces = [image] + [swap(image, x_mask(k)) for k in range(1, 4)]
    images_own = jnp.concatenate(pieces, axis=0)
    images_other = jnp.concatenate([swap(p, CORE) for p in pieces], axis=0)

    def fetch(stack):
        return [stack] + [swap(stack, z_mask(j), y_mask(j)) for j in range(1, 4)]

    texts_a, texts_b = fetch(jnp.stack(first[2:])), fetch(jnp.stack(first[:2]))
    sizes = (rows, half, feats)
    scales = jnp.stack([scaling, logit_offset_term[0]])
    images_shape, coeff_shape = (2 * quarter, feats), (2 * quarter, 2 * quarter)
    grads = pltpu.VMEM((4, 2, rows, feats), F32)
    images_scratch, coeff_scratch = pltpu.VMEM(images_shape, BF), pltpu.VMEM(coeff_shape, BF)
    parts_shape = [f32(step, feats)] + [bf16(step + 8, feats)] * 3

    def give(messages):
        return [swap(m, z_mask(j), y_mask(j)) for j, m in zip((1, 2, 3), messages)]

    own_a, *messages, t_rel, coeff_low, sums = call(
        functools.partial(tile_kernel, False, *sizes), "tile_first",
        parts_shape + [bf16(*images_shape), bf16(*coeff_shape), f32(8, 128)],
        info, scales, *texts_a, images_own, images_other, scalars=2, mib=36, products=2, scratch=[images_scratch, grads],
    )
    got_a = give(messages)
    (acc,) = call(image_kernel, "image_part", [f32(*images_shape)], t_rel, coeff_low, mib=30, products=1)
    texts_b[0] = after(texts_b[0], acc)
    parts = call(
        functools.partial(tile_kernel, True, *sizes), "tile_last",
        parts_shape + [f32(quarter + 8, feats), f32(rows + 8, feats)] + [f32(rows, feats)] * 3,
        info, scales, *texts_b, images_own, images_other, acc, sums,
        scalars=2, mib=36, products=3, scratch=[images_scratch, images_scratch, coeff_scratch, grads],
    )
    own_b, messages, img_own, img_others = parts[0], parts[1:4], parts[4], parts[5:]
    img_others, got_a = lax.optimization_barrier((img_others, got_a))
    got_b = give(messages)
    img, *messages = call(
        functools.partial(image_first_kernel, rows, feats), "image_first",
        [f32(rows + 8, feats)] + [bf16(rows + 8, feats)] * 3, img_own, *[swap(part, CORE) for part in img_others],
    )
    img_got = [swap(m, x_mask(k)) for k, m in zip((1, 2, 3), messages)]
    text, *messages = call(
        functools.partial(text_first_kernel, rows, feats), "text_first",
        [f32(rows, feats)] + [bf16(rows + 8, feats)] * 3, after(own_a, *messages), own_b, *got_a, *got_b,
        scratch=[pltpu.VMEM((quarter, feats), F32)],
    )
    got = [swap(m, y_mask(i), z_mask(i)) for i, m in zip((1, 2, 3), messages)]
    img_got[0] = after(img_got[0], text)
    (img,) = call(functools.partial(image_last_kernel, feats), "image_last", [f32(rows + 8, feats)], logit_scaler, img, *img_got, scalars=1)
    (text,) = call(text_last_kernel, "text_last", [f32(rows, feats)], logit_scaler, text, *got, scalars=1, products=2)
    keep, back = img[:, :half], after(swap(img[:, half:], z_mask(1)), text)
    image = jnp.concatenate(by(lo0, keep[:rows], back[:rows]), axis=0)
    sums = keep[rows:]
    sums = (sums + back[rows:]) + (swap(sums, z_mask(2)) + swap(sums, z_mask(3)))
    sums = sums[:, :128]
    whole = jnp.concatenate([text[:, :half], text[:, half:], image], axis=0)
    mine, other = by(on0, whole[:, :width], whole[:, width:])
    sums, other = lax.optimization_barrier((sums, other))
    other = swap(other, CORE)
    text_grad, image_grad = call(
        functools.partial(join_kernel, rows), "join", [f32(width, height)] * 2, info, mine, other, scalars=1
    )
    s1, s2, s3 = (after(swap(sums, y_mask(k)), text_grad, image_grad) for k in (1, 2, 3))
    sums = (sums + s1) + (s2 + s3)
    return (image_grad.T, text_grad.T, sums[0, :2])


def solution(mesh):
    placed = (P("batch", "dim"), P("batch", "dim"), P(), P())
    return jax.shard_map(
        body,
        mesh=mesh,
        in_specs=placed,
        out_specs=(P("batch", "dim"), P("batch", "dim"), P()),
        check_vma=False,
    )
```

```python
import functools

import jax
import jax.numpy as jnp
from jax import lax
from jax.experimental import pallas as pl
from jax.experimental.pallas import tpu as pltpu
from jax.sharding import PartitionSpec as P

BF = jnp.bfloat16
F32 = jnp.float32
AXES = ("batch", "dim")
CORE = 1


def x_mask(k):
    return k << 2


def y_mask(k):
    return k << 4


def z_mask(k):
    return ((k >> 1) << 6) | ((k & 1) << 1)


def swap(array, mask0, mask1=None):
    mask1 = mask0 if mask1 is None else mask1
    n = lax.axis_size("batch") * lax.axis_size("dim")
    return lax.ppermute(array, AXES, [(i, i ^ (mask1 if i & 1 else mask0)) for i in range(n)])


LOW = 2.0**-3.5


def encode(v, m):
    a = jnp.abs(v) * (127.0 * LOW / m) + LOW
    for _ in range(5):
        a = a * a
    return jnp.where(v < 0, -a, a)


def decode(code, m):
    c = code.astype(F32)
    a = jnp.exp(jnp.log(jnp.abs(c)) * (1.0 / 32.0)) * (1.0 / LOW) - 1.0
    v = a * (m * (1.0 / 127.0))
    return jnp.where(c < 0, -v, v)


def top_of(largest):
    return (largest * 1.01 + 1e-30).astype(BF).astype(F32)


def pairs(core_ref, rows, half, ta_ref, tb_ref, t_rel):
    on0, step = core_ref[0] == 0, 2 * rows
    for b in range(4):
        other = (ta_ref, tb_ref)[b >> 1]
        p0 = jnp.where(on0, ta_ref[b].astype(F32), other[2 * (b & 1)].astype(F32))
        p1 = jnp.where(on0, tb_ref[b].astype(F32), other[2 * (b & 1) + 1].astype(F32))
        top = jnp.concatenate([p0[:, :half], p1[:, :half]], axis=1)
        bottom = jnp.concatenate([p0[:, half:], p1[:, half:]], axis=1)
        t_rel[b * step : (b + 1) * step, :] = jnp.concatenate([top, bottom], axis=0).astype(BF)


def coefficients(near, rows, info_ref, scale_ref, t_rel, images, coeff_low):
    scaling, offset = scale_ref[0], scale_ref[1]
    step, columns = 2 * rows, images.shape[0]
    similar = lax.dot_general(t_rel[...], images[...], (((1,), (1,)), ((), ())), preferred_element_type=F32)
    temp, bias = jnp.zeros((1, columns), F32), jnp.zeros((1, columns), F32)
    for b in range(4):
        part = similar[b * step : (b + 1) * step]
        logits = scaling * part + offset
        if near and b == 0:
            row = lax.broadcasted_iota(jnp.int32, part.shape, 0)
            column = lax.broadcasted_iota(jnp.int32, part.shape, 1)
            matched = (row - rows * info_ref[1] == column) & (column < rows)
            sig = 1.0 / (1.0 + jnp.exp(jnp.where(matched, logits, -logits)))
            coeff = jnp.where(matched, -sig, sig)
        else:
            coeff = 1.0 / (1.0 + jnp.exp(-logits))
        coeff_low[b * step : (b + 1) * step, :] = coeff.astype(BF)
        temp = temp + jnp.sum(coeff * part, axis=0, keepdims=True)
        bias = bias + jnp.sum(coeff, axis=0, keepdims=True)
    even = lax.broadcasted_iota(jnp.int32, (8, 128), 1) % 2 == 0
    return jnp.where(even, jnp.sum(temp, axis=1, keepdims=True), jnp.sum(bias, axis=1, keepdims=True))


def text_parts(core_ref, rows, half, coeff_low, images, grads):
    on0, step = core_ref[0] == 0, 2 * rows
    part = jnp.dot(coeff_low[...], images[...], preferred_element_type=F32)
    for b in range(4):
        top, bottom = part[b * step : b * step + rows], part[b * step + rows : (b + 1) * step]
        for e, at in ((0, slice(0, half)), (1, slice(half, 2 * half))):
            place = jnp.where(on0, e, b >> 1), jnp.where(on0, b, 2 * (b & 1) + e)
            grads[place] = jnp.concatenate([top[:, at], bottom[:, at]], axis=1)


def image_parts(coeff_low, t_rel):
    return lax.dot_general(coeff_low[...], t_rel[...], (((0,), (0,)), ((), ())), preferred_element_type=F32)


def split_kernel(rows, info_ref, texts_ref, images_ref, keep_ref, send_ref):
    on0, step = info_ref[0] == 0, 2 * rows
    for at, ref in ((0, texts_ref), (step, images_ref)):
        whole = ref[...].astype(F32).T
        first, second = whole[:step], whole[step:]
        keep_ref[at : at + step, :] = jnp.where(on0, first, second).astype(BF)
        send_ref[at : at + step, :] = jnp.where(on0, second, first).astype(BF)


def join_kernel(rows, info_ref, own_ref, got_ref, texts_ref, images_ref):
    on0, step = info_ref[0] == 0, 2 * rows
    for at, ref in ((0, texts_ref), (step, images_ref)):
        own, got = own_ref[:, at : at + step], got_ref[:, at : at + step]
        ref[...] = jnp.concatenate([jnp.where(on0, own, got), jnp.where(on0, got, own)], axis=1)


def near_kernel(
    rows, half, feats, info_ref, scale_ref, ta_ref, tb_ref, im0_ref, im1_ref,
    grads, m_ref, t_rel, coeff_low, sums_ref, images,
):
    quarter = 4 * rows
    images[0:quarter, :] = im0_ref[...]
    images[quarter : 2 * quarter, :] = im1_ref[...]
    pairs(info_ref, rows, half, ta_ref, tb_ref, t_rel)
    sums_ref[...] = coefficients(True, rows, info_ref, scale_ref, t_rel, images, coeff_low)
    text_parts(info_ref, rows, half, coeff_low, images, grads)
    m_ref[...] = message([grads[1, i] for i in range(4)], feats)


def near_image_kernel(t_rel, coeff_low, acc_ref):
    acc_ref[...] = image_parts(coeff_low, t_rel)


def far_kernel(
    rows, half, feats, info_ref, scale_ref, ta_ref, tb_ref, im0_ref, im1_ref, before_ref, sums_before,
    ma_ref, mb_ref, own_ref, other_ref, images, t_rel, coeff_low, grads,
):
    quarter = 4 * rows
    images[0:quarter, :] = im0_ref[...]
    images[quarter : 2 * quarter, :] = im1_ref[...]
    pairs(info_ref, rows, half, ta_ref, tb_ref, t_rel)
    sums = coefficients(False, rows, info_ref, scale_ref, t_rel, images, coeff_low) + sums_before[...]
    text_parts(info_ref, rows, half, coeff_low, images, grads)
    for k, m_ref in ((0, ma_ref), (1, mb_ref)):
        m_ref[...] = message([grads[k, i] for i in range(4)], feats)
    acc = image_parts(coeff_low, t_rel) + before_ref[...]
    wide = jnp.concatenate([sums] * (feats // 128), axis=1)
    own_ref[...] = jnp.concatenate([acc[0:quarter], wide], axis=0)
    other_ref[...] = jnp.concatenate([acc[quarter : 2 * quarter], wide], axis=0)


def message(blocks, feats, extra=()):
    part = jnp.concatenate(blocks, axis=0)
    m = top_of(jnp.max(jnp.max(jnp.abs(part), axis=0, keepdims=True), axis=1, keepdims=True))
    tail = jnp.broadcast_to(m, (8 - len(extra), feats))
    return jnp.concatenate([encode(part, m), *extra, tail], axis=0).astype(BF)


def decoded(ref):
    whole = ref[...].astype(F32)
    n = whole.shape[0] - 8
    return decode(whole[:n], whole[n + 7 : n + 8]), whole[n:]


def split3(v):
    hi = v.astype(BF).astype(F32)
    mid = (v - hi).astype(BF).astype(F32)
    return [hi, mid, v - hi - mid]


def image_first_kernel(rows, feats, own_ref, other_ref, out_ref, *messages):
    total = own_ref[...] + other_ref[...]
    sums = total[4 * rows :]
    out_ref[...] = jnp.concatenate([total[0:rows], sums], axis=0)
    for i, m_ref in enumerate(messages):
        m_ref[...] = message([total[(i + 1) * rows : (i + 2) * rows]], feats, split3(sums[0:1]))


def with_scalars(own_ref, refs):
    n = own_ref.shape[0] - 8
    total, tails = own_ref[0:n, :], []
    for r in refs:
        value, tail = decoded(r)
        total = total + value
        tails.append(tail[0:1] + (tail[1:2] + tail[2:3]))
    return total, (own_ref[n : n + 1, :] + tails[0]) + (tails[1] + tails[2])


def image_last_kernel(feats, scale_ref, own_ref, r1_ref, r2_ref, r3_ref, out_ref, sums_ref):
    total, sums = with_scalars(own_ref, (r1_ref, r2_ref, r3_ref))
    out_ref[...] = total * scale_ref[0]
    sums_ref[...] = jnp.broadcast_to(sums, (8, feats))


def text_near_kernel(grads_ref, r1_ref, out_ref):
    out_ref[...] = jnp.concatenate([grads_ref[0, i] for i in range(4)], axis=0) + decoded(r1_ref)[0]


def text_first_kernel(rows, feats, own_ref, r2_ref, r3_ref, sums_ref, out_ref, m1_ref, m2_ref, m3_ref, total):
    tops = [r[4 * rows :, :].astype(F32)[7:8] for r in (r2_ref, r3_ref)]

    def add(step, carry):
        at = pl.ds(pl.multiple_of(step * 32, 32), 32)
        total[at, :] = own_ref[at, :] + decode(r2_ref[at, :], tops[0]) + decode(r3_ref[at, :], tops[1])
        return carry

    lax.fori_loop(0, 4 * rows // 32, add, 0)
    out_ref[...] = jnp.concatenate([total[0:rows, :], sums_ref[...]], axis=0)
    for i, m_ref in enumerate((m1_ref, m2_ref, m3_ref)):
        m_ref[...] = message([total[(i + 1) * rows : (i + 2) * rows, :]], feats, split3(sums_ref[0:1, :]))


def text_last_kernel(scale_ref, own_ref, r1_ref, r2_ref, r3_ref, out_ref, sums_ref):
    total, sums = with_scalars(own_ref, (r1_ref, r2_ref, r3_ref))
    out_ref[...] = total * scale_ref[0]
    sums_ref[...] = jnp.broadcast_to(sums[:, :128], (8, 128))


VMEM = pl.BlockSpec(memory_space=pltpu.VMEM)
SMEM = pl.BlockSpec(memory_space=pltpu.SMEM)


def grant(mib):
    return pltpu.CompilerParams(vmem_limit_bytes=mib * 1024 * 1024)


def after(array, *others):
    return lax.optimization_barrier((array, *others))[0]


def body(picture_embeds, caption_embeds, logit_scaler, logit_offset_term):
    height, width = picture_embeds.shape
    rows, half, feats = height // 4, 2 * width, 4 * width
    step, quarter = 2 * rows, 4 * rows
    index = lax.axis_index("batch") * lax.axis_size("dim") + lax.axis_index("dim")
    core, z_lo = index & 1, (index >> 1) & 1
    on0, lo0 = core == 0, z_lo == 0
    scaling = logit_scaler[0]

    def by(first_one, own, other):
        return [jnp.where(first_one, own, other), jnp.where(first_one, other, own)]

    def f32(*shape):
        return jax.ShapeDtypeStruct(shape, F32)

    def bf16(*shape):
        return jax.ShapeDtypeStruct(shape, BF)

    def call(kernel, name, out_shape, *args, scalars=0, scratch=(), mib=20, products=0):
        return pl.pallas_call(
            kernel,
            out_shape=out_shape,
            in_specs=[SMEM] * scalars + [VMEM] * (len(args) - scalars),
            out_specs=[VMEM] * len(out_shape),
            scratch_shapes=scratch,
            compiler_params=grant(mib),
            cost_estimate=pl.CostEstimate(
                flops=products * 2 * quarter * 2 * quarter * 2 * feats,
                bytes_accessed=sum(a.size * a.dtype.itemsize for a in (*args, *out_shape)),
                transcendentals=products * 4 * quarter * quarter,
            ),
            name=name,
        )(*args)

    info = jnp.stack([core, z_lo]).astype(jnp.int32)
    keep, send = call(
        functools.partial(split_kernel, rows), "split", [bf16(height, width)] * 2, info, caption_embeds.T, picture_embeds.T, scalars=1
    )
    chip = jnp.concatenate(by(on0, keep, swap(send, CORE)), axis=1)
    packed = jnp.concatenate([chip[:rows], chip[rows:step]], axis=1)
    keep, send = by(lo0, chip[step : step + rows], chip[step + rows :])
    first = [packed] + [swap(packed, y_mask(i), z_mask(i)) for i in range(1, 4)]
    image = jnp.concatenate([keep, swap(send, z_mask(1))], axis=1)
    stack = jnp.stack(first)
    second1, second3 = (swap(stack, z_mask(j), y_mask(j)) for j in (1, 3))
    images_own = jnp.concatenate([image] + [swap(image, x_mask(k)) for k in range(1, 4)], axis=0)
    images_other = swap(images_own, CORE)
    second2 = swap(after(stack, images_own), z_mask(2), y_mask(2))
    second1, second3 = lax.optimization_barrier((second1, second3))

    sizes = (rows, half, feats)
    scales = jnp.stack([scaling, logit_offset_term[0]])
    images_shape, coeff_shape = (2 * quarter, feats), (2 * quarter, 2 * quarter)
    grads = pltpu.VMEM((2, 4, rows, feats), F32)
    scratch = [pltpu.VMEM(images_shape, BF), pltpu.VMEM(images_shape, BF), pltpu.VMEM(coeff_shape, BF), grads]
    text, m1, t_near, c_near, sums = call(
        functools.partial(near_kernel, *sizes), "tile_near",
        [f32(2, 4, rows, feats), bf16(quarter + 8, feats), bf16(*images_shape), bf16(*coeff_shape), f32(8, 128)],
        info, scales, stack, second1, images_own, images_other,
        scalars=2, mib=36, products=2, scratch=[scratch[0]],
    )
    got1 = swap(m1, z_mask(1), y_mask(1))
    (acc,) = call(near_image_kernel, "image_near", [f32(*images_shape)], t_near, c_near, mib=30, products=1)
    second2 = after(second2, acc)
    m2, m3, img_own, img_other = call(
        functools.partial(far_kernel, *sizes), "tile_far",
        [bf16(quarter + 8, feats), bf16(quarter + 8, feats), f32(quarter + 8, feats), f32(quarter + 8, feats)],
        info, scales, second2, second3, images_own, images_other, acc, sums,
        scalars=2, mib=40, products=3, scratch=scratch,
    )
    img_other, got1 = lax.optimization_barrier((img_other, got1))
    got2, got3 = swap(m2, z_mask(2), y_mask(2)), swap(m3, z_mask(3), y_mask(3))
    img, *messages = call(
        functools.partial(image_first_kernel, rows, feats), "image_first",
        [f32(rows + 8, feats)] + [bf16(rows + 8, feats)] * 3, img_own, swap(img_other, CORE),
    )
    img_got = [swap(m, x_mask(k)) for k, m in zip((1, 2, 3), messages)]
    (text,) = call(text_near_kernel, "text_near", [f32(quarter, feats)], after(text, *messages), got1)
    img, sums = call(
        functools.partial(image_last_kernel, feats), "image_last", [f32(rows, feats), f32(8, feats)],
        logit_scaler, img, *img_got, scalars=1,
    )
    text, *messages = call(
        functools.partial(text_first_kernel, rows, feats), "text_first",
        [f32(rows + 8, feats)] + [bf16(rows + 8, feats)] * 3, text, got2, got3, sums,
        scratch=[pltpu.VMEM((quarter, feats), F32)],
    )
    got = [swap(m, y_mask(i), z_mask(i)) for i, m in zip((1, 2, 3), messages)]
    text, sums = call(
        text_last_kernel, "text_last", [f32(rows, feats), f32(8, 128)], logit_scaler, text, *got, scalars=1, products=2
    )
    image = jnp.concatenate(by(lo0, img[:, :half], after(swap(img[:, half:], z_mask(1)), text)), axis=0)
    whole = jnp.concatenate([text[:, :half], text[:, half:], image], axis=0)
    mine, other = by(on0, whole[:, :width], whole[:, width:])
    sums = after(sums, other)
    other = swap(other.T, CORE)
    text_grad, image_grad = call(
        functools.partial(join_kernel, rows), "join", [f32(width, height)] * 2, info, mine.T, other, scalars=1
    )
    s1, s2, s3 = (after(swap(sums, z_mask(k), y_mask(k)), text_grad, image_grad) for k in (1, 2, 3))
    sums = (sums + s1) + (s2 + s3)
    return (image_grad.T, text_grad.T, sums[0, :2])


def solution(mesh):
    placed = (P("batch", "dim"), P("batch", "dim"), P(), P())
    return jax.shard_map(
        body,
        mesh=mesh,
        in_specs=placed,
        out_specs=(P("batch", "dim"), P("batch", "dim"), P()),
        check_vma=False,
    )
```

```python
import functools

import jax
import jax.numpy as jnp
from jax import lax
from jax.experimental import pallas as pl
from jax.experimental.pallas import tpu as pltpu
from jax.sharding import PartitionSpec as P

BF = jnp.bfloat16
F32 = jnp.float32
AXES = ("batch", "dim")
CORE = 1


def x_mask(k):
    return k << 2


def y_mask(k):
    return k << 4


def z_mask(k):
    return ((k >> 1) << 6) | ((k & 1) << 1)


def swap(array, mask0, mask1=None):
    mask1 = mask0 if mask1 is None else mask1
    n = lax.axis_size("batch") * lax.axis_size("dim")
    return lax.ppermute(array, AXES, [(i, i ^ (mask1 if i & 1 else mask0)) for i in range(n)])


LOW = 2.0**-3.5


def encode(v, m):
    a = jnp.abs(v) * (127.0 * LOW / m) + LOW
    for _ in range(5):
        a = a * a
    return jnp.where(v < 0, -a, a)


def decode(code, m):
    c = code.astype(F32)
    a = jnp.exp(jnp.log(jnp.abs(c)) * (1.0 / 32.0)) * (1.0 / LOW) - 1.0
    v = a * (m * (1.0 / 127.0))
    return jnp.where(c < 0, -v, v)


def top_of(largest):
    return (largest * 1.01 + 1e-30).astype(BF).astype(F32)


def pairs(core_ref, rows, half, ta_ref, tb_ref, t_rel):
    on0, step = core_ref[0] == 0, 2 * rows
    for b in range(4):
        other = (ta_ref, tb_ref)[b >> 1]
        p0 = jnp.where(on0, ta_ref[b].astype(F32), other[2 * (b & 1)].astype(F32))
        p1 = jnp.where(on0, tb_ref[b].astype(F32), other[2 * (b & 1) + 1].astype(F32))
        top = jnp.concatenate([p0[:, :half], p1[:, :half]], axis=1)
        bottom = jnp.concatenate([p0[:, half:], p1[:, half:]], axis=1)
        t_rel[b * step : (b + 1) * step, :] = jnp.concatenate([top, bottom], axis=0).astype(BF)


def coefficients(near, rows, info_ref, scale_ref, t_rel, images, coeff_low):
    scaling, offset = scale_ref[0], scale_ref[1]
    step, columns = 2 * rows, images.shape[0]
    similar = lax.dot_general(t_rel[...], images[...], (((1,), (1,)), ((), ())), preferred_element_type=F32)
    temp, bias = jnp.zeros((1, columns), F32), jnp.zeros((1, columns), F32)
    for b in range(4):
        part = similar[b * step : (b + 1) * step]
        logits = scaling * part + offset
        if near and b == 0:
            row = lax.broadcasted_iota(jnp.int32, part.shape, 0)
            column = lax.broadcasted_iota(jnp.int32, part.shape, 1)
            matched = (row - rows * info_ref[1] == column) & (column < rows)
            sig = 1.0 / (1.0 + jnp.exp(jnp.where(matched, logits, -logits)))
            coeff = jnp.where(matched, -sig, sig)
        else:
            coeff = 1.0 / (1.0 + jnp.exp(-logits))
        coeff_low[b * step : (b + 1) * step, :] = coeff.astype(BF)
        temp = temp + jnp.sum(coeff * part, axis=0, keepdims=True)
        bias = bias + jnp.sum(coeff, axis=0, keepdims=True)
    even = lax.broadcasted_iota(jnp.int32, (8, 128), 1) % 2 == 0
    return jnp.where(even, jnp.sum(temp, axis=1, keepdims=True), jnp.sum(bias, axis=1, keepdims=True))


def text_parts(core_ref, rows, half, coeff_low, images, grads):
    on0, step = core_ref[0] == 0, 2 * rows
    part = jnp.dot(coeff_low[...], images[...], preferred_element_type=F32)
    for b in range(4):
        top, bottom = part[b * step : b * step + rows], part[b * step + rows : (b + 1) * step]
        for e, at in ((0, slice(0, half)), (1, slice(half, 2 * half))):
            place = jnp.where(on0, e, b >> 1), jnp.where(on0, b, 2 * (b & 1) + e)
            grads[place] = jnp.concatenate([top[:, at], bottom[:, at]], axis=1)


def image_parts(coeff_low, t_rel):
    return lax.dot_general(coeff_low[...], t_rel[...], (((0,), (0,)), ((), ())), preferred_element_type=F32)


def split_kernel(rows, info_ref, texts_ref, images_ref, keep_ref, send_ref):
    on0, step = info_ref[0] == 0, 2 * rows
    for at, ref in ((0, texts_ref), (step, images_ref)):
        whole = ref[...].astype(F32).T
        first, second = whole[:step], whole[step:]
        keep_ref[at : at + step, :] = jnp.where(on0, first, second).astype(BF)
        send_ref[at : at + step, :] = jnp.where(on0, second, first).astype(BF)


def join_kernel(rows, info_ref, own_ref, got_ref, texts_ref, images_ref):
    on0, step = info_ref[0] == 0, 2 * rows
    for at, ref in ((0, texts_ref), (step, images_ref)):
        own, got = own_ref[at : at + step, :], got_ref[at : at + step, :]
        ref[...] = jnp.concatenate([jnp.where(on0, own, got), jnp.where(on0, got, own)], axis=0).T


def near_kernel(
    rows, half, feats, info_ref, scale_ref, ta_ref, tb_ref, im0_ref, im1_ref,
    grads, m_ref, t_rel, coeff_low, sums_ref, images,
):
    quarter = 4 * rows
    images[0:quarter, :] = im0_ref[...]
    images[quarter : 2 * quarter, :] = im1_ref[...]
    pairs(info_ref, rows, half, ta_ref, tb_ref, t_rel)
    sums_ref[...] = coefficients(True, rows, info_ref, scale_ref, t_rel, images, coeff_low)
    text_parts(info_ref, rows, half, coeff_low, images, grads)
    m_ref[...] = message([grads[1, i] for i in range(4)], feats)


def near_image_kernel(t_rel, coeff_low, acc_ref):
    acc_ref[...] = image_parts(coeff_low, t_rel)


def far_kernel(
    rows, half, feats, info_ref, scale_ref, ta_ref, tb_ref, im0_ref, im1_ref, before_ref, sums_before,
    ma_ref, mb_ref, own_ref, other_ref, images, t_rel, coeff_low, grads,
):
    quarter = 4 * rows
    images[0:quarter, :] = im0_ref[...]
    images[quarter : 2 * quarter, :] = im1_ref[...]
    pairs(info_ref, rows, half, ta_ref, tb_ref, t_rel)
    sums = coefficients(False, rows, info_ref, scale_ref, t_rel, images, coeff_low) + sums_before[...]
    text_parts(info_ref, rows, half, coeff_low, images, grads)
    for k, m_ref in ((0, ma_ref), (1, mb_ref)):
        m_ref[...] = message([grads[k, i] for i in range(4)], feats)
    acc = image_parts(coeff_low, t_rel) + before_ref[...]
    wide = jnp.concatenate([sums] * (feats // 128), axis=1)
    own_ref[...] = jnp.concatenate([acc[0:quarter], wide], axis=0)
    other_ref[...] = jnp.concatenate([acc[quarter : 2 * quarter], wide], axis=0)


def message(blocks, feats, extra=()):
    part = jnp.concatenate(blocks, axis=0)
    m = top_of(jnp.max(jnp.max(jnp.abs(part), axis=0, keepdims=True), axis=1, keepdims=True))
    tail = jnp.broadcast_to(m, (8 - len(extra), feats))
    return jnp.concatenate([encode(part, m), *extra, tail], axis=0).astype(BF)


def decoded(ref):
    whole = ref[...].astype(F32)
    n = whole.shape[0] - 8
    return decode(whole[:n], whole[n + 7 : n + 8]), whole[n:]


def split3(v):
    hi = v.astype(BF).astype(F32)
    mid = (v - hi).astype(BF).astype(F32)
    return [hi, mid, v - hi - mid]


def image_first_kernel(rows, feats, own_ref, other_ref, out_ref, *messages):
    total = own_ref[...] + other_ref[...]
    sums = total[4 * rows :]
    out_ref[...] = jnp.concatenate([total[0:rows], sums], axis=0)
    for i, m_ref in enumerate(messages):
        m_ref[...] = message([total[(i + 1) * rows : (i + 2) * rows]], feats, split3(sums[0:1]))


def with_scalars(own_ref, refs):
    n = own_ref.shape[0] - 8
    total, tails = own_ref[0:n, :], []
    for r in refs:
        value, tail = decoded(r)
        total = total + value
        tails.append(tail[0:1] + (tail[1:2] + tail[2:3]))
    return total, (own_ref[n : n + 1, :] + tails[0]) + (tails[1] + tails[2])


def image_last_kernel(feats, scale_ref, own_ref, r1_ref, r2_ref, r3_ref, out_ref, sums_ref):
    total, sums = with_scalars(own_ref, (r1_ref, r2_ref, r3_ref))
    out_ref[...] = total * scale_ref[0]
    sums_ref[...] = jnp.broadcast_to(sums, (8, feats))


def text_near_kernel(grads_ref, r1_ref, out_ref):
    out_ref[...] = jnp.concatenate([grads_ref[0, i] for i in range(4)], axis=0) + decoded(r1_ref)[0]


def text_first_kernel(rows, feats, own_ref, r2_ref, r3_ref, sums_ref, out_ref, m1_ref, m2_ref, m3_ref, total):
    tops = [r[4 * rows :, :].astype(F32)[7:8] for r in (r2_ref, r3_ref)]

    def add(step, carry):
        at = pl.ds(pl.multiple_of(step * 32, 32), 32)
        total[at, :] = own_ref[at, :] + decode(r2_ref[at, :], tops[0]) + decode(r3_ref[at, :], tops[1])
        return carry

    lax.fori_loop(0, 4 * rows // 32, add, 0)
    out_ref[...] = jnp.concatenate([total[0:rows, :], sums_ref[...]], axis=0)
    for i, m_ref in enumerate((m1_ref, m2_ref, m3_ref)):
        m_ref[...] = message([total[(i + 1) * rows : (i + 2) * rows, :]], feats, split3(sums_ref[0:1, :]))


def text_last_kernel(scale_ref, own_ref, r1_ref, r2_ref, r3_ref, out_ref, sums_ref):
    total, sums = with_scalars(own_ref, (r1_ref, r2_ref, r3_ref))
    out_ref[...] = total * scale_ref[0]
    sums_ref[...] = jnp.broadcast_to(sums[:, :128], (8, 128))


VMEM = pl.BlockSpec(memory_space=pltpu.VMEM)
SMEM = pl.BlockSpec(memory_space=pltpu.SMEM)


def grant(mib):
    return pltpu.CompilerParams(vmem_limit_bytes=mib * 1024 * 1024)


def after(array, *others):
    return lax.optimization_barrier((array, *others))[0]


def body(picture_embeds, caption_embeds, logit_scaler, logit_offset_term):
    height, width = picture_embeds.shape
    rows, half, feats = height // 4, 2 * width, 4 * width
    step, quarter = 2 * rows, 4 * rows
    index = lax.axis_index("batch") * lax.axis_size("dim") + lax.axis_index("dim")
    core, z_lo = index & 1, (index >> 1) & 1
    on0, lo0 = core == 0, z_lo == 0
    scaling = logit_scaler[0]

    def by(first_one, own, other):
        return [jnp.where(first_one, own, other), jnp.where(first_one, other, own)]

    def f32(*shape):
        return jax.ShapeDtypeStruct(shape, F32)

    def bf16(*shape):
        return jax.ShapeDtypeStruct(shape, BF)

    def call(kernel, name, out_shape, *args, scalars=0, scratch=(), mib=20, products=0):
        return pl.pallas_call(
            kernel,
            out_shape=out_shape,
            in_specs=[SMEM] * scalars + [VMEM] * (len(args) - scalars),
            out_specs=[VMEM] * len(out_shape),
            scratch_shapes=scratch,
            compiler_params=grant(mib),
            cost_estimate=pl.CostEstimate(
                flops=products * 2 * quarter * 2 * quarter * 2 * feats,
                bytes_accessed=sum(a.size * a.dtype.itemsize for a in (*args, *out_shape)),
                transcendentals=products * 4 * quarter * quarter,
            ),
            name=name,
        )(*args)

    info = jnp.stack([core, z_lo]).astype(jnp.int32)
    keep, send = call(
        functools.partial(split_kernel, rows), "split", [bf16(height, width)] * 2, info, caption_embeds.T, picture_embeds.T, scalars=1
    )
    chip = jnp.concatenate(by(on0, keep, swap(send, CORE)), axis=1)
    packed = jnp.concatenate([chip[:rows], chip[rows:step]], axis=1)
    keep, send = by(lo0, chip[step : step + rows], chip[step + rows :])
    first = [packed] + [swap(packed, y_mask(i), z_mask(i)) for i in range(1, 4)]
    image = jnp.concatenate([keep, swap(send, z_mask(1))], axis=1)
    stack = jnp.stack(first)
    second1, second3 = (swap(stack, z_mask(j), y_mask(j)) for j in (1, 3))
    images_own = jnp.concatenate([image] + [swap(image, x_mask(k)) for k in range(1, 4)], axis=0)
    images_other = swap(images_own, CORE)
    second2 = swap(after(stack, images_own), z_mask(2), y_mask(2))
    second1, second3 = lax.optimization_barrier((second1, second3))

    sizes = (rows, half, feats)
    scales = jnp.stack([scaling, logit_offset_term[0]])
    images_shape, coeff_shape = (2 * quarter, feats), (2 * quarter, 2 * quarter)
    grads = pltpu.VMEM((2, 4, rows, feats), F32)
    scratch = [pltpu.VMEM(images_shape, BF), pltpu.VMEM(images_shape, BF), pltpu.VMEM(coeff_shape, BF), grads]
    text, m1, t_near, c_near, sums = call(
        functools.partial(near_kernel, *sizes), "tile_near",
        [f32(2, 4, rows, feats), bf16(quarter + 8, feats), bf16(*images_shape), bf16(*coeff_shape), f32(8, 128)],
        info, scales, stack, second1, images_own, images_other,
        scalars=2, mib=36, products=2, scratch=[scratch[0]],
    )
    got1 = swap(m1, z_mask(1), y_mask(1))
    (acc,) = call(near_image_kernel, "image_near", [f32(*images_shape)], t_near, c_near, mib=30, products=1)
    second2 = after(second2, acc)
    m2, m3, img_own, img_other = call(
        functools.partial(far_kernel, *sizes), "tile_far",
        [bf16(quarter + 8, feats), bf16(quarter + 8, feats), f32(quarter + 8, feats), f32(quarter + 8, feats)],
        info, scales, second2, second3, images_own, images_other, acc, sums,
        scalars=2, mib=40, products=3, scratch=scratch,
    )
    img_other, got1 = lax.optimization_barrier((img_other, got1))
    got2, got3 = swap(m2, z_mask(2), y_mask(2)), swap(m3, z_mask(3), y_mask(3))
    img, *messages = call(
        functools.partial(image_first_kernel, rows, feats), "image_first",
        [f32(rows + 8, feats)] + [bf16(rows + 8, feats)] * 3, img_own, swap(img_other, CORE),
    )
    img_got = [swap(m, x_mask(k)) for k, m in zip((1, 2, 3), messages)]
    (text,) = call(text_near_kernel, "text_near", [f32(quarter, feats)], after(text, *messages), got1)
    img, sums = call(
        functools.partial(image_last_kernel, feats), "image_last", [f32(rows, feats), f32(8, feats)],
        logit_scaler, img, *img_got, scalars=1,
    )
    text, *messages = call(
        functools.partial(text_first_kernel, rows, feats), "text_first",
        [f32(rows + 8, feats)] + [bf16(rows + 8, feats)] * 3, text, got2, got3, sums,
        scratch=[pltpu.VMEM((quarter, feats), F32)],
    )
    got = [swap(m, y_mask(i), z_mask(i)) for i, m in zip((1, 2, 3), messages)]
    text, sums = call(
        text_last_kernel, "text_last", [f32(rows, feats), f32(8, 128)], logit_scaler, text, *got, scalars=1, products=2
    )
    image = jnp.concatenate(by(lo0, img[:, :half], after(swap(img[:, half:], z_mask(1)), text)), axis=0)
    whole = jnp.concatenate([text[:, :half], text[:, half:], image], axis=0)
    mine, other = by(on0, whole[:, :width], whole[:, width:])
    sums = after(sums, other)
    other = swap(other, CORE)
    text_grad, image_grad = call(
        functools.partial(join_kernel, rows), "join", [f32(width, height)] * 2, info, mine, other, scalars=1
    )
    s1, s2, s3 = (after(swap(sums, z_mask(k), y_mask(k)), text_grad, image_grad) for k in (1, 2, 3))
    sums = (sums + s1) + (s2 + s3)
    return (image_grad.T, text_grad.T, sums[0, :2])


def solution(mesh):
    placed = (P("batch", "dim"), P("batch", "dim"), P(), P())
    return jax.shard_map(
        body,
        mesh=mesh,
        in_specs=placed,
        out_specs=(P("batch", "dim"), P("batch", "dim"), P()),
        check_vma=False,
    )
```

```python
import functools

import jax
import jax.numpy as jnp
from jax import lax
from jax.experimental import pallas as pl
from jax.experimental.pallas import tpu as pltpu
from jax.sharding import PartitionSpec as P

BF = jnp.bfloat16
F32 = jnp.float32
AXES = ("batch", "dim")
CORE = 1


def x_mask(k):
    return k << 2


def y_mask(k):
    return k << 4


def z_mask(k):
    return ((k >> 1) << 6) | ((k & 1) << 1)


def swap(array, mask0, mask1=None):
    mask1 = mask0 if mask1 is None else mask1
    n = lax.axis_size("batch") * lax.axis_size("dim")
    return lax.ppermute(array, AXES, [(i, i ^ (mask1 if i & 1 else mask0)) for i in range(n)])


LOW = 2.0**-3.5


def encode(v, m):
    a = jnp.abs(v) * (127.0 * LOW / m) + LOW
    for _ in range(5):
        a = a * a
    return jnp.where(v < 0, -a, a)


def decode(code, m):
    c = code.astype(F32)
    a = jnp.exp(jnp.log(jnp.abs(c)) * (1.0 / 32.0)) * (1.0 / LOW) - 1.0
    v = a * (m * (1.0 / 127.0))
    return jnp.where(c < 0, -v, v)


def top_of(largest):
    return (largest * 1.01 + 1e-30).astype(BF).astype(F32)


def pairs(core_ref, rows, half, ta_ref, tb_ref, t_rel):
    on0, step = core_ref[0] == 0, 2 * rows
    for b in range(4):
        other = (ta_ref, tb_ref)[b >> 1]
        p0 = jnp.where(on0, ta_ref[b].astype(F32), other[2 * (b & 1)].astype(F32))
        p1 = jnp.where(on0, tb_ref[b].astype(F32), other[2 * (b & 1) + 1].astype(F32))
        top = jnp.concatenate([p0[:, :half], p1[:, :half]], axis=1)
        bottom = jnp.concatenate([p0[:, half:], p1[:, half:]], axis=1)
        t_rel[b * step : (b + 1) * step, :] = jnp.concatenate([top, bottom], axis=0).astype(BF)


def coefficients(near, rows, info_ref, scale_ref, t_rel, images, coeff_low):
    scaling, offset = scale_ref[0], scale_ref[1]
    step, columns = 2 * rows, images.shape[0]
    similar = lax.dot_general(t_rel[...], images[...], (((1,), (1,)), ((), ())), preferred_element_type=F32)
    temp, bias = jnp.zeros((1, columns), F32), jnp.zeros((1, columns), F32)
    for b in range(4):
        part = similar[b * step : (b + 1) * step]
        logits = scaling * part + offset
        if near and b == 0:
            row = lax.broadcasted_iota(jnp.int32, part.shape, 0)
            column = lax.broadcasted_iota(jnp.int32, part.shape, 1)
            matched = (row - rows * info_ref[1] == column) & (column < rows)
            sig = 1.0 / (1.0 + jnp.exp(jnp.where(matched, logits, -logits)))
            coeff = jnp.where(matched, -sig, sig)
        else:
            coeff = 1.0 / (1.0 + jnp.exp(-logits))
        coeff_low[b * step : (b + 1) * step, :] = coeff.astype(BF)
        temp = temp + jnp.sum(coeff * part, axis=0, keepdims=True)
        bias = bias + jnp.sum(coeff, axis=0, keepdims=True)
    even = lax.broadcasted_iota(jnp.int32, (8, 128), 1) % 2 == 0
    return jnp.where(even, jnp.sum(temp, axis=1, keepdims=True), jnp.sum(bias, axis=1, keepdims=True))


def text_parts(core_ref, rows, half, coeff_low, images, grads):
    on0, step = core_ref[0] == 0, 2 * rows
    part = jnp.dot(coeff_low[...], images[...], preferred_element_type=F32)
    for b in range(4):
        top, bottom = part[b * step : b * step + rows], part[b * step + rows : (b + 1) * step]
        for e, at in ((0, slice(0, half)), (1, slice(half, 2 * half))):
            place = jnp.where(on0, e, b >> 1), jnp.where(on0, b, 2 * (b & 1) + e)
            grads[place] = jnp.concatenate([top[:, at], bottom[:, at]], axis=1)


def image_parts(coeff_low, t_rel):
    return lax.dot_general(coeff_low[...], t_rel[...], (((0,), (0,)), ((), ())), preferred_element_type=F32)


def split_kernel(rows, info_ref, texts_ref, images_ref, keep_ref, send_ref):
    on0, step = info_ref[0] == 0, 2 * rows
    for at, ref in ((0, texts_ref), (step, images_ref)):
        whole = ref[...].astype(F32).T
        first, second = whole[:step], whole[step:]
        keep_ref[at : at + step, :] = jnp.where(on0, first, second).astype(BF)
        send_ref[at : at + step, :] = jnp.where(on0, second, first).astype(BF)


def join_kernel(rows, info_ref, own_ref, got_ref, texts_ref, images_ref, whole, sems):
    on0, step = info_ref[0] == 0, 2 * rows
    copies = []
    for k, ref in enumerate((texts_ref, images_ref)):
        own, got = own_ref[k * step : (k + 1) * step, :], got_ref[k * step : (k + 1) * step, :]
        whole[k] = jnp.concatenate([jnp.where(on0, own, got), jnp.where(on0, got, own)], axis=0).T
        copies.append(pltpu.make_async_copy(whole.at[k], ref, sems.at[k]))
        copies[k].start()
    for copy in copies:
        copy.wait()


def near_kernel(
    rows, half, feats, info_ref, scale_ref, ta_ref, tb_ref, im0_ref, im1_ref,
    grads, m_ref, t_rel, coeff_low, sums_ref, images,
):
    quarter = 4 * rows
    images[0:quarter, :] = im0_ref[...]
    images[quarter : 2 * quarter, :] = im1_ref[...]
    pairs(info_ref, rows, half, ta_ref, tb_ref, t_rel)
    sums_ref[...] = coefficients(True, rows, info_ref, scale_ref, t_rel, images, coeff_low)
    text_parts(info_ref, rows, half, coeff_low, images, grads)
    m_ref[...] = message([grads[1, i] for i in range(4)], feats)


def near_image_kernel(t_rel, coeff_low, acc_ref):
    acc_ref[...] = image_parts(coeff_low, t_rel)


def far_kernel(
    rows, half, feats, info_ref, scale_ref, ta_ref, tb_ref, im0_ref, im1_ref, before_ref, sums_before,
    ma_ref, mb_ref, own_ref, other_ref, images, t_rel, coeff_low, grads,
):
    quarter = 4 * rows
    images[0:quarter, :] = im0_ref[...]
    images[quarter : 2 * quarter, :] = im1_ref[...]
    pairs(info_ref, rows, half, ta_ref, tb_ref, t_rel)
    sums = coefficients(False, rows, info_ref, scale_ref, t_rel, images, coeff_low) + sums_before[...]
    text_parts(info_ref, rows, half, coeff_low, images, grads)
    for k, m_ref in ((0, ma_ref), (1, mb_ref)):
        m_ref[...] = message([grads[k, i] for i in range(4)], feats)
    acc = image_parts(coeff_low, t_rel) + before_ref[...]
    wide = jnp.concatenate([sums] * (feats // 128), axis=1)
    own_ref[...] = jnp.concatenate([acc[0:quarter], wide], axis=0)
    other_ref[...] = jnp.concatenate([acc[quarter : 2 * quarter], wide], axis=0)


def message(blocks, feats, extra=()):
    part = jnp.concatenate(blocks, axis=0)
    m = top_of(jnp.max(jnp.max(jnp.abs(part), axis=0, keepdims=True), axis=1, keepdims=True))
    tail = jnp.broadcast_to(m, (8 - len(extra), feats))
    return jnp.concatenate([encode(part, m), *extra, tail], axis=0).astype(BF)


def decoded(ref):
    whole = ref[...].astype(F32)
    n = whole.shape[0] - 8
    return decode(whole[:n], whole[n + 7 : n + 8]), whole[n:]


def split3(v):
    hi = v.astype(BF).astype(F32)
    mid = (v - hi).astype(BF).astype(F32)
    return [hi, mid, v - hi - mid]


def image_first_kernel(rows, feats, own_ref, other_ref, out_ref, *messages):
    total = own_ref[...] + other_ref[...]
    sums = total[4 * rows :]
    out_ref[...] = jnp.concatenate([total[0:rows], sums], axis=0)
    for i, m_ref in enumerate(messages):
        m_ref[...] = message([total[(i + 1) * rows : (i + 2) * rows]], feats, split3(sums[0:1]))


def with_scalars(own_ref, refs):
    n = own_ref.shape[0] - 8
    total, tails = own_ref[0:n, :], []
    for r in refs:
        value, tail = decoded(r)
        total = total + value
        tails.append(tail[0:1] + (tail[1:2] + tail[2:3]))
    return total, (own_ref[n : n + 1, :] + tails[0]) + (tails[1] + tails[2])


def image_last_kernel(feats, scale_ref, own_ref, r1_ref, r2_ref, r3_ref, out_ref, sums_ref):
    total, sums = with_scalars(own_ref, (r1_ref, r2_ref, r3_ref))
    out_ref[...] = total * scale_ref[0]
    sums_ref[...] = jnp.broadcast_to(sums, (8, feats))


def text_near_kernel(grads_ref, r1_ref, out_ref):
    out_ref[...] = jnp.concatenate([grads_ref[0, i] for i in range(4)], axis=0) + decoded(r1_ref)[0]


def text_first_kernel(rows, feats, own_ref, r2_ref, r3_ref, sums_ref, out_ref, m1_ref, m2_ref, m3_ref, total):
    tops = [r[4 * rows :, :].astype(F32)[7:8] for r in (r2_ref, r3_ref)]

    def add(step, carry):
        at = pl.ds(pl.multiple_of(step * 32, 32), 32)
        total[at, :] = own_ref[at, :] + decode(r2_ref[at, :], tops[0]) + decode(r3_ref[at, :], tops[1])
        return carry

    lax.fori_loop(0, 4 * rows // 32, add, 0, unroll=2)
    out_ref[...] = jnp.concatenate([total[0:rows, :], sums_ref[...]], axis=0)
    for i, m_ref in enumerate((m1_ref, m2_ref, m3_ref)):
        m_ref[...] = message([total[(i + 1) * rows : (i + 2) * rows, :]], feats, split3(sums_ref[0:1, :]))


def text_last_kernel(scale_ref, own_ref, r1_ref, r2_ref, r3_ref, out_ref, sums_ref):
    total, sums = with_scalars(own_ref, (r1_ref, r2_ref, r3_ref))
    out_ref[...] = total * scale_ref[0]
    sums_ref[...] = jnp.broadcast_to(sums[:, :128], (8, 128))


VMEM = pl.BlockSpec(memory_space=pltpu.VMEM)
HBM = pl.BlockSpec(memory_space=pl.ANY)
SMEM = pl.BlockSpec(memory_space=pltpu.SMEM)


def grant(mib):
    return pltpu.CompilerParams(vmem_limit_bytes=mib * 1024 * 1024)


def after(array, *others):
    return lax.optimization_barrier((array, *others))[0]


def body(picture_embeds, caption_embeds, logit_scaler, logit_offset_term):
    height, width = picture_embeds.shape
    rows, half, feats = height // 4, 2 * width, 4 * width
    step, quarter = 2 * rows, 4 * rows
    index = lax.axis_index("batch") * lax.axis_size("dim") + lax.axis_index("dim")
    core, z_lo = index & 1, (index >> 1) & 1
    on0, lo0 = core == 0, z_lo == 0
    scaling = logit_scaler[0]

    def by(first_one, own, other):
        return [jnp.where(first_one, own, other), jnp.where(first_one, other, own)]

    def f32(*shape):
        return jax.ShapeDtypeStruct(shape, F32)

    def bf16(*shape):
        return jax.ShapeDtypeStruct(shape, BF)

    def call(kernel, name, out_shape, *args, scalars=0, scratch=(), mib=20, products=0, out=VMEM):
        return pl.pallas_call(
            kernel,
            out_shape=out_shape,
            in_specs=[SMEM] * scalars + [VMEM] * (len(args) - scalars),
            out_specs=[out] * len(out_shape),
            scratch_shapes=scratch,
            compiler_params=grant(mib),
            cost_estimate=pl.CostEstimate(
                flops=products * 2 * quarter * 2 * quarter * 2 * feats,
                bytes_accessed=sum(a.size * a.dtype.itemsize for a in (*args, *out_shape)),
                transcendentals=products * 4 * quarter * quarter,
            ),
            name=name,
        )(*args)

    info = jnp.stack([core, z_lo]).astype(jnp.int32)
    keep, send = call(
        functools.partial(split_kernel, rows), "split", [bf16(height, width)] * 2, info, caption_embeds.T, picture_embeds.T, scalars=1
    )
    chip = jnp.concatenate(by(on0, keep, swap(send, CORE)), axis=1)
    packed = jnp.concatenate([chip[:rows], chip[rows:step]], axis=1)
    keep, send = by(lo0, chip[step : step + rows], chip[step + rows :])
    first = [packed] + [swap(packed, y_mask(i), z_mask(i)) for i in range(1, 4)]
    image = jnp.concatenate([keep, swap(send, z_mask(1))], axis=1)
    stack = jnp.stack(first)
    second1, second3 = (swap(stack, z_mask(j), y_mask(j)) for j in (1, 3))
    images_own = jnp.concatenate([image] + [swap(image, x_mask(k)) for k in range(1, 4)], axis=0)
    images_other = swap(images_own, CORE)
    second2 = swap(after(stack, images_own), z_mask(2), y_mask(2))
    second1, second3 = lax.optimization_barrier((second1, second3))

    sizes = (rows, half, feats)
    scales = jnp.stack([scaling, logit_offset_term[0]])
    images_shape, coeff_shape = (2 * quarter, feats), (2 * quarter, 2 * quarter)
    grads = pltpu.VMEM((2, 4, rows, feats), F32)
    scratch = [pltpu.VMEM(images_shape, BF), pltpu.VMEM(images_shape, BF), pltpu.VMEM(coeff_shape, BF), grads]
    text, m1, t_near, c_near, sums = call(
        functools.partial(near_kernel, *sizes), "tile_near",
        [f32(2, 4, rows, feats), bf16(quarter + 8, feats), bf16(*images_shape), bf16(*coeff_shape), f32(8, 128)],
        info, scales, stack, second1, images_own, images_other,
        scalars=2, mib=36, products=2, scratch=[scratch[0]],
    )
    got1 = swap(m1, z_mask(1), y_mask(1))
    (acc,) = call(near_image_kernel, "image_near", [f32(*images_shape)], t_near, c_near, mib=30, products=1)
    second2 = after(second2, acc)
    m2, m3, img_own, img_other = call(
        functools.partial(far_kernel, *sizes), "tile_far",
        [bf16(quarter + 8, feats), bf16(quarter + 8, feats), f32(quarter + 8, feats), f32(quarter + 8, feats)],
        info, scales, second2, second3, images_own, images_other, acc, sums,
        scalars=2, mib=40, products=3, scratch=scratch,
    )
    img_other, got1 = lax.optimization_barrier((img_other, got1))
    got2, got3 = swap(m2, z_mask(2), y_mask(2)), swap(m3, z_mask(3), y_mask(3))
    img, *messages = call(
        functools.partial(image_first_kernel, rows, feats), "image_first",
        [f32(rows + 8, feats)] + [bf16(rows + 8, feats)] * 3, img_own, swap(img_other, CORE),
    )
    img_got = [swap(m, x_mask(k)) for k, m in zip((1, 2, 3), messages)]
    (text,) = call(text_near_kernel, "text_near", [f32(quarter, feats)], after(text, *messages), got1)
    img, sums = call(
        functools.partial(image_last_kernel, feats), "image_last", [f32(rows, feats), f32(8, feats)],
        logit_scaler, img, *img_got, scalars=1,
    )
    text, *messages = call(
        functools.partial(text_first_kernel, rows, feats), "text_first",
        [f32(rows + 8, feats)] + [bf16(rows + 8, feats)] * 3, text, got2, got3, sums,
        scratch=[pltpu.VMEM((quarter, feats), F32)],
    )
    got = [swap(m, y_mask(i), z_mask(i)) for i, m in zip((1, 2, 3), messages)]
    text, sums = call(
        text_last_kernel, "text_last", [f32(rows, feats), f32(8, 128)], logit_scaler, text, *got, scalars=1, products=2
    )
    image = jnp.concatenate(by(lo0, img[:, :half], after(swap(img[:, half:], z_mask(1)), text)), axis=0)
    whole = jnp.concatenate([text[:, :half], text[:, half:], image], axis=0)
    mine, other = by(on0, whole[:, :width], whole[:, width:])
    sums = after(sums, other)
    other = swap(other, CORE)
    text_grad, image_grad = call(
        functools.partial(join_kernel, rows), "join", [f32(width, height)] * 2, info, mine, other, scalars=1,
        out=HBM, scratch=[pltpu.VMEM((2, width, height), F32), pltpu.SemaphoreType.DMA((2,))],
    )
    s1, s2, s3 = (after(swap(sums, z_mask(k), y_mask(k)), text_grad, image_grad) for k in (1, 2, 3))
    sums = (sums + s1) + (s2 + s3)
    return (image_grad.T, text_grad.T, sums[0, :2])


def solution(mesh):
    placed = (P("batch", "dim"), P("batch", "dim"), P(), P())
    return jax.shard_map(
        body,
        mesh=mesh,
        in_specs=placed,
        out_specs=(P("batch", "dim"), P("batch", "dim"), P()),
        check_vma=False,
    )
```

```python
import functools

import jax
import jax.numpy as jnp
from jax import lax
from jax.experimental import pallas as pl
from jax.experimental.pallas import tpu as pltpu
from jax.sharding import PartitionSpec as P

BF = jnp.bfloat16
F32 = jnp.float32
AXES = ("batch", "dim")
CORE = 1


def x_mask(k):
    return k << 2


def y_mask(k):
    return k << 4


def z_mask(k):
    return ((k >> 1) << 6) | ((k & 1) << 1)


def swap(array, mask0, mask1=None):
    mask1 = mask0 if mask1 is None else mask1
    n = lax.axis_size("batch") * lax.axis_size("dim")
    return lax.ppermute(array, AXES, [(i, i ^ (mask1 if i & 1 else mask0)) for i in range(n)])


LOW = 2.0**-3.5


def encode(v, m):
    a = jnp.abs(v) * (127.0 * LOW / m) + LOW
    for _ in range(5):
        a = a * a
    return jnp.where(v < 0, -a, a)


def decode(code, m):
    c = code.astype(F32)
    a = jnp.exp(jnp.log(jnp.abs(c)) * (1.0 / 32.0)) * (1.0 / LOW) - 1.0
    v = a * (m * (1.0 / 127.0))
    return jnp.where(c < 0, -v, v)


def top_of(largest):
    return (largest * 1.01 + 1e-30).astype(BF).astype(F32)


def pairs(core_ref, rows, half, ta_ref, tb_ref, t_rel):
    on0, step = core_ref[0] == 0, 2 * rows
    for b in range(4):
        other = (ta_ref, tb_ref)[b >> 1]
        p0 = jnp.where(on0, ta_ref[b].astype(F32), other[2 * (b & 1)].astype(F32))
        p1 = jnp.where(on0, tb_ref[b].astype(F32), other[2 * (b & 1) + 1].astype(F32))
        top = jnp.concatenate([p0[:, :half], p1[:, :half]], axis=1)
        bottom = jnp.concatenate([p0[:, half:], p1[:, half:]], axis=1)
        t_rel[b * step : (b + 1) * step, :] = jnp.concatenate([top, bottom], axis=0).astype(BF)


def coefficients(near, rows, info_ref, scale_ref, t_rel, images, coeff_low):
    scaling, offset = scale_ref[0], scale_ref[1]
    step, columns = 2 * rows, images.shape[0]
    similar = lax.dot_general(t_rel[...], images[...], (((1,), (1,)), ((), ())), preferred_element_type=F32)
    temp, bias = jnp.zeros((1, columns), F32), jnp.zeros((1, columns), F32)
    for b in range(4):
        part = similar[b * step : (b + 1) * step]
        logits = scaling * part + offset
        if near and b == 0:
            row = lax.broadcasted_iota(jnp.int32, part.shape, 0)
            column = lax.broadcasted_iota(jnp.int32, part.shape, 1)
            matched = (row - rows * info_ref[1] == column) & (column < rows)
            sig = 1.0 / (1.0 + jnp.exp(jnp.where(matched, logits, -logits)))
            coeff = jnp.where(matched, -sig, sig)
        else:
            coeff = 1.0 / (1.0 + jnp.exp(-logits))
        coeff_low[b * step : (b + 1) * step, :] = coeff.astype(BF)
        temp = temp + jnp.sum(coeff * part, axis=0, keepdims=True)
        bias = bias + jnp.sum(coeff, axis=0, keepdims=True)
    even = lax.broadcasted_iota(jnp.int32, (8, 128), 1) % 2 == 0
    return jnp.where(even, jnp.sum(temp, axis=1, keepdims=True), jnp.sum(bias, axis=1, keepdims=True))


def text_parts(core_ref, rows, half, coeff_low, images, grads):
    on0, step = core_ref[0] == 0, 2 * rows
    part = jnp.dot(coeff_low[...], images[...], preferred_element_type=F32)
    for b in range(4):
        top, bottom = part[b * step : b * step + rows], part[b * step + rows : (b + 1) * step]
        for e, at in ((0, slice(0, half)), (1, slice(half, 2 * half))):
            place = jnp.where(on0, e, b >> 1), jnp.where(on0, b, 2 * (b & 1) + e)
            grads[place] = jnp.concatenate([top[:, at], bottom[:, at]], axis=1)


def image_parts(coeff_low, t_rel):
    return lax.dot_general(coeff_low[...], t_rel[...], (((0,), (0,)), ((), ())), preferred_element_type=F32)


def split_kernel(rows, width, info_ref, both_ref, keep_ref, send_ref):
    on0, step = info_ref[0] == 0, 2 * rows
    for k in range(2):
        whole = both_ref[k * width : (k + 1) * width, :].astype(F32).T
        first, second = whole[:step], whole[step:]
        keep_ref[k * step : (k + 1) * step, :] = jnp.where(on0, first, second).astype(BF)
        send_ref[k * step : (k + 1) * step, :] = jnp.where(on0, second, first).astype(BF)


def join_kernel(rows, info_ref, own_ref, got_ref, texts_ref, images_ref):
    on0, step = info_ref[0] == 0, 2 * rows
    for at, ref in ((0, texts_ref), (step, images_ref)):
        own, got = own_ref[at : at + step, :], got_ref[at : at + step, :]
        ref[...] = jnp.concatenate([jnp.where(on0, own, got), jnp.where(on0, got, own)], axis=0).T


def near_kernel(
    rows, half, feats, info_ref, scale_ref, ta_ref, tb_ref, im0_ref, im1_ref,
    grads, m_ref, t_rel, coeff_low, sums_ref, images,
):
    quarter = 4 * rows
    images[0:quarter, :] = im0_ref[...]
    images[quarter : 2 * quarter, :] = im1_ref[...]
    pairs(info_ref, rows, half, ta_ref, tb_ref, t_rel)
    sums_ref[...] = coefficients(True, rows, info_ref, scale_ref, t_rel, images, coeff_low)
    text_parts(info_ref, rows, half, coeff_low, images, grads)
    m_ref[...] = message([grads[1, i] for i in range(4)], feats)


def near_image_kernel(t_rel, coeff_low, acc_ref):
    acc_ref[...] = image_parts(coeff_low, t_rel)


def far_kernel(
    rows, half, feats, info_ref, scale_ref, ta_ref, tb_ref, im0_ref, im1_ref, before_ref, sums_before,
    ma_ref, mb_ref, own_ref, other_ref, images, t_rel, coeff_low, grads,
):
    quarter = 4 * rows
    images[0:quarter, :] = im0_ref[...]
    images[quarter : 2 * quarter, :] = im1_ref[...]
    pairs(info_ref, rows, half, ta_ref, tb_ref, t_rel)
    sums = coefficients(False, rows, info_ref, scale_ref, t_rel, images, coeff_low) + sums_before[...]
    text_parts(info_ref, rows, half, coeff_low, images, grads)
    for k, m_ref in ((0, ma_ref), (1, mb_ref)):
        m_ref[...] = message([grads[k, i] for i in range(4)], feats)
    acc = image_parts(coeff_low, t_rel) + before_ref[...]
    wide = jnp.concatenate([sums] * (feats // 128), axis=1)
    own_ref[...] = jnp.concatenate([acc[0:quarter], wide], axis=0)
    other_ref[...] = jnp.concatenate([acc[quarter : 2 * quarter], wide], axis=0)


def message(blocks, feats, extra=()):
    part = jnp.concatenate(blocks, axis=0)
    m = top_of(jnp.max(jnp.max(jnp.abs(part), axis=0, keepdims=True), axis=1, keepdims=True))
    tail = jnp.broadcast_to(m, (8 - len(extra), feats))
    return jnp.concatenate([encode(part, m), *extra, tail], axis=0).astype(BF)


def decoded(ref):
    whole = ref[...].astype(F32)
    n = whole.shape[0] - 8
    return decode(whole[:n], whole[n + 7 : n + 8]), whole[n:]


def split3(v):
    hi = v.astype(BF).astype(F32)
    mid = (v - hi).astype(BF).astype(F32)
    return [hi, mid, v - hi - mid]


def image_first_kernel(rows, feats, own_ref, other_ref, out_ref, *messages):
    total = own_ref[...] + other_ref[...]
    sums = total[4 * rows :]
    out_ref[...] = jnp.concatenate([total[0:rows], sums], axis=0)
    for i, m_ref in enumerate(messages):
        m_ref[...] = message([total[(i + 1) * rows : (i + 2) * rows]], feats, split3(sums[0:1]))


def with_scalars(own_ref, refs):
    n = own_ref.shape[0] - 8
    total, tails = own_ref[0:n, :], []
    for r in refs:
        value, tail = decoded(r)
        total = total + value
        tails.append(tail[0:1] + (tail[1:2] + tail[2:3]))
    return total, (own_ref[n : n + 1, :] + tails[0]) + (tails[1] + tails[2])


def image_last_kernel(feats, scale_ref, own_ref, r1_ref, r2_ref, r3_ref, out_ref, sums_ref):
    total, sums = with_scalars(own_ref, (r1_ref, r2_ref, r3_ref))
    out_ref[...] = total * scale_ref[0]
    sums_ref[...] = jnp.broadcast_to(sums, (8, feats))


def text_near_kernel(grads_ref, r1_ref, out_ref):
    out_ref[...] = jnp.concatenate([grads_ref[0, i] for i in range(4)], axis=0) + decoded(r1_ref)[0]


def text_first_kernel(rows, feats, own_ref, r2_ref, r3_ref, sums_ref, out_ref, m1_ref, m2_ref, m3_ref, total):
    tops = [r[4 * rows :, :].astype(F32)[7:8] for r in (r2_ref, r3_ref)]

    def add(step, carry):
        at = pl.ds(pl.multiple_of(step * 32, 32), 32)
        total[at, :] = own_ref[at, :] + decode(r2_ref[at, :], tops[0]) + decode(r3_ref[at, :], tops[1])
        return carry

    lax.fori_loop(0, 4 * rows // 32, add, 0)
    out_ref[...] = jnp.concatenate([total[0:rows, :], sums_ref[...]], axis=0)
    for i, m_ref in enumerate((m1_ref, m2_ref, m3_ref)):
        m_ref[...] = message([total[(i + 1) * rows : (i + 2) * rows, :]], feats, split3(sums_ref[0:1, :]))


def text_last_kernel(scale_ref, own_ref, r1_ref, r2_ref, r3_ref, out_ref, sums_ref):
    total, sums = with_scalars(own_ref, (r1_ref, r2_ref, r3_ref))
    out_ref[...] = total * scale_ref[0]
    sums_ref[...] = jnp.broadcast_to(sums[:, :128], (8, 128))


VMEM = pl.BlockSpec(memory_space=pltpu.VMEM)
SMEM = pl.BlockSpec(memory_space=pltpu.SMEM)


def grant(mib):
    return pltpu.CompilerParams(vmem_limit_bytes=mib * 1024 * 1024)


def after(array, *others):
    return lax.optimization_barrier((array, *others))[0]


def body(picture_embeds, caption_embeds, logit_scaler, logit_offset_term):
    height, width = picture_embeds.shape
    rows, half, feats = height // 4, 2 * width, 4 * width
    step, quarter = 2 * rows, 4 * rows
    index = lax.axis_index("batch") * lax.axis_size("dim") + lax.axis_index("dim")
    core, z_lo = index & 1, (index >> 1) & 1
    on0, lo0 = core == 0, z_lo == 0
    scaling = logit_scaler[0]

    def by(first_one, own, other):
        return [jnp.where(first_one, own, other), jnp.where(first_one, other, own)]

    def f32(*shape):
        return jax.ShapeDtypeStruct(shape, F32)

    def bf16(*shape):
        return jax.ShapeDtypeStruct(shape, BF)

    def call(kernel, name, out_shape, *args, scalars=0, scratch=(), mib=20, products=0):
        return pl.pallas_call(
            kernel,
            out_shape=out_shape,
            in_specs=[SMEM] * scalars + [VMEM] * (len(args) - scalars),
            out_specs=[VMEM] * len(out_shape),
            scratch_shapes=scratch,
            compiler_params=grant(mib),
            cost_estimate=pl.CostEstimate(
                flops=products * 2 * quarter * 2 * quarter * 2 * feats,
                bytes_accessed=sum(a.size * a.dtype.itemsize for a in (*args, *out_shape)),
                transcendentals=products * 4 * quarter * quarter,
            ),
            name=name,
        )(*args)

    info = jnp.stack([core, z_lo]).astype(jnp.int32)
    both = jnp.concatenate([caption_embeds.T, picture_embeds.T], axis=0)
    keep, send = call(functools.partial(split_kernel, rows, width), "split", [bf16(height, width)] * 2, info, both, scalars=1)
    chip = jnp.concatenate(by(on0, keep, swap(send, CORE)), axis=1)
    packed = jnp.concatenate([chip[:rows], chip[rows:step]], axis=1)
    keep, send = by(lo0, chip[step : step + rows], chip[step + rows :])
    first = [packed] + [swap(packed, y_mask(i), z_mask(i)) for i in range(1, 4)]
    image = jnp.concatenate([keep, swap(send, z_mask(1))], axis=1)
    stack = jnp.stack(first)
    second1, second3 = (swap(stack, z_mask(j), y_mask(j)) for j in (1, 3))
    images_own = jnp.concatenate([image] + [swap(image, x_mask(k)) for k in range(1, 4)], axis=0)
    images_other = swap(images_own, CORE)
    second2 = swap(after(stack, images_own), z_mask(2), y_mask(2))
    second1, second3 = lax.optimization_barrier((second1, second3))

    sizes = (rows, half, feats)
    scales = jnp.stack([scaling, logit_offset_term[0]])
    images_shape, coeff_shape = (2 * quarter, feats), (2 * quarter, 2 * quarter)
    grads = pltpu.VMEM((2, 4, rows, feats), F32)
    scratch = [pltpu.VMEM(images_shape, BF), pltpu.VMEM(images_shape, BF), pltpu.VMEM(coeff_shape, BF), grads]
    text, m1, t_near, c_near, sums = call(
        functools.partial(near_kernel, *sizes), "tile_near",
        [f32(2, 4, rows, feats), bf16(quarter + 8, feats), bf16(*images_shape), bf16(*coeff_shape), f32(8, 128)],
        info, scales, stack, second1, images_own, images_other,
        scalars=2, mib=36, products=2, scratch=[scratch[0]],
    )
    got1 = swap(m1, z_mask(1), y_mask(1))
    (acc,) = call(near_image_kernel, "image_near", [f32(*images_shape)], t_near, c_near, mib=30, products=1)
    second2 = after(second2, acc)
    m2, m3, img_own, img_other = call(
        functools.partial(far_kernel, *sizes), "tile_far",
        [bf16(quarter + 8, feats), bf16(quarter + 8, feats), f32(quarter + 8, feats), f32(quarter + 8, feats)],
        info, scales, second2, second3, images_own, images_other, acc, sums,
        scalars=2, mib=40, products=3, scratch=scratch,
    )
    img_other, got1 = lax.optimization_barrier((img_other, got1))
    got2, got3 = swap(m2, z_mask(2), y_mask(2)), swap(m3, z_mask(3), y_mask(3))
    img, *messages = call(
        functools.partial(image_first_kernel, rows, feats), "image_first",
        [f32(rows + 8, feats)] + [bf16(rows + 8, feats)] * 3, img_own, swap(img_other, CORE),
    )
    img_got = [swap(m, x_mask(k)) for k, m in zip((1, 2, 3), messages)]
    (text,) = call(text_near_kernel, "text_near", [f32(quarter, feats)], after(text, *messages), got1)
    img, sums = call(
        functools.partial(image_last_kernel, feats), "image_last", [f32(rows, feats), f32(8, feats)],
        logit_scaler, img, *img_got, scalars=1,
    )
    text, *messages = call(
        functools.partial(text_first_kernel, rows, feats), "text_first",
        [f32(rows + 8, feats)] + [bf16(rows + 8, feats)] * 3, text, got2, got3, sums,
        scratch=[pltpu.VMEM((quarter, feats), F32)],
    )
    got = [swap(m, y_mask(i), z_mask(i)) for i, m in zip((1, 2, 3), messages)]
    text, sums = call(
        text_last_kernel, "text_last", [f32(rows, feats), f32(8, 128)], logit_scaler, text, *got, scalars=1, products=2
    )
    image = jnp.concatenate(by(lo0, img[:, :half], after(swap(img[:, half:], z_mask(1)), text)), axis=0)
    whole = jnp.concatenate([text[:, :half], text[:, half:], image], axis=0)
    mine, other = by(on0, whole[:, :width], whole[:, width:])
    sums = after(sums, other)
    other = swap(other, CORE)
    text_grad, image_grad = call(
        functools.partial(join_kernel, rows), "join", [f32(width, height)] * 2, info, mine, other, scalars=1
    )
    s1, s2, s3 = (after(swap(sums, z_mask(k), y_mask(k)), text_grad, image_grad) for k in (1, 2, 3))
    sums = (sums + s1) + (s2 + s3)
    return (image_grad.T, text_grad.T, sums[0, :2])


def solution(mesh):
    placed = (P("batch", "dim"), P("batch", "dim"), P(), P())
    return jax.shard_map(
        body,
        mesh=mesh,
        in_specs=placed,
        out_specs=(P("batch", "dim"), P("batch", "dim"), P()),
        check_vma=False,
    )
```

```python
import functools

import jax
import jax.numpy as jnp
from jax import lax
from jax.experimental import pallas as pl
from jax.experimental.pallas import tpu as pltpu
from jax.sharding import PartitionSpec as P

BF = jnp.bfloat16
F32 = jnp.float32
AXES = ("batch", "dim")
CORE = 1


def x_mask(k):
    return k << 2


def y_mask(k):
    return k << 4


def z_mask(k):
    return ((k >> 1) << 6) | ((k & 1) << 1)


def swap(array, mask0, mask1=None):
    mask1 = mask0 if mask1 is None else mask1
    n = lax.axis_size("batch") * lax.axis_size("dim")
    return lax.ppermute(array, AXES, [(i, i ^ (mask1 if i & 1 else mask0)) for i in range(n)])


LOW = 2.0**-3.5


def encode(v, m):
    a = jnp.abs(v) * (127.0 * LOW / m) + LOW
    for _ in range(5):
        a = a * a
    return jnp.where(v < 0, -a, a)


def decode(code, m):
    c = code.astype(F32)
    a = jnp.exp(jnp.log(jnp.abs(c)) * (1.0 / 32.0)) * (1.0 / LOW) - 1.0
    v = a * (m * (1.0 / 127.0))
    return jnp.where(c < 0, -v, v)


def top_of(largest):
    return (largest * 1.01 + 1e-30).astype(BF).astype(F32)


def pairs(core_ref, rows, half, ta_ref, tb_ref, t_rel):
    on0, step = core_ref[0] == 0, 2 * rows
    for b in range(4):
        other = (ta_ref, tb_ref)[b >> 1]
        p0 = jnp.where(on0, ta_ref[b].astype(F32), other[2 * (b & 1)].astype(F32))
        p1 = jnp.where(on0, tb_ref[b].astype(F32), other[2 * (b & 1) + 1].astype(F32))
        top = jnp.concatenate([p0[:, :half], p1[:, :half]], axis=1)
        bottom = jnp.concatenate([p0[:, half:], p1[:, half:]], axis=1)
        t_rel[b * step : (b + 1) * step, :] = jnp.concatenate([top, bottom], axis=0).astype(BF)


def coefficients(near, rows, info_ref, scale_ref, t_rel, images, coeff_low):
    scaling, offset = scale_ref[0], scale_ref[1]
    step, columns = 2 * rows, images.shape[0]
    similar = lax.dot_general(t_rel[...], images[...], (((1,), (1,)), ((), ())), preferred_element_type=F32)
    temp, bias = jnp.zeros((1, columns), F32), jnp.zeros((1, columns), F32)
    for b in range(4):
        part = similar[b * step : (b + 1) * step]
        logits = scaling * part + offset
        if near and b == 0:
            row = lax.broadcasted_iota(jnp.int32, part.shape, 0)
            column = lax.broadcasted_iota(jnp.int32, part.shape, 1)
            matched = (row - rows * info_ref[1] == column) & (column < rows)
            sig = 1.0 / (1.0 + jnp.exp(jnp.where(matched, logits, -logits)))
            coeff = jnp.where(matched, -sig, sig)
        else:
            coeff = 1.0 / (1.0 + jnp.exp(-logits))
        coeff_low[b * step : (b + 1) * step, :] = coeff.astype(BF)
        temp = temp + jnp.sum(coeff * part, axis=0, keepdims=True)
        bias = bias + jnp.sum(coeff, axis=0, keepdims=True)
    even = lax.broadcasted_iota(jnp.int32, (8, 128), 1) % 2 == 0
    return jnp.where(even, jnp.sum(temp, axis=1, keepdims=True), jnp.sum(bias, axis=1, keepdims=True))


def text_parts(core_ref, rows, half, coeff_low, images, grads):
    on0, step = core_ref[0] == 0, 2 * rows
    part = jnp.dot(coeff_low[...], images[...], preferred_element_type=F32)
    for b in range(4):
        top, bottom = part[b * step : b * step + rows], part[b * step + rows : (b + 1) * step]
        for e, at in ((0, slice(0, half)), (1, slice(half, 2 * half))):
            place = jnp.where(on0, e, b >> 1), jnp.where(on0, b, 2 * (b & 1) + e)
            grads[place] = jnp.concatenate([top[:, at], bottom[:, at]], axis=1)


def image_parts(coeff_low, t_rel):
    return lax.dot_general(coeff_low[...], t_rel[...], (((0,), (0,)), ((), ())), preferred_element_type=F32)


def split_kernel(rows, width, info_ref, both_ref, keep_ref, send_ref):
    on0, step = info_ref[0] == 0, 2 * rows
    for k in range(2):
        whole = both_ref[k * width : (k + 1) * width, :].astype(F32).T
        first, second = whole[:step], whole[step:]
        keep_ref[k * step : (k + 1) * step, :] = jnp.where(on0, first, second).astype(BF)
        send_ref[k * step : (k + 1) * step, :] = jnp.where(on0, second, first).astype(BF)


def join_kernel(rows, info_ref, own_ref, got_ref, texts_ref, images_ref):
    on0, step = info_ref[0] == 0, 2 * rows
    for at, ref in ((0, texts_ref), (step, images_ref)):
        own, got = own_ref[at : at + step, :], got_ref[at : at + step, :]
        ref[...] = jnp.concatenate([jnp.where(on0, own, got), jnp.where(on0, got, own)], axis=0).T


def near_kernel(
    rows, half, feats, info_ref, scale_ref, ta_ref, tb_ref, im0_ref, im1_ref,
    grads, m_ref, t_rel, coeff_low, sums_ref, images,
):
    quarter = 4 * rows
    images[0:quarter, :] = im0_ref[...]
    images[quarter : 2 * quarter, :] = im1_ref[...]
    pairs(info_ref, rows, half, ta_ref, tb_ref, t_rel)
    sums_ref[...] = coefficients(True, rows, info_ref, scale_ref, t_rel, images, coeff_low)
    text_parts(info_ref, rows, half, coeff_low, images, grads)
    m_ref[...] = message([grads[1, i] for i in range(4)], feats)


def near_image_kernel(t_rel, coeff_low, acc_ref):
    acc_ref[...] = image_parts(coeff_low, t_rel)


def far_kernel(
    rows, half, feats, info_ref, scale_ref, ta_ref, tb_ref, im0_ref, im1_ref, before_ref, sums_before,
    ma_ref, mb_ref, own_ref, other_ref, images, t_rel, coeff_low, grads,
):
    quarter = 4 * rows
    images[0:quarter, :] = im0_ref[...]
    images[quarter : 2 * quarter, :] = im1_ref[...]
    pairs(info_ref, rows, half, ta_ref, tb_ref, t_rel)
    sums = coefficients(False, rows, info_ref, scale_ref, t_rel, images, coeff_low) + sums_before[...]
    text_parts(info_ref, rows, half, coeff_low, images, grads)
    for k, m_ref in ((0, ma_ref), (1, mb_ref)):
        m_ref[...] = message([grads[k, i] for i in range(4)], feats)
    acc = image_parts(coeff_low, t_rel) + before_ref[...]
    wide = jnp.concatenate([sums] * (feats // 128), axis=1)
    own_ref[...] = jnp.concatenate([acc[0:quarter], wide], axis=0)
    other_ref[...] = jnp.concatenate([acc[quarter : 2 * quarter], wide], axis=0)


def message(blocks, feats, extra=()):
    part = jnp.concatenate(blocks, axis=0)
    m = top_of(jnp.max(jnp.max(jnp.abs(part), axis=0, keepdims=True), axis=1, keepdims=True))
    tail = jnp.broadcast_to(m, (8 - len(extra), feats))
    return jnp.concatenate([encode(part, m), *extra, tail], axis=0).astype(BF)


def decoded(ref):
    whole = ref[...].astype(F32)
    n = whole.shape[0] - 8
    return decode(whole[:n], whole[n + 7 : n + 8]), whole[n:]


def split3(v):
    hi = v.astype(BF).astype(F32)
    mid = (v - hi).astype(BF).astype(F32)
    return [hi, mid, v - hi - mid]


def image_first_kernel(rows, feats, own_ref, other_ref, out_ref, *messages):
    total = own_ref[...] + other_ref[...]
    sums = total[4 * rows :]
    out_ref[...] = jnp.concatenate([total[0:rows], sums], axis=0)
    for i, m_ref in enumerate(messages):
        m_ref[...] = message([total[(i + 1) * rows : (i + 2) * rows]], feats, split3(sums[0:1]))


def with_scalars(own_ref, refs):
    n = own_ref.shape[0] - 8
    total, tails = own_ref[0:n, :], []
    for r in refs:
        value, tail = decoded(r)
        total = total + value
        tails.append(tail[0:1] + (tail[1:2] + tail[2:3]))
    return total, (own_ref[n : n + 1, :] + tails[0]) + (tails[1] + tails[2])


def image_last_kernel(feats, scale_ref, own_ref, r2_ref, r3_ref, r1_ref, out_ref, sums_ref):
    total, sums = with_scalars(own_ref, (r1_ref, r2_ref, r3_ref))
    out_ref[...] = total * scale_ref[0]
    sums_ref[...] = jnp.broadcast_to(sums, (8, feats))


def text_near_kernel(grads_ref, r1_ref, out_ref):
    out_ref[...] = jnp.concatenate([grads_ref[0, i] for i in range(4)], axis=0) + decoded(r1_ref)[0]


def text_first_kernel(rows, feats, own_ref, r2_ref, r3_ref, sums_ref, out_ref, m1_ref, m2_ref, m3_ref, total):
    tops = [r[4 * rows :, :].astype(F32)[7:8] for r in (r2_ref, r3_ref)]

    def add(step, carry):
        at = pl.ds(pl.multiple_of(step * 32, 32), 32)
        total[at, :] = own_ref[at, :] + decode(r2_ref[at, :], tops[0]) + decode(r3_ref[at, :], tops[1])
        return carry

    lax.fori_loop(0, 4 * rows // 32, add, 0)
    out_ref[...] = jnp.concatenate([total[0:rows, :], sums_ref[...]], axis=0)
    for i, m_ref in enumerate((m1_ref, m2_ref, m3_ref)):
        m_ref[...] = message([total[(i + 1) * rows : (i + 2) * rows, :]], feats, split3(sums_ref[0:1, :]))


def text_last_kernel(scale_ref, own_ref, r2_ref, r3_ref, r1_ref, out_ref, sums_ref):
    total, sums = with_scalars(own_ref, (r1_ref, r2_ref, r3_ref))
    out_ref[...] = total * scale_ref[0]
    sums_ref[...] = jnp.broadcast_to(sums[:, :128], (8, 128))


VMEM = pl.BlockSpec(memory_space=pltpu.VMEM)
SMEM = pl.BlockSpec(memory_space=pltpu.SMEM)


def grant(mib):
    return pltpu.CompilerParams(vmem_limit_bytes=mib * 1024 * 1024)


def after(array, *others):
    return lax.optimization_barrier((array, *others))[0]


def body(picture_embeds, caption_embeds, logit_scaler, logit_offset_term):
    height, width = picture_embeds.shape
    rows, half, feats = height // 4, 2 * width, 4 * width
    step, quarter = 2 * rows, 4 * rows
    index = lax.axis_index("batch") * lax.axis_size("dim") + lax.axis_index("dim")
    core, z_lo = index & 1, (index >> 1) & 1
    on0, lo0 = core == 0, z_lo == 0
    scaling = logit_scaler[0]

    def by(first_one, own, other):
        return [jnp.where(first_one, own, other), jnp.where(first_one, other, own)]

    def f32(*shape):
        return jax.ShapeDtypeStruct(shape, F32)

    def bf16(*shape):
        return jax.ShapeDtypeStruct(shape, BF)

    def call(kernel, name, out_shape, *args, scalars=0, scratch=(), mib=20, products=0):
        return pl.pallas_call(
            kernel,
            out_shape=out_shape,
            in_specs=[SMEM] * scalars + [VMEM] * (len(args) - scalars),
            out_specs=[VMEM] * len(out_shape),
            scratch_shapes=scratch,
            compiler_params=grant(mib),
            cost_estimate=pl.CostEstimate(
                flops=products * 2 * quarter * 2 * quarter * 2 * feats,
                bytes_accessed=sum(a.size * a.dtype.itemsize for a in (*args, *out_shape)),
                transcendentals=products * 4 * quarter * quarter,
            ),
            name=name,
        )(*args)

    info = jnp.stack([core, z_lo]).astype(jnp.int32)
    both = jnp.concatenate([caption_embeds.T, picture_embeds.T], axis=0)
    keep, send = call(functools.partial(split_kernel, rows, width), "split", [bf16(height, width)] * 2, info, both, scalars=1)
    chip = jnp.concatenate(by(on0, keep, swap(send, CORE)), axis=1)
    packed = jnp.concatenate([chip[:rows], chip[rows:step]], axis=1)
    keep, send = by(lo0, chip[step : step + rows], chip[step + rows :])
    first = [packed] + [swap(packed, y_mask(i), z_mask(i)) for i in range(1, 4)]
    image = jnp.concatenate([keep, swap(send, z_mask(1))], axis=1)
    stack = jnp.stack(first)
    second1, second3 = (swap(stack, z_mask(j), y_mask(j)) for j in (1, 3))
    images_own = jnp.concatenate([image] + [swap(image, x_mask(k)) for k in range(1, 4)], axis=0)
    images_other = swap(images_own, CORE)
    second2 = swap(after(stack, images_own), z_mask(2), y_mask(2))
    second1, second3 = lax.optimization_barrier((second1, second3))

    sizes = (rows, half, feats)
    scales = jnp.stack([scaling, logit_offset_term[0]])
    images_shape, coeff_shape = (2 * quarter, feats), (2 * quarter, 2 * quarter)
    grads = pltpu.VMEM((2, 4, rows, feats), F32)
    scratch = [pltpu.VMEM(images_shape, BF), pltpu.VMEM(images_shape, BF), pltpu.VMEM(coeff_shape, BF), grads]
    text, m1, t_near, c_near, sums = call(
        functools.partial(near_kernel, *sizes), "tile_near",
        [f32(2, 4, rows, feats), bf16(quarter + 8, feats), bf16(*images_shape), bf16(*coeff_shape), f32(8, 128)],
        info, scales, stack, second1, images_own, images_other,
        scalars=2, mib=36, products=2, scratch=[scratch[0]],
    )
    got1 = swap(m1, z_mask(1), y_mask(1))
    (acc,) = call(near_image_kernel, "image_near", [f32(*images_shape)], t_near, c_near, mib=30, products=1)
    second2 = after(second2, acc)
    m2, m3, img_own, img_other = call(
        functools.partial(far_kernel, *sizes), "tile_far",
        [bf16(quarter + 8, feats), bf16(quarter + 8, feats), f32(quarter + 8, feats), f32(quarter + 8, feats)],
        info, scales, second2, second3, images_own, images_other, acc, sums,
        scalars=2, mib=40, products=3, scratch=scratch,
    )
    img_other, got1 = lax.optimization_barrier((img_other, got1))
    got2, got3 = swap(m2, z_mask(2), y_mask(2)), swap(m3, z_mask(3), y_mask(3))
    img, *messages = call(
        functools.partial(image_first_kernel, rows, feats), "image_first",
        [f32(rows + 8, feats)] + [bf16(rows + 8, feats)] * 3, img_own, swap(img_other, CORE),
    )
    img_got = [swap(m, x_mask(k)) for k, m in zip((1, 2, 3), messages)]
    (text,) = call(text_near_kernel, "text_near", [f32(quarter, feats)], after(text, *messages), got1)
    img, sums = call(
        functools.partial(image_last_kernel, feats), "image_last", [f32(rows, feats), f32(8, feats)],
        logit_scaler, img, img_got[1], img_got[2], img_got[0], scalars=1,
    )
    text, *messages = call(
        functools.partial(text_first_kernel, rows, feats), "text_first",
        [f32(rows + 8, feats)] + [bf16(rows + 8, feats)] * 3, text, got2, got3, sums,
        scratch=[pltpu.VMEM((quarter, feats), F32)],
    )
    got = [swap(m, y_mask(i), z_mask(i)) for i, m in zip((1, 2, 3), messages)]
    text, sums = call(
        text_last_kernel, "text_last", [f32(rows, feats), f32(8, 128)], logit_scaler, text, got[1], got[2], got[0], scalars=1, products=2
    )
    image = jnp.concatenate(by(lo0, img[:, :half], after(swap(img[:, half:], z_mask(1)), text)), axis=0)
    whole = jnp.concatenate([text[:, :half], text[:, half:], image], axis=0)
    mine, other = by(on0, whole[:, :width], whole[:, width:])
    sums = after(sums, other)
    other = swap(other, CORE)
    text_grad, image_grad = call(
        functools.partial(join_kernel, rows), "join", [f32(width, height)] * 2, info, mine, other, scalars=1
    )
    s1, s2, s3 = (after(swap(sums, z_mask(k), y_mask(k)), text_grad, image_grad) for k in (1, 2, 3))
    sums = (sums + s1) + (s2 + s3)
    return (image_grad.T, text_grad.T, sums[0, :2])


def solution(mesh):
    placed = (P("batch", "dim"), P("batch", "dim"), P(), P())
    return jax.shard_map(
        body,
        mesh=mesh,
        in_specs=placed,
        out_specs=(P("batch", "dim"), P("batch", "dim"), P()),
        check_vma=False,
    )
```

```python
import functools

import jax
import jax.numpy as jnp
from jax import lax
from jax.experimental import pallas as pl
from jax.experimental.pallas import tpu as pltpu
from jax.sharding import PartitionSpec as P

BF = jnp.bfloat16
F32 = jnp.float32
AXES = ("batch", "dim")
CORE = 1


def x_mask(k):
    return k << 2


def y_mask(k):
    return k << 4


def z_mask(k):
    return ((k >> 1) << 6) | ((k & 1) << 1)


def swap(array, mask0, mask1=None):
    mask1 = mask0 if mask1 is None else mask1
    n = lax.axis_size("batch") * lax.axis_size("dim")
    return lax.ppermute(array, AXES, [(i, i ^ (mask1 if i & 1 else mask0)) for i in range(n)])


LOW = 2.0**-3.5


def encode(v, m):
    a = jnp.abs(v) * (127.0 * LOW / m) + LOW
    for _ in range(5):
        a = a * a
    return jnp.where(v < 0, -a, a)


def decode(code, m):
    c = code.astype(F32)
    a = jnp.exp(jnp.log(jnp.abs(c)) * (1.0 / 32.0)) * (1.0 / LOW) - 1.0
    v = a * (m * (1.0 / 127.0))
    return jnp.where(c < 0, -v, v)


def top_of(largest):
    return (largest * 1.01 + 1e-30).astype(BF).astype(F32)


def pairs(core_ref, rows, half, ta_ref, tb_ref, t_rel):
    on0, step = core_ref[0] == 0, 2 * rows
    for b in range(4):
        other = (ta_ref, tb_ref)[b >> 1]
        p0 = jnp.where(on0, ta_ref[b].astype(F32), other[2 * (b & 1)].astype(F32))
        p1 = jnp.where(on0, tb_ref[b].astype(F32), other[2 * (b & 1) + 1].astype(F32))
        top = jnp.concatenate([p0[:, :half], p1[:, :half]], axis=1)
        bottom = jnp.concatenate([p0[:, half:], p1[:, half:]], axis=1)
        t_rel[b * step : (b + 1) * step, :] = jnp.concatenate([top, bottom], axis=0).astype(BF)


def coefficients(near, rows, info_ref, scale_ref, t_rel, images, coeff_low):
    scaling, offset = scale_ref[0], scale_ref[1]
    step, columns = 2 * rows, images.shape[0]
    similar = lax.dot_general(t_rel[...], images[...], (((1,), (1,)), ((), ())), preferred_element_type=F32)
    temp, bias = jnp.zeros((1, columns), F32), jnp.zeros((1, columns), F32)
    for b in range(4):
        part = similar[b * step : (b + 1) * step]
        logits = scaling * part + offset
        if near and b == 0:
            row = lax.broadcasted_iota(jnp.int32, part.shape, 0)
            column = lax.broadcasted_iota(jnp.int32, part.shape, 1)
            matched = (row - rows * info_ref[1] == column) & (column < rows)
            sig = 1.0 / (1.0 + jnp.exp(jnp.where(matched, logits, -logits)))
            coeff = jnp.where(matched, -sig, sig)
        else:
            coeff = 1.0 / (1.0 + jnp.exp(-logits))
        coeff_low[b * step : (b + 1) * step, :] = coeff.astype(BF)
        temp = temp + jnp.sum(coeff * part, axis=0, keepdims=True)
        bias = bias + jnp.sum(coeff, axis=0, keepdims=True)
    even = lax.broadcasted_iota(jnp.int32, (8, 128), 1) % 2 == 0
    return jnp.where(even, jnp.sum(temp, axis=1, keepdims=True), jnp.sum(bias, axis=1, keepdims=True))


def text_parts(core_ref, rows, half, coeff_low, images, grads):
    on0, step = core_ref[0] == 0, 2 * rows
    part = jnp.dot(coeff_low[...], images[...], preferred_element_type=F32)
    for b in range(4):
        top, bottom = part[b * step : b * step + rows], part[b * step + rows : (b + 1) * step]
        for e, at in ((0, slice(0, half)), (1, slice(half, 2 * half))):
            place = jnp.where(on0, e, b >> 1), jnp.where(on0, b, 2 * (b & 1) + e)
            grads[place] = jnp.concatenate([top[:, at], bottom[:, at]], axis=1)


def image_parts(coeff_low, t_rel):
    return lax.dot_general(coeff_low[...], t_rel[...], (((0,), (0,)), ((), ())), preferred_element_type=F32)


def split_kernel(rows, width, info_ref, both_ref, keep_ref, send_ref):
    on0, step = info_ref[0] == 0, 2 * rows
    for k in range(2):
        whole = both_ref[k * width : (k + 1) * width, :].astype(F32).T
        first, second = whole[:step], whole[step:]
        keep_ref[k * step : (k + 1) * step, :] = jnp.where(on0, first, second).astype(BF)
        send_ref[k * step : (k + 1) * step, :] = jnp.where(on0, second, first).astype(BF)


def join_kernel(rows, info_ref, own_ref, got_ref, texts_ref, images_ref):
    on0, step = info_ref[0] == 0, 2 * rows
    for at, ref in ((0, texts_ref), (step, images_ref)):
        own, got = own_ref[at : at + step, :], got_ref[at : at + step, :]
        ref[...] = jnp.concatenate([jnp.where(on0, own, got), jnp.where(on0, got, own)], axis=0).T


def near_kernel(
    rows, half, feats, info_ref, scale_ref, ta_ref, tb_ref, im0_ref, im1_ref,
    grads, m_ref, t_rel, coeff_low, sums_ref, images,
):
    quarter = 4 * rows
    images[0:quarter, :] = im0_ref[...]
    images[quarter : 2 * quarter, :] = im1_ref[...]
    pairs(info_ref, rows, half, ta_ref, tb_ref, t_rel)
    sums_ref[...] = coefficients(True, rows, info_ref, scale_ref, t_rel, images, coeff_low)
    text_parts(info_ref, rows, half, coeff_low, images, grads)
    m_ref[...] = message([grads[1, i] for i in range(4)], feats)


def near_image_kernel(t_rel, coeff_low, acc_ref):
    acc_ref[...] = image_parts(coeff_low, t_rel)


def far_kernel(
    rows, half, feats, info_ref, scale_ref, ta_ref, tb_ref, im0_ref, im1_ref, before_ref, sums_before,
    ma_ref, mb_ref, own_ref, other_ref, images, t_rel, coeff_low, grads,
):
    quarter = 4 * rows
    images[0:quarter, :] = im0_ref[...]
    images[quarter : 2 * quarter, :] = im1_ref[...]
    pairs(info_ref, rows, half, ta_ref, tb_ref, t_rel)
    sums = coefficients(False, rows, info_ref, scale_ref, t_rel, images, coeff_low) + sums_before[...]
    text_parts(info_ref, rows, half, coeff_low, images, grads)
    for k, m_ref in ((0, ma_ref), (1, mb_ref)):
        m_ref[...] = message([grads[k, i] for i in range(4)], feats)
    acc = image_parts(coeff_low, t_rel) + before_ref[...]
    wide = jnp.concatenate([sums] * (feats // 128), axis=1)
    own_ref[...] = jnp.concatenate([acc[0:quarter], wide], axis=0)
    other_ref[...] = jnp.concatenate([acc[quarter : 2 * quarter], wide], axis=0)


def message(blocks, feats, extra=()):
    part = jnp.concatenate(blocks, axis=0)
    m = top_of(jnp.max(jnp.max(jnp.abs(part), axis=0, keepdims=True), axis=1, keepdims=True))
    tail = jnp.broadcast_to(m, (8 - len(extra), feats))
    return jnp.concatenate([encode(part, m), *extra, tail], axis=0).astype(BF)


def decoded(ref):
    whole = ref[...].astype(F32)
    n = whole.shape[0] - 8
    return decode(whole[:n], whole[n + 7 : n + 8]), whole[n:]


def split3(v):
    hi = v.astype(BF).astype(F32)
    mid = (v - hi).astype(BF).astype(F32)
    return [hi, mid, v - hi - mid]


def image_first_kernel(rows, feats, own_ref, other_ref, out_ref, *messages):
    total = own_ref[...] + other_ref[...]
    sums = total[4 * rows :]
    out_ref[...] = jnp.concatenate([total[0:rows], sums], axis=0)
    for i, m_ref in enumerate(messages):
        m_ref[...] = message([total[(i + 1) * rows : (i + 2) * rows]], feats, split3(sums[0:1]))


def with_scalars(own_ref, refs):
    n = own_ref.shape[0] - 8
    total, tails = own_ref[0:n, :], []
    for r in refs:
        value, tail = decoded(r)
        total = total + value
        tails.append(tail[0:1] + (tail[1:2] + tail[2:3]))
    return total, (own_ref[n : n + 1, :] + tails[0]) + (tails[1] + tails[2])


def image_last_kernel(feats, scale_ref, own_ref, r2_ref, r3_ref, r1_ref, out_ref, sums_ref):
    total, sums = with_scalars(own_ref, (r1_ref, r2_ref, r3_ref))
    out_ref[...] = total * scale_ref[0]
    sums_ref[...] = jnp.broadcast_to(sums, (8, feats))


def text_near_kernel(grads_ref, r1_ref, out_ref):
    out_ref[...] = jnp.concatenate([grads_ref[0, i] for i in range(4)], axis=0) + decoded(r1_ref)[0]


def text_first_kernel(rows, feats, own_ref, r2_ref, r3_ref, sums_ref, out_ref, m1_ref, m2_ref, m3_ref, total):
    tops = [r[4 * rows :, :].astype(F32)[7:8] for r in (r2_ref, r3_ref)]

    def add(step, carry):
        at = pl.ds(pl.multiple_of(step * 32, 32), 32)
        total[at, :] = own_ref[at, :] + decode(r2_ref[at, :], tops[0]) + decode(r3_ref[at, :], tops[1])
        return carry

    lax.fori_loop(0, 4 * rows // 32, add, 0)
    out_ref[...] = jnp.concatenate([total[0:rows, :], sums_ref[...]], axis=0)
    for i, m_ref in enumerate((m1_ref, m2_ref, m3_ref)):
        m_ref[...] = message([total[(i + 1) * rows : (i + 2) * rows, :]], feats, split3(sums_ref[0:1, :]))


def text_last_kernel(scale_ref, own_ref, r2_ref, r3_ref, r1_ref, out_ref, sums_ref):
    total, sums = with_scalars(own_ref, (r1_ref, r2_ref, r3_ref))
    out_ref[...] = total * scale_ref[0]
    sums_ref[...] = jnp.broadcast_to(sums[:, :128], (8, 128))


VMEM = pl.BlockSpec(memory_space=pltpu.VMEM)
SMEM = pl.BlockSpec(memory_space=pltpu.SMEM)


def grant(mib):
    return pltpu.CompilerParams(vmem_limit_bytes=mib * 1024 * 1024)


def after(array, *others):
    return lax.optimization_barrier((array, *others))[0]


def body(picture_embeds, caption_embeds, logit_scaler, logit_offset_term):
    height, width = picture_embeds.shape
    rows, half, feats = height // 4, 2 * width, 4 * width
    step, quarter = 2 * rows, 4 * rows
    index = lax.axis_index("batch") * lax.axis_size("dim") + lax.axis_index("dim")
    core, z_lo = index & 1, (index >> 1) & 1
    on0, lo0 = core == 0, z_lo == 0
    scaling = logit_scaler[0]

    def by(first_one, own, other):
        return [jnp.where(first_one, own, other), jnp.where(first_one, other, own)]

    def f32(*shape):
        return jax.ShapeDtypeStruct(shape, F32)

    def bf16(*shape):
        return jax.ShapeDtypeStruct(shape, BF)

    def call(kernel, name, out_shape, *args, scalars=0, scratch=(), mib=20, products=0):
        return pl.pallas_call(
            kernel,
            out_shape=out_shape,
            in_specs=[SMEM] * scalars + [VMEM] * (len(args) - scalars),
            out_specs=[VMEM] * len(out_shape),
            scratch_shapes=scratch,
            compiler_params=grant(mib),
            cost_estimate=pl.CostEstimate(
                flops=products * 2 * quarter * 2 * quarter * 2 * feats,
                bytes_accessed=sum(a.size * a.dtype.itemsize for a in (*args, *out_shape)),
                transcendentals=products * 4 * quarter * quarter,
            ),
            name=name,
        )(*args)

    info = jnp.stack([core, z_lo]).astype(jnp.int32)
    both = jnp.concatenate([caption_embeds.T, picture_embeds.T], axis=0)
    keep, send = call(functools.partial(split_kernel, rows, width), "split", [bf16(height, width)] * 2, info, both, scalars=1)
    chip = jnp.concatenate(by(on0, keep, swap(send, CORE)), axis=1)
    packed = jnp.concatenate([chip[:rows], chip[rows:step]], axis=1)
    keep, send = by(lo0, chip[step : step + rows], chip[step + rows :])
    first = [packed] + [swap(packed, y_mask(i), z_mask(i)) for i in range(1, 4)]
    image = jnp.concatenate([keep, swap(send, z_mask(1))], axis=1)
    stack = jnp.stack(first)
    second1, second3 = (swap(stack, z_mask(j), y_mask(j)) for j in (1, 3))
    images_own = jnp.concatenate([image] + [swap(image, x_mask(k)) for k in range(1, 4)], axis=0)
    images_other = swap(images_own, CORE)
    second2 = swap(after(stack, images_own), z_mask(2), y_mask(2))
    second1, second3 = lax.optimization_barrier((second1, second3))

    sizes = (rows, half, feats)
    scales = jnp.stack([scaling, logit_offset_term[0]])
    images_shape, coeff_shape = (2 * quarter, feats), (2 * quarter, 2 * quarter)
    grads = pltpu.VMEM((2, 4, rows, feats), F32)
    scratch = [pltpu.VMEM(images_shape, BF), pltpu.VMEM(images_shape, BF), pltpu.VMEM(coeff_shape, BF), grads]
    text, m1, t_near, c_near, sums = call(
        functools.partial(near_kernel, *sizes), "tile_near",
        [f32(2, 4, rows, feats), bf16(quarter + 8, feats), bf16(*images_shape), bf16(*coeff_shape), f32(8, 128)],
        info, scales, stack, second1, images_own, images_other,
        scalars=2, mib=36, products=2, scratch=[scratch[0]],
    )
    got1 = swap(m1, z_mask(1), y_mask(1))
    (acc,) = call(near_image_kernel, "image_near", [f32(*images_shape)], t_near, c_near, mib=30, products=1)
    second2 = after(second2, acc)
    m2, m3, img_own, img_other = call(
        functools.partial(far_kernel, *sizes), "tile_far",
        [bf16(quarter + 8, feats), bf16(quarter + 8, feats), f32(quarter + 8, feats), f32(quarter + 8, feats)],
        info, scales, second2, second3, images_own, images_other, acc, sums,
        scalars=2, mib=40, products=3, scratch=scratch,
    )
    img_other, got1 = lax.optimization_barrier((img_other, got1))
    got2, got3 = swap(m2, z_mask(2), y_mask(2)), swap(m3, z_mask(3), y_mask(3))
    img, *messages = call(
        functools.partial(image_first_kernel, rows, feats), "image_first",
        [f32(rows + 8, feats)] + [bf16(rows + 8, feats)] * 3, img_own, swap(img_other, CORE),
    )
    img_got = [swap(m, x_mask(k)) for k, m in zip((1, 2, 3), messages)]
    (text,) = call(text_near_kernel, "text_near", [f32(quarter, feats)], after(text, *messages), got1)
    img, sums = call(
        functools.partial(image_last_kernel, feats), "image_last", [f32(rows, feats), f32(8, feats)],
        logit_scaler, img, img_got[1], img_got[2], img_got[0], scalars=1,
    )
    text, *messages = call(
        functools.partial(text_first_kernel, rows, feats), "text_first",
        [f32(rows + 8, feats)] + [bf16(rows + 8, feats)] * 3, text, got2, got3, sums,
        scratch=[pltpu.VMEM((quarter, feats), F32)],
    )
    got = [swap(m, y_mask(i), z_mask(i)) for i, m in zip((1, 2, 3), messages)]
    back = swap(img[:, half:], z_mask(1))
    got[1] = after(got[1], back)
    text, sums = call(
        text_last_kernel, "text_last", [f32(rows, feats), f32(8, 128)], logit_scaler, text, got[1], got[2], got[0], scalars=1, products=2
    )
    image = jnp.concatenate(by(lo0, img[:, :half], back), axis=0)
    whole = jnp.concatenate([text[:, :half], text[:, half:], image], axis=0)
    mine, other = by(on0, whole[:, :width], whole[:, width:])
    sums = after(sums, other)
    other = swap(other, CORE)
    text_grad, image_grad = call(
        functools.partial(join_kernel, rows), "join", [f32(width, height)] * 2, info, mine, other, scalars=1
    )
    s1, s2, s3 = (after(swap(sums, z_mask(k), y_mask(k)), text_grad, image_grad) for k in (1, 2, 3))
    sums = (sums + s1) + (s2 + s3)
    return (image_grad.T, text_grad.T, sums[0, :2])


def solution(mesh):
    placed = (P("batch", "dim"), P("batch", "dim"), P(), P())
    return jax.shard_map(
        body,
        mesh=mesh,
        in_specs=placed,
        out_specs=(P("batch", "dim"), P("batch", "dim"), P()),
        check_vma=False,
    )
```
